512 devices in a mesh: seq: 128 (over z, y, core), grp: 4 (over x).
Axes of the slice: x: 4, y: 8, z: 8, core: 2. Of those that a mesh axis runs over, the one named last changes fastest.
Arguments:
- q_pre: bfloat16 [8192, 4096], P('seq', 'grp'), may hold values from -180 to 180, as said below
- k_pre: bfloat16 [8192, 1024], P('seq', 'grp'), may hold values from -6 to 6
- v_pre: bfloat16 [8192, 1024], P('seq', 'grp'), may hold values from -6 to 6
- old_k: bfloat16 [128, 40, 16, 1024], P('seq', 'grp'), may hold values from -6 to 6
- old_v: bfloat16 [128, 40, 16, 1024], P('seq', 'grp'), may hold values from -6 to 6
- src_page: int32 [128, 8], P('seq'), may hold values from 0 to 511
- page_row: int32 [128, 48], P('seq', 'grp'), may hold values from 0 to 31
- page_len: int32 [128, 48], P('seq', 'grp'), may hold values from 1 to 16
- q_dec: bfloat16 [32, 4, 4096], replicated, may hold values from -180 to 180, as said below
- dec_k: bfloat16 [32, 4, 1024], replicated, may hold values from -6 to 6
- dec_v: bfloat16 [32, 4, 1024], replicated, may hold values from -6 to 6
Outputs:
- attn_pre: bfloat16 [8192, 4096], P('seq', 'grp')
- dec_out: bfloat16 [4096, 128], P(('seq', 'grp'))
The draws below stay inside these ranges and needn't reach their ends.
Inputs may be any that keep to these rules, and one draw needn't show every extreme that they name: `q_pre`: queries of the prefill block. `q_dec`: queries of the decode rows.
All inputs are finite; a program needn't handle non-finite values.
Results may differ from the reference program's by a relative error of at most 0.01025.
Values may be sent and summed in bfloat16 or wider, within the bound.
No kernel may reach another device: no remote copies, remote signals or barrier semaphores. Data moves between devices by JAX's collectives and lax.ppermute only.
A program may use at most 64 MiB of HBM per device.

```python
import math
import jax
import jax.numpy as jnp
import numpy as np
from jax import lax

HEAD = 128
QH = 32
KVH = 8
TOK_DEV = 64
PAGE = 16
OLD = 10
NEWP = 2
ROWS = 32
STEPS = 4
STRETCH = 8192
CPAGES = 512
POOL = 12
N_SEQ = 128
N_GRP = 4


def scaled_queries(key, shape):
    base_key = jax.random.fold_in(key, 0)
    base = jnp.clip(jax.random.normal(base_key, shape, jnp.float32), -6.0, 6.0)
    return base.astype(jnp.bfloat16)


def draw_q_pre(key, part):
    key = jax.random.fold_in(key, 11)
    return scaled_queries(key, (STRETCH, QH * HEAD))


def draw_q_dec(key, part):
    key = jax.random.fold_in(key, 12)
    return scaled_queries(key, (ROWS, STEPS, QH * HEAD))


def place_ends(drawn, stream_key, low, high):
    longest = drawn.shape.index(max(drawn.shape))
    spots = []
    for shift in (0, 1):
        where = [jax.random.randint(jax.random.fold_in(stream_key, axis), (), 0, length) for axis, length in enumerate(drawn.shape)]
        where[longest] = (where[longest] + shift) % drawn.shape[longest]
        spots.append(tuple(where))
    return drawn.at[spots[0]].set(low).at[spots[1]].set(high)


def level_of(key, dims, cuts, smallest, top_value):
    def one(dim, blocks):
        draws = jax.random.uniform(jax.random.fold_in(jax.random.fold_in(key, 6), dim), (blocks,), jnp.float32, smallest / len(cuts), top_value / len(cuts))
        return jnp.repeat(jnp.exp(draws), dims[dim] // blocks).reshape((-1,) + (1,) * (len(dims) - dim - 1))

    loudness = one(*cuts[0])
    for cut in cuts[1:]:
        loudness = loudness * one(*cut)
    return loudness


def rank_bounds(count, lean):
    weights = [(1 << 20) // math.isqrt(standing ** lean) + 1 for standing in range(1, count + 1)]
    deviation = 1 + sum(weights) // (1 << 30)
    return np.cumsum(np.array([max(1, weight // deviation) for weight in weights]))


def ranked_ids(own_key, shape, number_of, slope):
    grid = rank_bounds(number_of, slope)
    ticket = jax.random.randint(jax.random.fold_in(own_key, 1), shape, 0, int(grid[number_of - 1]))
    grade = jnp.searchsorted(jnp.asarray(grid, jnp.int32), ticket, side="right")
    return jax.random.permutation(jax.random.fold_in(own_key, 2), number_of)[grade].astype(jnp.int32)


def gaussian(stream_key, extent, deviation, limit, pieces=(), kind=jnp.bfloat16):
    entries = jax.random.normal(stream_key, extent, jnp.float32) * deviation
    if len(pieces) > 0:
        entries = level_of(stream_key, extent, pieces, -0.22, 0.18) * entries
    return jnp.clip(entries, min=-limit, max=limit).astype(kind)


def setup_inputs(seed: int = 0) -> dict:
    splits = jax.random.split(jax.random.key(seed), 12)
    return {
        "q_pre": draw_q_pre(jax.random.fold_in(splits[11], 71), 0),
        "k_pre": gaussian(splits[1], (STRETCH, KVH * HEAD), 1.0, 6.0, ((0, 128), (1, 4))),
        "v_pre": gaussian(splits[2], (STRETCH, KVH * HEAD), 1.0, 6.0, ((0, 128), (1, 4))),
        "old_k": gaussian(splits[3], (N_SEQ, N_GRP * OLD, PAGE, KVH * HEAD), 1.0, 6.0, ((0, 128), (1, 4))),
        "old_v": gaussian(splits[4], (N_SEQ, N_GRP * OLD, PAGE, KVH * HEAD), 1.0, 6.0, ((0, 128), (1, 4))),
        "src_page": place_ends(jax.random.randint(splits[5], (N_SEQ, N_GRP * NEWP), 0, CPAGES), jax.random.fold_in(splits[5], 1), 0, CPAGES - 1).astype(jnp.int32),
        "page_row": place_ends(ranked_ids(splits[6], (N_SEQ, N_GRP * POOL), ROWS, 2), jax.random.fold_in(splits[6], 3), 0, ROWS - 1).astype(jnp.int32),
        "page_len": place_ends(jax.random.randint(splits[7], (N_SEQ, N_GRP * POOL), 1, PAGE + 1), jax.random.fold_in(splits[7], 1), 1, PAGE).astype(jnp.int32),
        "q_dec": draw_q_dec(jax.random.fold_in(splits[11], 71), 0),
        "dec_k": gaussian(splits[9], (ROWS, STEPS, KVH * HEAD), 1.0, 6.0),
        "dec_v": gaussian(splits[10], (ROWS, STEPS, KVH * HEAD), 1.0, 6.0),
    }


NEG = -1.0e30


def prefill_rows(q_pre, k_pre, v_pre):
    scale = 1.0 / (HEAD ** 0.5)
    gqa = QH // KVH
    keys = k_pre.astype(jnp.float32).reshape(STRETCH, KVH, HEAD)
    values = v_pre.astype(jnp.float32).reshape(STRETCH, KVH, HEAD)
    key_pos = jnp.arange(STRETCH, dtype=jnp.int32)
    blocks = q_pre.reshape(STRETCH // TOK_DEV, TOK_DEV, KVH, gqa, HEAD)

    def one_block(args):
        block, index = args
        q_pos = index * TOK_DEV + jnp.arange(TOK_DEV, dtype=jnp.int32)
        scores = jnp.einsum("tgjd,ugd->tgju", block.astype(jnp.float32), keys) * scale
        allowed = (key_pos[None, :] <= q_pos[:, None])[:, None, None, :]
        scores = jnp.where(allowed, scores, NEG)
        top = jnp.max(scores, axis=-1, keepdims=True)
        weights = jnp.where(allowed, jnp.exp(scores - top), 0.0).astype(jnp.bfloat16)
        weights = lax.optimization_barrier(weights).astype(jnp.float32)
        total = jnp.sum(weights, axis=-1)
        mixed = jnp.einsum("tgju,ugd->tgjd", weights, values)
        return (mixed / total[..., None]).astype(jnp.bfloat16)

    out = lax.map(one_block, (blocks, jnp.arange(STRETCH // TOK_DEV, dtype=jnp.int32)))
    return out.reshape(STRETCH, QH * HEAD)


def build_pool(old, stretch, src_page):
    pages = stretch.reshape(CPAGES, PAGE, KVH * HEAD)
    fresh = pages[src_page.reshape(-1).astype(jnp.int32)].reshape(N_SEQ, N_GRP, NEWP, PAGE, KVH * HEAD)
    stale = old.reshape(N_SEQ, N_GRP, OLD, PAGE, KVH * HEAD)
    return jnp.concatenate([stale, fresh], axis=2).reshape(N_SEQ * N_GRP, POOL, PAGE, KVH * HEAD)


def decode_rows(q_dec, dec_k, dec_v, pool_k, pool_v, page_row, page_len):
    scale = 1.0 / (HEAD ** 0.5)
    gqa = QH // KVH
    queries = q_dec.astype(jnp.float32).reshape(ROWS, STEPS, KVH, gqa, HEAD)
    owners = page_row.reshape(N_SEQ * N_GRP, POOL)
    lengths = page_len.reshape(N_SEQ * N_GRP, POOL)
    row_ids = jnp.arange(ROWS, dtype=jnp.int32)
    token_ids = jnp.arange(PAGE, dtype=jnp.int32)

    def page_scores(keys, owner, length):
        q_page = queries[owner]
        k_page = keys.astype(jnp.float32).reshape(POOL, PAGE, KVH, HEAD)
        scores = jnp.einsum("psgjd,ptgd->psgjt", q_page, k_page) * scale
        valid = (token_ids[None, :] < length[:, None])[:, None, None, None, :]
        return jnp.where(valid, scores, NEG), valid

    def find_max(carry, args):
        keys, owner, length = args
        scores, valid = page_scores(keys, owner, length)
        page_top = jnp.max(scores, axis=-1)
        hit = owner[None, :] == row_ids[:, None]
        row_top = jnp.max(jnp.where(hit[:, :, None, None, None], page_top[None], NEG), axis=1)
        return jnp.maximum(carry, row_top), None

    start = jnp.full((ROWS, STEPS, KVH, gqa), NEG, jnp.float32)
    top, _ = lax.scan(find_max, start, (pool_k, owners, lengths))
    own_k = dec_k.astype(jnp.float32).reshape(ROWS, STEPS, KVH, HEAD)
    own_v = dec_v.astype(jnp.float32).reshape(ROWS, STEPS, KVH, HEAD)
    own_scores = jnp.einsum("rsgjd,rugd->rsgju", queries, own_k) * scale
    steps = jnp.arange(STEPS, dtype=jnp.int32)
    causal = (steps[None, :] <= steps[:, None])[None, :, None, None, :]
    own_scores = jnp.where(causal, own_scores, NEG)
    top = jnp.maximum(top, jnp.max(own_scores, axis=-1))

    def add_terms(carry, args):
        total, mixed = carry
        keys, vals, owner, length = args
        scores, valid = page_scores(keys, owner, length)
        weights = jnp.where(valid, jnp.exp(scores - top[owner][..., None]), 0.0).astype(jnp.bfloat16)
        weights = lax.optimization_barrier(weights).astype(jnp.float32)
        v_page = vals.astype(jnp.float32).reshape(POOL, PAGE, KVH, HEAD)
        page_mix = jnp.einsum("psgjt,ptgd->psgjd", weights, v_page)
        total = total + jax.ops.segment_sum(jnp.sum(weights, axis=-1), owner, ROWS)
        mixed = mixed + jax.ops.segment_sum(page_mix, owner, ROWS)
        return (total, mixed), None

    own_w = jnp.where(causal, jnp.exp(own_scores - top[..., None]), 0.0).astype(jnp.bfloat16)
    own_w = lax.optimization_barrier(own_w).astype(jnp.float32)
    total0 = jnp.sum(own_w, axis=-1)
    mixed0 = jnp.einsum("rsgju,rugd->rsgjd", own_w, own_v)
    (total, mixed), _ = lax.scan(add_terms, (total0, mixed0), (pool_k, pool_v, owners, lengths))
    out = (mixed / total[..., None]).astype(jnp.bfloat16)
    return out.reshape(ROWS * STEPS * QH, HEAD)


def reference(q_pre, k_pre, v_pre, old_k, old_v, src_page, page_row, page_len, q_dec, dec_k, dec_v):
    attn_pre = prefill_rows(q_pre, k_pre, v_pre)
    pool_k = build_pool(old_k, k_pre, src_page)
    pool_v = build_pool(old_v, v_pre, src_page)
    dec_out = decode_rows(q_dec, dec_k, dec_v, pool_k, pool_v, page_row, page_len)
    return attn_pre, dec_out
```

```python
import functools
import math

import jax
import jax.numpy as jnp
from jax import lax
from jax.experimental import pallas as pl
from jax.experimental.pallas import tpu as pltpu
from jax.sharding import PartitionSpec as P

HEAD = 128
PAGE = 16
OLD = 10
NEWP = 2
ROWS = 32
STEPS = 4
ITEMS = ROWS * STEPS
SIDE = 8
NG = 4
TOK = 64
BLK = 2 * TOK
KEYS = SIDE * BLK
QROWS = 4 * BLK
HEADS = 8
TWO = 2 * HEAD
EXP2_SCALE = math.log2(math.e) / math.sqrt(HEAD)
NEG = -(2.0**100)
HIDE = -(2.0**80)
LOWEST = -(2.0**60)
META = 16
KV_MSG = 2 * BLK + META
Q_MSG = QROWS + META
PAIR_MSG = 6 * TOK + META
HALF = OLD * PAGE
X_MSG = 2 * HALF + META
OLD_TOK = NG * HALF
DEC_TOK = OLD_TOK + 128
PER = ITEMS // SIDE
DEC_MSG = HEADS * PER + PER
O_MSG = Q_MSG + DEC_MSG
LAST_MSG = 4 * TOK + 16
NT = (((1,), (1,)), ((), ()))
F32 = jnp.float32
BF16 = jnp.bfloat16


def seq_of(z, y, core):
    return (z * SIDE + y) * 2 + core


ALONG_Z = [[[seq_of(i, j, c) for i in range(SIDE)] for j in range(SIDE)] for c in range(2)]
ALONG_Y = [[[seq_of(j, i, c) for i in range(SIDE)] for j in range(SIDE)] for c in range(2)]
KEY_GROUPS = ALONG_Z[0] + ALONG_Y[1]
QUERY_GROUPS = ALONG_Y[0] + ALONG_Z[1]


def iota(shape, dim):
    return lax.broadcasted_iota(jnp.int32, shape, dim)


def spot():
    seq, grp = lax.axis_index("seq"), lax.axis_index("grp")
    core = seq & 1
    y = (seq >> 1) & (SIDE - 1)
    z = seq >> 4
    even = core == 0
    return seq, grp, z, y, core, jnp.where(even, z, y), jnp.where(even, y, z)


def aligned(x, by):
    return pl.multiple_of(x, by)


def call(kernel, outs, args, scratch=(), limit=32, specs=None, out_specs=None, cost=None, alias=None):
    whole = pl.BlockSpec(memory_space=pltpu.VMEM)
    name = kernel.__name__.removesuffix("_kernel")
    return pl.pallas_call(
        kernel,
        out_shape=[jax.ShapeDtypeStruct(s, t) for s, t in outs],
        in_specs=[specs.get(n, whole) if specs else whole for n in range(len(args))],
        out_specs=out_specs or [whole] * len(outs),
        scratch_shapes=list(scratch),
        compiler_params=pltpu.CompilerParams(vmem_limit_bytes=limit * 1024 * 1024),
        cost_estimate=cost,
        input_output_aliases=alias or {},
        name=name,
    )(*args)


SMEM = pl.BlockSpec(memory_space=pltpu.SMEM)


def split_kernel(q, k, v, src_page, page_row, page_len, keep, send, src_s, row_s, len_s, sems):
    _, grp, z, y, core, w, u = spot()
    pairs = [(src_page, src_s), (page_row, row_s), (page_len, len_s)]
    for dst, head in ((keep, core), (send, 1 - core)):
        one = pl.ds(aligned(head * HEAD, HEAD), HEAD)
        pairs.append((k.at[:, one], dst.at[pl.ds(0, TOK), :]))
        pairs.append((v.at[:, one], dst.at[pl.ds(TOK, TOK), :]))
        for h in range(4):
            cols = pl.ds(aligned((head * 4 + h) * HEAD, HEAD), HEAD)
            pairs.append((q.at[:, cols], dst.at[pl.ds((2 + h) * TOK, TOK), :]))
    copies = [pltpu.make_async_copy(a, b, sems.at[n]) for n, (a, b) in enumerate(pairs)]
    for copy in copies:
        copy.start()
    for copy in copies[:3]:
        copy.wait()
    sub, lane = iota((META, 128), 0), iota((META, 128), 1)
    for dst, at in ((keep, w), (send, u)):
        tile = jnp.zeros((META, 128), F32)
        for n in range(NEWP):
            src = src_s[0, grp * NEWP + n]
            values = (src >> 2, src & 3, row_s[0, OLD + n], len_s[0, OLD + n])
            for m, value in enumerate(values):
                here = (lane == at * 4 + core * 2 + n) & ((sub & 3) == m) & (sub < 8)
                tile = jnp.where(here, value.astype(F32), tile)
        dst[6 * TOK :, :] = tile.astype(BF16)
    for copy in copies[3:]:
        copy.wait()


def keys_kernel(keep, got, kv_send, q_blk):
    core = spot()[4]
    for src, start in ((keep, core * TOK), (got, (1 - core) * TOK)):
        for n in range(2):
            kv_send[0, pl.ds(aligned(n * BLK + start, TOK), TOK), :] = src[n * TOK : (n + 1) * TOK, :]
        for h in range(4):
            q_blk[pl.ds(aligned(h * BLK + start, TOK), TOK), :] = src[
                (2 + h) * TOK : (3 + h) * TOK, :
            ]
    meta = keep[6 * TOK :, :].astype(F32) + got[6 * TOK :, :].astype(F32)
    kv_send[0, 2 * BLK :, :] = meta.astype(BF16)
    for n in range(1, SIDE):
        kv_send[n] = kv_send[0]


def queries_kernel(q_blk, kv, q_send):
    u = spot()[6]
    tile = sum(kv[n, 2 * BLK :, :].astype(F32) for n in range(SIDE))
    tile = pltpu.roll(tile, (u & 3) * 32, 1)
    tile = jnp.where(iota((META, 128), 0) >> 2 == u >> 2, tile, 0.0).astype(BF16)
    for n in range(SIDE):
        q_send[n, :QROWS, :] = q_blk[...]
        q_send[n, QROWS:, :] = tile


def pages_kernel(qs_far, old_k, old_v, page_row, page_len, x_send, qs, sem):
    copy = pltpu.make_async_copy(qs_far.at[:, pl.ds(QROWS, META), :], qs, sem)
    copy.start()
    copy.wait()
    sub, lane = iota((META, 128), 0), iota((META, 128), 1)
    tile = sum(qs[n].astype(F32) for n in range(SIDE))
    for n in range(OLD):
        tile = jnp.where((sub == 8) & (lane == n), page_row[0, n].astype(F32), tile)
        tile = jnp.where((sub == 9) & (lane == n), page_len[0, n].astype(F32), tile)
    for n in range(NG):
        x_send[n, :HALF, :] = old_k[:, n * TWO : (n + 1) * TWO]
        x_send[n, HALF : 2 * HALF, :] = old_v[:, n * TWO : (n + 1) * TWO]
        x_send[n, 2 * HALF :, :HEAD] = tile.astype(BF16)
        x_send[n, 2 * HALF :, HEAD:] = jnp.zeros((META, HEAD), BF16)


def attend_kernel(qs_far, kv_far, out, qs, kv, vs, tri, qx_a, qx_b, kx_a, kx_b, s_a, s_b, sems):
    _, _, z, y, core, _, _ = spot()
    load_kv = pltpu.make_async_copy(kv_far, kv, sems.at[0])
    load_q = pltpu.make_async_copy(qs_far, qs, sems.at[1])
    load_kv.start()
    load_q.start()
    row, col = iota((BLK, BLK), 0), iota((BLK, BLK), 1)
    tri[...] = jnp.where(col > row, HIDE, 0.0)
    same = jnp.where(row == col, 1.0, 0.0).astype(BF16)
    for h in range(4):
        qx_a[h * BLK : (h + 1) * BLK, HEAD:] = same
        qx_b[h * BLK : (h + 1) * BLK, HEAD:] = same
    vs[:, HEAD:] = jnp.where(iota((KEYS, HEAD), 1) == 0, 1.0, 0.0).astype(BF16)
    load_kv.wait()
    for n in range(SIDE):
        at = slice(n * BLK, (n + 1) * BLK)
        flipped = jnp.transpose(kv[n, :BLK, :].astype(F32)).astype(BF16)
        kx_a[:HEAD, at] = flipped
        kx_b[:HEAD, at] = flipped
        vs[at, :HEAD] = kv[n, BLK : 2 * BLK, :]
    load_q.wait()

    def score(n, qx, kx, s):
        even = core == 0
        full = jnp.where(
            even,
            z + jnp.where(y < n, 1, 0),
            jnp.where(z < n, SIDE, jnp.where(z == n, y, 0)),
        )
        edge = jnp.where(jnp.where(even, y, z) == n, full, SIDE)
        for m in range(SIDE):
            hidden = jnp.where(m == edge, tri[...], HIDE)
            kx[HEAD:, m * BLK : (m + 1) * BLK] = jnp.where(m < full, 0.0, hidden).astype(BF16)
        qx[:, :HEAD] = qs[n, :QROWS, :]
        s[...] = jnp.dot(qx[...], kx[...], preferred_element_type=F32)

    def mix(n, s):
        lane = iota((BLK, 128), 1)
        stats = jnp.zeros((BLK, 128), F32)
        for part in range(2):
            rows = slice(part * 2 * BLK, (part + 1) * 2 * BLK)
            scores = s[rows, :]
            top = EXP2_SCALE * jnp.max(scores, axis=1, keepdims=True)
            top = jnp.maximum(top, LOWEST).astype(BF16).astype(F32)
            weights = jnp.exp2(scores * EXP2_SCALE - top).astype(BF16)
            mixed = jnp.dot(weights, vs[...], preferred_element_type=F32)
            out[n, rows, :] = mixed[:, :HEAD].astype(BF16)
            total = mixed[:, HEAD : HEAD + 1]
            high = total.astype(BF16).astype(F32)
            for h in range(2):
                one = slice(h * BLK, (h + 1) * BLK)
                at = part * 2 + h
                stats = jnp.where(lane == at, top[one], stats)
                stats = jnp.where(lane == 4 + at, high[one], stats)
                stats = jnp.where(lane == 8 + at, (total - high)[one], stats)
        out[n, QROWS:Q_MSG, :] = jnp.transpose(stats)[:META].astype(BF16)

    score(0, qx_a, kx_a, s_a)

    def two(i, _):
        score(2 * i + 1, qx_b, kx_b, s_b)
        mix(2 * i, s_a)
        score(jnp.minimum(2 * i + 2, SIDE - 1), qx_a, kx_a, s_a)
        mix(2 * i + 1, s_b)

    lax.fori_loop(0, SIDE // 2, two, None)


def decode_kernel(q, xr, k_own, v_own, k_dec, v_dec, _, out, ks, vs, cs, ds, sem):
    seq, _, _, _, core, _, _ = spot()
    for n in range(NG):
        ks[n * HALF : (n + 1) * HALF, :] = xr[n, :HALF, :]
        vs[n * HALF : (n + 1) * HALF, :] = xr[n, HALF : 2 * HALF, :]
    for dst, own, dec in ((ks, k_own, k_dec), (vs, v_own, v_dec)):
        dst[OLD_TOK : OLD_TOK + TOK, :] = own[...]
        dst[OLD_TOK + TOK :, :] = dec[...]

    def hot(flag):
        return jnp.where(flag, 1.0, 0.0).astype(BF16)

    def item(shape):
        i = iota(shape, 0)
        swapped = ((i >> 1) & 7) * 16 + (i >> 4) * 2 + (i & 1)
        return jnp.where(core == 0, swapped, i)

    which = item((ITEMS, 128))
    lane = iota((ITEMS, 128), 1)
    row = (which >> 2).astype(F32)
    count = jnp.where((which == seq) & (lane >= TOK) & (lane - TOK <= (seq & 3)), 1.0, 0.0)
    token = iota((128, 128), 0)
    page, at = (token >> 4).astype(F32), (token & 15).astype(F32)
    place_f = seq.astype(F32)
    old_token = iota((OLD_TOK, 128), 0)
    old_at = (old_token & 15).astype(F32)
    old_page = (old_token >> 4) - iota((OLD_TOK, 128), 1)
    old_count = 0.0
    for n in range(NG):
        meta = xr[n, 2 * HALF :, :HEAD].astype(F32)
        for part in (0, 4):
            high, low, owner, length = (meta[part + m : part + m + 1, :] for m in range(4))
            inside = (high == place_f) & (low == page) & (at < length) & (token < TOK)
            count = count + lax.dot_general(
                hot(row == owner), hot(inside), NT, preferred_element_type=F32
            )
        owner, length = meta[8:9, :], meta[9:10, :]
        inside = (old_page == n * OLD) & (old_at < length)
        old_count = old_count + lax.dot_general(
            hot(row == owner), hot(inside), NT, preferred_element_type=F32
        )
    cs[:, :OLD_TOK] = old_count
    cs[:, OLD_TOK:] = count

    order = hot(which == lane)
    stats = jnp.zeros((ITEMS, 128), F32)
    for h in range(HEADS):
        kv = slice(h // 4 * HEAD, (h // 4 + 1) * HEAD)
        query = jnp.dot(order, q[:, h * HEAD : (h + 1) * HEAD], preferred_element_type=F32).astype(BF16)
        scores = EXP2_SCALE * lax.dot_general(query, ks[:, kv], NT, preferred_element_type=F32)
        terms = cs[...]
        scores = jnp.where(terms > 0.5, scores, NEG)
        top = jnp.max(scores, axis=1, keepdims=True).astype(BF16).astype(F32)
        weights = (jnp.exp2(scores - top) * terms).astype(BF16)
        total = jnp.sum(weights.astype(F32), axis=1, keepdims=True)
        mixed = jnp.dot(weights, vs[:, kv], preferred_element_type=F32)
        ds[:, h * PER : (h + 1) * PER, :] = mixed.astype(BF16).reshape(SIDE, PER, HEAD)
        high = total.astype(BF16).astype(F32)
        stats = jnp.where(lane == h, top, stats)
        stats = jnp.where(lane == HEADS + h, high, stats)
        stats = jnp.where(lane == 2 * HEADS + h, total - high, stats)
    ds[:, HEADS * PER :, :] = stats.astype(BF16).reshape(SIDE, PER, 128)
    copy = pltpu.make_async_copy(ds, out.at[:, pl.ds(Q_MSG, DEC_MSG), :], sem)
    copy.start()
    copy.wait()


def combine(values, stats, split):
    mixes, tops, totals = [], [], []
    for h in range(HEADS):
        top_of = [s[:, h : h + 1] for s in stats]
        top = functools.reduce(jnp.maximum, top_of)
        total, mixed = 0.0, 0.0
        for value, s, t in zip(values, stats, top_of):
            factor = jnp.exp2(t - top)
            each = s[:, HEADS + h : HEADS + h + 1]
            if split:
                each = each + s[:, 2 * HEADS + h : 2 * HEADS + h + 1]
            total = total + each * factor
            mixed = mixed + value(h) * factor
        mixes.append(mixed)
        tops.append(top)
        totals.append(total)
    return mixes, tops, totals


def stat_tile(tops, totals, split=False):
    lane = iota((tops[0].shape[0], 128), 1)
    tile = jnp.zeros(lane.shape, F32)
    for h in range(HEADS):
        tile = jnp.where(lane == h, tops[h], tile)
        if split:
            high = totals[h].astype(BF16).astype(F32)
            tile = jnp.where(lane == HEADS + h, high, tile)
            tile = jnp.where(lane == 2 * HEADS + h, totals[h] - high, tile)
        else:
            tile = jnp.where(lane == HEADS + h, totals[h], tile)
    return tile


def merge_kernel(got, attn, dec_send):
    stats = [got[n, QROWS:Q_MSG, :].astype(F32) for n in range(SIDE)]
    tops = [s[0:4] for s in stats]
    top = functools.reduce(jnp.maximum, tops)
    factors = [jnp.exp2(t - top) for t in tops]
    total = sum(f * (s[4:8] + s[8:12]) for f, s in zip(factors, stats))
    shares = jnp.concatenate([f / total for f in factors] + [jnp.zeros((96, 128), F32)], 0)
    shares = jnp.transpose(shares)
    for h in range(4):
        rows = slice(h * BLK, (h + 1) * BLK)
        out = 0.0
        for n in range(SIDE):
            out = out + got[n, rows, :].astype(F32) * shares[:, n * 4 + h : n * 4 + h + 1]
        attn[rows, :] = out.astype(BF16)

    def values(n):
        return lambda h: got[n, Q_MSG + h * PER : Q_MSG + (h + 1) * PER, :].astype(F32)

    mixes, tops, totals = combine(
        [values(n) for n in range(SIDE)],
        [got[n, O_MSG - PER :, :].astype(F32) for n in range(SIDE)],
        True,
    )
    for m, piece in enumerate(mixes + [stat_tile(tops, totals)]):
        for n in range(SIDE):
            dec_send[n, 2 * m : 2 * m + 2, :] = piece[2 * n : 2 * n + 2, :]


def pair_kernel(got, attn, attn_keep, dec_keep, send):
    core = spot()[4]
    even = core == 0

    def values(n):
        return lambda h: got[n, 2 * h : 2 * h + 2, :]

    mixes, tops, totals = combine(
        [values(n) for n in range(SIDE)], [got[n, 16:18, :] for n in range(SIDE)], False
    )
    keep_stats = stat_tile(tops, totals)
    send_stats = stat_tile(tops, totals, True)
    dec_keep[8:, :] = jnp.broadcast_to(jnp.where(even, keep_stats[0:1], keep_stats[1:2]), (8, 128))
    sent = []
    for h in range(HEADS):
        dec_keep[h : h + 1, :] = jnp.where(even, mixes[h][0:1], mixes[h][1:2])
        sent.append(jnp.where(even, mixes[h][1:2], mixes[h][0:1]))
    sent.append(jnp.where(even, send_stats[1:2], send_stats[0:1]))
    sent.append(jnp.zeros((7, 128), F32))
    send[4 * TOK :, :] = jnp.concatenate(sent, 0).astype(BF16)
    for h in range(4):
        rows = slice(h * TOK, (h + 1) * TOK)
        attn_keep[rows, :] = attn[pl.ds(aligned(h * BLK + core * TOK, TOK), TOK), :]
        send[rows, :] = attn[pl.ds(aligned(h * BLK + (1 - core) * TOK, TOK), TOK), :]


def final_kernel(attn_keep, dec_keep, got, attn_out, dec_out):
    core = spot()[4]
    for h in range(4):
        rows = slice(h * TOK, (h + 1) * TOK)
        for src, head in ((attn_keep, core), (got, 1 - core)):
            attn_out[:, pl.ds(aligned((head * 4 + h) * HEAD, HEAD), HEAD)] = src[rows, :]
    theirs = got[4 * TOK :, :].astype(F32)
    other = theirs[8:9, :]
    for h in range(HEADS):
        top_a, top_b = dec_keep[8:9, h : h + 1], other[:, h : h + 1]
        total_a = dec_keep[8:9, HEADS + h : HEADS + h + 1]
        total_b = other[:, HEADS + h : HEADS + h + 1] + other[:, 2 * HEADS + h : 2 * HEADS + h + 1]
        top = jnp.maximum(top_a, top_b)
        scale_a, scale_b = jnp.exp2(top_a - top), jnp.exp2(top_b - top)
        mixed = dec_keep[h : h + 1, :] * scale_a + theirs[h : h + 1, :] * scale_b
        dec_out[h : h + 1, :] = (mixed / (total_a * scale_a + total_b * scale_b)).astype(BF16)


def exchange(x, groups):
    return lax.all_to_all(x, "seq", 0, 0, axis_index_groups=groups, tiled=True)


def to_other_core(x):
    return lax.ppermute(x, "seq", [(n, n ^ 1) for n in range(2 * SIDE * SIDE)])


def body(q_pre, k_pre, v_pre, old_k, old_v, src_page, page_row, page_len, q_dec, dec_k, dec_v):
    seq, grp = lax.axis_index("seq"), lax.axis_index("grp")
    far = pl.BlockSpec(memory_space=pltpu.HBM)
    anywhere = pl.BlockSpec(memory_space=pl.ANY)
    counts = page_row.shape[1]
    keep, send = call(
        split_kernel,
        [((PAIR_MSG, 128), BF16)] * 2,
        (q_pre, k_pre, v_pre, src_page, page_row, page_len),
        scratch=(
            pltpu.SMEM(src_page.shape, jnp.int32),
            pltpu.SMEM((1, counts), jnp.int32),
            pltpu.SMEM((1, counts), jnp.int32),
            pltpu.SemaphoreType.DMA((15,)),
        ),
        specs={n: far for n in range(6)},
    )
    got = to_other_core(send)
    kv_send, q_blk = call(
        keys_kernel,
        [((SIDE, KV_MSG, 128), BF16), ((QROWS, 128), BF16)],
        (keep, got),
    )
    kv = exchange(kv_send, KEY_GROUPS)
    (q_send,) = call(queries_kernel, [((SIDE, Q_MSG, 128), BF16)], (q_blk, kv))
    qs = exchange(q_send, QUERY_GROUPS)
    (x_send,) = call(
        pages_kernel,
        [((NG, X_MSG, TWO), BF16)],
        (qs, old_k.reshape(HALF, -1), old_v.reshape(HALF, -1), page_row, page_len),
        scratch=(pltpu.VMEM((SIDE, META, 128), BF16), pltpu.SemaphoreType.DMA),
        specs={0: far, 3: SMEM, 4: SMEM},
    )
    xr = lax.all_to_all(x_send, "grp", 0, 0, tiled=True)
    work = QROWS * SIDE * KEYS
    (o_send,) = call(
        attend_kernel,
        [((SIDE, O_MSG, 128), BF16)],
        (qs, kv),
        scratch=(
            pltpu.VMEM((SIDE, Q_MSG, 128), BF16),
            pltpu.VMEM((SIDE, KV_MSG, 128), BF16),
            pltpu.VMEM((KEYS, TWO), BF16),
            pltpu.VMEM((BLK, BLK), F32),
            pltpu.VMEM((QROWS, TWO), BF16),
            pltpu.VMEM((QROWS, TWO), BF16),
            pltpu.VMEM((TWO, KEYS), BF16),
            pltpu.VMEM((TWO, KEYS), BF16),
            pltpu.VMEM((QROWS, KEYS), F32),
            pltpu.VMEM((QROWS, KEYS), F32),
            pltpu.SemaphoreType.DMA((2,)),
        ),
        specs={0: far, 1: far},
        cost=pl.CostEstimate(flops=work * 512, bytes_accessed=4 * 1024 * 1024, transcendentals=work),
    )

    q_mine = lax.dynamic_slice_in_dim(q_dec, grp * HEADS * HEAD, HEADS * HEAD, 2)
    q_mine = q_mine.reshape(ITEMS, HEADS * HEAD)

    def own_tokens(x):
        part = lax.dynamic_slice(x, (seq // STEPS, 0, grp * TWO), (1, STEPS, TWO))[0]
        return jnp.pad(part, ((0, TOK - STEPS), (0, 0)))

    (o_send,) = call(
        decode_kernel,
        [((SIDE, O_MSG, 128), BF16)],
        (q_mine, xr, k_pre, v_pre, own_tokens(dec_k), own_tokens(dec_v), o_send),
        scratch=(
            pltpu.VMEM((DEC_TOK, TWO), BF16),
            pltpu.VMEM((DEC_TOK, TWO), BF16),
            pltpu.VMEM((ITEMS, DEC_TOK), F32),
            pltpu.VMEM((SIDE, DEC_MSG, 128), BF16),
            pltpu.SemaphoreType.DMA,
        ),
        specs={6: anywhere},
        out_specs=[anywhere],
        alias={6: 0},
    )
    attn, dec_send = call(
        merge_kernel,
        [((QROWS, 128), BF16), ((SIDE, 18, 128), F32)],
        (exchange(o_send, QUERY_GROUPS),),
    )
    attn_keep, dec_keep, last = call(
        pair_kernel,
        [((4 * TOK, 128), BF16), ((16, 128), F32), ((LAST_MSG, 128), BF16)],
        (exchange(dec_send, KEY_GROUPS), attn),
    )
    attn_out, dec_out = call(
        final_kernel,
        [((TOK, HEADS * HEAD), BF16), ((HEADS, HEAD), BF16)],
        (attn_keep, dec_keep, to_other_core(last)),
    )
    return attn_out, dec_out


def solution(mesh):
    return jax.shard_map(
        body,
        mesh=mesh,
        in_specs=(
            P("seq", "grp"),
            P("seq", "grp"),
            P("seq", "grp"),
            P("seq", "grp", None, None),
            P("seq", "grp", None, None),
            P("seq", None),
            P("seq", "grp"),
            P("seq", "grp"),
            P(),
            P(),
            P(),
        ),
        out_specs=(P("seq", "grp"), P(("seq", "grp"), None)),
        check_vma=False,
    )
```

```python
import functools
import math

import jax
import jax.numpy as jnp
from jax import lax
from jax.experimental import pallas as pl
from jax.experimental.pallas import tpu as pltpu
from jax.sharding import PartitionSpec as P

HEAD = 128
PAGE = 16
OLD = 10
NEWP = 2
ROWS = 32
STEPS = 4
ITEMS = ROWS * STEPS
SIDE = 8
NG = 4
TOK = 64
BLK = 2 * TOK
KEYS = SIDE * BLK
QROWS = 4 * BLK
HEADS = 8
TWO = 2 * HEAD
EXP2_SCALE = math.log2(math.e) / math.sqrt(HEAD)
NEG = -(2.0**100)
HIDE = -(2.0**80)
LOWEST = -(2.0**60)
META = 16
PAIR_MSG = 6 * TOK + META
HALF = OLD * PAGE
X_MSG = 2 * HALF + META
OLD_TOK = NG * HALF
DEC_TOK = OLD_TOK + 128
PER = ITEMS // SIDE
DEC_MSG = HEADS * PER + PER
KV_DEC = 2 * BLK + META
KV_MSG = KV_DEC + DEC_MSG
FRONT = META + KEYS
CHUNK = FRONT + KEYS
PAGES = KEYS // PAGE
LAST_MSG = 4 * TOK + 16
FRESH = 16
NT = (((1,), (1,)), ((), ()))
F32 = jnp.float32
BF16 = jnp.bfloat16


def seq_of(z, y, core):
    return (z * SIDE + y) * 2 + core


ALONG_Z = [[[seq_of(i, j, c) for i in range(SIDE)] for j in range(SIDE)] for c in range(2)]
ALONG_Y = [[[seq_of(j, i, c) for i in range(SIDE)] for j in range(SIDE)] for c in range(2)]
KEY_GROUPS = ALONG_Z[0] + ALONG_Y[1]
QUERY_GROUPS = ALONG_Y[0] + ALONG_Z[1]


def iota(shape, dim):
    return lax.broadcasted_iota(jnp.int32, shape, dim)


def spot():
    seq, grp = lax.axis_index("seq"), lax.axis_index("grp")
    core = seq & 1
    y = (seq >> 1) & (SIDE - 1)
    z = seq >> 4
    even = core == 0
    return seq, grp, z, y, core, jnp.where(even, z, y), jnp.where(even, y, z)


def aligned(x, by):
    return pl.multiple_of(x, by)


def call(kernel, outs, args, scratch=(), limit=32, specs=None, out_specs=None, cost=None, alias=None):
    whole = pl.BlockSpec(memory_space=pltpu.VMEM)
    name = kernel.__name__.removesuffix("_kernel")
    return pl.pallas_call(
        kernel,
        out_shape=[jax.ShapeDtypeStruct(s, t) for s, t in outs],
        in_specs=[specs.get(n, whole) if specs else whole for n in range(len(args))],
        out_specs=out_specs or [whole] * len(outs),
        scratch_shapes=list(scratch),
        compiler_params=pltpu.CompilerParams(vmem_limit_bytes=limit * 1024 * 1024),
        cost_estimate=cost,
        input_output_aliases=alias or {},
        name=name,
    )(*args)


SMEM = pl.BlockSpec(memory_space=pltpu.SMEM)


def pages_kernel(old_k, old_v, src_page, page_row, page_len, *rest):
    outs, (src_s, row_s, len_s, sems) = rest[:NG], rest[NG:]
    grp = spot()[1]
    pairs = [(src_page, src_s), (page_row, row_s), (page_len, len_s)]
    for d in range(NG):
        cols = pl.ds(aligned(((grp + d) % NG) * TWO, TWO), TWO)
        pairs.append((old_k.at[:, cols], outs[d].at[pl.ds(0, HALF), :]))
        pairs.append((old_v.at[:, cols], outs[d].at[pl.ds(HALF, HALF), :]))
    copies = [pltpu.make_async_copy(a, b, sems.at[n]) for n, (a, b) in enumerate(pairs)]
    for copy in copies:
        copy.start()
    for copy in copies[:3]:
        copy.wait()
    sub, lane = iota((META, TWO), 0), iota((META, TWO), 1)
    tile = jnp.zeros((META, TWO), F32)
    for n in range(NEWP):
        src = src_s[0, grp * NEWP + n]
        values = (src >> 2, src & 3, row_s[0, OLD + n], len_s[0, OLD + n])
        for m, value in enumerate(values):
            tile = jnp.where((lane == n) & (sub == m), value.astype(F32), tile)
    for n in range(OLD):
        tile = jnp.where((sub == 8) & (lane == n), row_s[0, n].astype(F32), tile)
        tile = jnp.where((sub == 9) & (lane == n), len_s[0, n].astype(F32), tile)
    for d in range(NG):
        outs[d][2 * HALF :, :] = tile.astype(BF16)
    for copy in copies[3:]:
        copy.wait()


def split_kernel(q, k, v, x0, x1, x2, x3, keep, send, sems):
    _, _, _, _, core, w, u = spot()
    pairs = []
    for dst, head in ((keep, core), (send, 1 - core)):
        one = pl.ds(aligned(head * HEAD, HEAD), HEAD)
        pairs.append((k.at[:, one], dst.at[pl.ds(0, TOK), :]))
        pairs.append((v.at[:, one], dst.at[pl.ds(TOK, TOK), :]))
        for h in range(4):
            cols = pl.ds(aligned((head * 4 + h) * HEAD, HEAD), HEAD)
            pairs.append((q.at[:, cols], dst.at[pl.ds((2 + h) * TOK, TOK), :]))
    copies = [pltpu.make_async_copy(a, b, sems.at[n]) for n, (a, b) in enumerate(pairs)]
    for copy in copies:
        copy.start()
    fresh = (iota((META, 128), 0) < 4) & (iota((META, 128), 1) < NEWP)
    for dst, at in ((keep, w), (send, u)):
        tile = jnp.zeros((META, 128), F32)
        for d, x in enumerate((x0, x1, x2, x3)):
            part = jnp.where(fresh, x[2 * HALF :, :HEAD].astype(F32), 0.0)
            tile = tile + pltpu.roll(part, at * 16 + core * 8 + d * NEWP, 1)
        dst[6 * TOK :, :] = tile.astype(BF16)
    for copy in copies:
        copy.wait()


def local_kernel(keep, got, q, x0, x1, x2, x3, k_dec, v_dec, kv_send, q_blk, ks, vs, cs, kb):
    seq, _, _, _, core, _, _ = spot()
    for src, start in ((keep, core * TOK), (got, (1 - core) * TOK)):
        kb[pl.ds(aligned(start, TOK), TOK), :] = src[:TOK, :].astype(F32)
        kv_send[0, pl.ds(aligned(BLK + start, TOK), TOK), :] = src[TOK : 2 * TOK, :]
        for h in range(4):
            q_blk[pl.ds(aligned(h * BLK + start, TOK), TOK), :] = src[
                (2 + h) * TOK : (3 + h) * TOK, :
            ]
    kv_send[0, :BLK, :] = jnp.transpose(kb[...]).astype(BF16)
    meta = keep[6 * TOK :, :].astype(F32) + got[6 * TOK :, :].astype(F32)
    kv_send[0, 2 * BLK : KV_DEC, :] = meta.astype(BF16)
    for n in range(1, SIDE):
        kv_send[n, :KV_DEC, :] = kv_send[0, :KV_DEC, :]

    parts = (x0, x1, x2, x3)
    for n, part in enumerate(parts):
        ks[n * HALF : (n + 1) * HALF, :] = part[:HALF, :]
        vs[n * HALF : (n + 1) * HALF, :] = part[HALF : 2 * HALF, :]
    ks[OLD_TOK:, :] = k_dec[...]
    vs[OLD_TOK:, :] = v_dec[...]

    def hot(flag):
        return jnp.where(flag, 1.0, 0.0).astype(BF16)

    i = iota((ITEMS, 128), 0)
    swapped = ((i >> 1) & 7) * 16 + (i >> 4) * 2 + (i & 1)
    which = jnp.where(core == 0, i, swapped)
    lane = iota((ITEMS, 128), 1)
    row = (which >> 2).astype(F32)
    token = iota((OLD_TOK, 128), 0)
    at = (token & 15).astype(F32)
    page = (token >> 4) - iota((OLD_TOK, 128), 1)
    count = 0.0
    for n, part in enumerate(parts):
        numbers = part[2 * HALF :, :HEAD].astype(F32)
        owner, length = numbers[8:9, :], numbers[9:10, :]
        inside = (page == n * OLD) & (at < length)
        count = count + lax.dot_general(
            hot(row == owner), hot(inside), NT, preferred_element_type=F32
        )
    cs[:, :OLD_TOK] = count
    cs[:, OLD_TOK:] = jnp.where((which == seq) & (lane <= (seq & 3)), 1.0, 0.0)

    order = hot(which == lane)
    stats = jnp.zeros((ITEMS, 128), F32)
    for h in range(HEADS):
        kv = slice(h // 4 * HEAD, (h // 4 + 1) * HEAD)
        query = jnp.dot(order, q[:, h * HEAD : (h + 1) * HEAD], preferred_element_type=F32).astype(BF16)
        scores = EXP2_SCALE * lax.dot_general(query, ks[:, kv], NT, preferred_element_type=F32)
        terms = cs[...]
        scores = jnp.where(terms > 0.5, scores, NEG)
        top = jnp.max(scores, axis=1, keepdims=True).astype(BF16).astype(F32)
        weights = (jnp.exp2(scores - top) * terms).astype(BF16)
        total = jnp.sum(weights.astype(F32), axis=1, keepdims=True)
        mixed = jnp.dot(weights, vs[:, kv], preferred_element_type=F32)
        rows = slice(KV_DEC + h * PER, KV_DEC + (h + 1) * PER)
        kv_send[:, rows, :] = mixed.astype(BF16).reshape(SIDE, PER, HEAD)
        high = total.astype(BF16).astype(F32)
        stats = jnp.where(lane == h, top, stats)
        stats = jnp.where(lane == HEADS + h, high, stats)
        stats = jnp.where(lane == 2 * HEADS + h, total - high, stats)
    kv_send[:, KV_DEC + HEADS * PER :, :] = stats.astype(BF16).reshape(SIDE, PER, 128)


def attend_kernel(q, q_dec, *refs):
    bufs = refs[:9]
    attn, fresh_o, fresh_s = refs[9:12]
    vs_a, vs_b, tri, qx, kx_a, kx_b, s_a, s_b, acc, tops = refs[12:]
    seq, _, z, y, core, _, u = spot()
    even = core == 0
    keys_at = [bufs[d] if d < 5 else bufs[d + 1] for d in range(SIDE)]
    row, col = iota((BLK, BLK), 0), iota((BLK, BLK), 1)
    tri[...] = jnp.where(col > row, HIDE, 0.0)
    same = jnp.where(row == col, 1.0, 0.0).astype(BF16)
    qx[:, :HEAD] = q[...]
    for h in range(4):
        qx[h * BLK : (h + 1) * BLK, HEAD:] = same
    first = jnp.where(iota((KEYS, HEAD), 1) == 0, 1.0, 0.0).astype(BF16)
    vs_a[:, HEAD:] = first
    vs_b[:, HEAD:] = first
    acc[...] = jnp.zeros_like(acc)
    tops[...] = jnp.full_like(tops, LOWEST)

    numbers = jnp.concatenate([ref[:META, :].astype(F32) for ref in keys_at], axis=1)
    source = numbers[0:1, :] * 4.0 + numbers[1:2, :]
    mine = numbers[2:3, :] == (seq >> 2).astype(F32)
    slots = source.shape[1]
    live = mine & (iota((PAGE, slots), 0).astype(F32) < numbers[3:4, :])
    live = jnp.where(live, 1.0, 0.0).astype(BF16)
    spread = iota((PAGES, KEYS), 1) >> 4 == iota((PAGES, KEYS), 0)
    spread = jnp.where(spread, 1.0, 0.0).astype(BF16)
    at = (iota((PAGE, KEYS), 1) & 15) == iota((PAGE, KEYS), 0)

    def far(d):
        return (u - d + SIDE) & (SIDE - 1)

    def score(d, kx, vs, s):
        n = far(d)
        full = jnp.where(
            even,
            z + jnp.where(n < y, 1, 0),
            jnp.where(n < z, SIDE, jnp.where(n == z, y, 0)),
        )
        edge = jnp.where(n == u, full, SIDE)
        for m in range(SIDE):
            cols = slice(m * BLK, (m + 1) * BLK)
            kx[:HEAD, cols] = keys_at[d][META + m * BLK : META + (m + 1) * BLK, :]
            hidden = jnp.where(m == edge, tri[...], HIDE)
            kx[HEAD:, cols] = jnp.where(m < full, 0.0, hidden).astype(BF16)
        vs[:, :HEAD] = bufs[5][...] if d == 4 else keys_at[d][FRONT:, :]
        s[...] = jnp.dot(qx[...], kx[...], preferred_element_type=F32)

    def mix(s, vs):
        for part in range(2):
            rows = slice(part * 2 * BLK, (part + 1) * 2 * BLK)
            scores = s[rows, :]
            before = tops[rows, :]
            top = jnp.maximum(before, EXP2_SCALE * jnp.max(scores, axis=1, keepdims=True))
            tops[rows, :] = top
            weights = jnp.exp2(scores * EXP2_SCALE - top[:, :1]).astype(BF16)
            mixed = jnp.dot(weights, vs[...], preferred_element_type=F32)
            acc[rows, :] = acc[rows, :] * jnp.exp2(before - top)[:, :1] + mixed

    def copied(d, kx, vs, state):
        before, mixed = state
        n = far(d)
        page = iota((PAGES, slots), 0)
        w = page >> 3
        chip = jnp.where(even, w * SIDE + n, n * SIDE + w)
        page = (chip * SIDE + (page & 7)).astype(F32)
        there = jnp.where(source == page, 1.0, 0.0).astype(BF16)
        count = lax.dot_general(live, there, NT, preferred_element_type=F32)
        high = count.astype(BF16)
        low = (count - high.astype(F32)).astype(BF16)
        count = jnp.dot(high, spread, preferred_element_type=F32) + jnp.dot(
            low, spread, preferred_element_type=F32
        )
        terms = jnp.sum(jnp.where(at, count, 0.0), axis=0, keepdims=True)
        scores = EXP2_SCALE * jnp.dot(q_dec[...], kx[:HEAD, :], preferred_element_type=F32)
        scores = jnp.where(terms > 0.5, scores, NEG)
        top = jnp.max(scores, axis=1, keepdims=True).astype(BF16).astype(F32)
        top = jnp.maximum(before, top)
        weights = (jnp.exp2(scores - top) * terms).astype(BF16)
        mixed = mixed * jnp.exp2(before - top)
        return top, mixed + jnp.dot(weights, vs[...], preferred_element_type=F32)

    sides = ((kx_a, vs_a, s_a), (kx_b, vs_b, s_b))
    state = (jnp.full((FRESH, 1), NEG, F32), jnp.zeros((FRESH, TWO), F32))
    score(0, *sides[0])
    for d in range(SIDE):
        kx, vs, s = sides[d % 2]
        if d + 1 < SIDE:
            score(d + 1, *sides[(d + 1) % 2])
        mix(s, vs)
        state = copied(d, kx, vs, state)
    attn[...] = (acc[:, :HEAD] / acc[:, HEAD : HEAD + 1]).astype(BF16)
    top, mixed = state
    fresh_o[...] = mixed[:, :HEAD]
    lane = iota((FRESH, 128), 1)
    fresh_s[...] = jnp.where(lane == 0, top, jnp.where(lane == 1, mixed[:, HEAD : HEAD + 1], 0.0))


def combine(values, stats, split):
    mixes, tops, totals = [], [], []
    for h in range(HEADS):
        top_of = [s[:, h : h + 1] for s in stats]
        top = functools.reduce(jnp.maximum, top_of)
        total, mixed = 0.0, 0.0
        for value, s, t in zip(values, stats, top_of):
            factor = jnp.exp2(t - top)
            each = s[:, HEADS + h : HEADS + h + 1]
            if split:
                each = each + s[:, 2 * HEADS + h : 2 * HEADS + h + 1]
            total = total + each * factor
            mixed = mixed + value(h) * factor
        mixes.append(mixed)
        tops.append(top)
        totals.append(total)
    return mixes, tops, totals


def stat_tile(tops, totals, split=False):
    lane = iota((tops[0].shape[0], 128), 1)
    tile = jnp.zeros(lane.shape, F32)
    for h in range(HEADS):
        tile = jnp.where(lane == h, tops[h], tile)
        if split:
            high = totals[h].astype(BF16).astype(F32)
            tile = jnp.where(lane == HEADS + h, high, tile)
            tile = jnp.where(lane == 2 * HEADS + h, totals[h] - high, tile)
        else:
            tile = jnp.where(lane == HEADS + h, totals[h], tile)
    return tile


def merge_kernel(got, chunk, dec_send):
    chunk[:META, :] = sum(got[n, 2 * BLK : KV_DEC, :].astype(F32) for n in range(SIDE)).astype(BF16)
    for n in range(SIDE):
        chunk[META + n * BLK : META + (n + 1) * BLK, :] = got[n, :BLK, :]
        chunk[FRONT + n * BLK : FRONT + (n + 1) * BLK, :] = got[n, BLK : 2 * BLK, :]

    def values(n):
        return lambda h: got[n, KV_DEC + h * PER : KV_DEC + (h + 1) * PER, :].astype(F32)

    mixes, tops, totals = combine(
        [values(n) for n in range(SIDE)],
        [got[n, KV_MSG - PER :, :].astype(F32) for n in range(SIDE)],
        True,
    )
    for m, piece in enumerate(mixes + [stat_tile(tops, totals)]):
        for n in range(SIDE):
            dec_send[n, 2 * m : 2 * m + 2, :] = piece[2 * n : 2 * n + 2, :]


def pair_kernel(got, attn, fresh_o, fresh_s, attn_keep, dec_keep, send):
    core = spot()[4]
    even = core == 0

    def values(n):
        return lambda h: got[n, 2 * h : 2 * h + 2, :]

    def fresh(h):
        return jnp.concatenate([fresh_o[h % 4 : h % 4 + 1, :], fresh_o[4 + h % 4 : 5 + h % 4, :]], 0)

    lane = iota((2, 128), 1)
    stats = jnp.zeros((2, 128), F32)
    for h in range(HEADS):
        both = jnp.concatenate([fresh_s[h % 4 : h % 4 + 1, :], fresh_s[4 + h % 4 : 5 + h % 4, :]], 0)
        here = core == h // 4
        stats = jnp.where(lane == h, jnp.where(here, both[:, 0:1], NEG), stats)
        stats = jnp.where(lane == HEADS + h, jnp.where(here, both[:, 1:2], 0.0), stats)
    mixes, tops, totals = combine(
        [values(n) for n in range(SIDE)] + [fresh],
        [got[n, 16:18, :] for n in range(SIDE)] + [stats],
        False,
    )
    keep_stats = stat_tile(tops, totals)
    send_stats = stat_tile(tops, totals, True)
    dec_keep[8:, :] = jnp.broadcast_to(jnp.where(even, keep_stats[0:1], keep_stats[1:2]), (8, 128))
    sent = []
    for h in range(HEADS):
        dec_keep[h : h + 1, :] = jnp.where(even, mixes[h][0:1], mixes[h][1:2])
        sent.append(jnp.where(even, mixes[h][1:2], mixes[h][0:1]))
    sent.append(jnp.where(even, send_stats[1:2], send_stats[0:1]))
    sent.append(jnp.zeros((7, 128), F32))
    send[4 * TOK :, :] = jnp.concatenate(sent, 0).astype(BF16)
    for h in range(4):
        rows = slice(h * TOK, (h + 1) * TOK)
        attn_keep[rows, :] = attn[pl.ds(aligned(h * BLK + core * TOK, TOK), TOK), :]
        send[rows, :] = attn[pl.ds(aligned(h * BLK + (1 - core) * TOK, TOK), TOK), :]


def final_kernel(attn_keep, dec_keep, got, attn_out, dec_out):
    core = spot()[4]
    for h in range(4):
        rows = slice(h * TOK, (h + 1) * TOK)
        for src, head in ((attn_keep, core), (got, 1 - core)):
            attn_out[:, pl.ds(aligned((head * 4 + h) * HEAD, HEAD), HEAD)] = src[rows, :]
    theirs = got[4 * TOK :, :].astype(F32)
    other = theirs[8:9, :]
    for h in range(HEADS):
        top_a, top_b = dec_keep[8:9, h : h + 1], other[:, h : h + 1]
        total_a = dec_keep[8:9, HEADS + h : HEADS + h + 1]
        total_b = other[:, HEADS + h : HEADS + h + 1] + other[:, 2 * HEADS + h : 2 * HEADS + h + 1]
        top = jnp.maximum(top_a, top_b)
        scale_a, scale_b = jnp.exp2(top_a - top), jnp.exp2(top_b - top)
        mixed = dec_keep[h : h + 1, :] * scale_a + theirs[h : h + 1, :] * scale_b
        dec_out[h : h + 1, :] = (mixed / (total_a * scale_a + total_b * scale_b)).astype(BF16)


def exchange(x, groups):
    return lax.all_to_all(x, "seq", 0, 0, axis_index_groups=groups, tiled=True)


def to_other_core(x):
    return lax.ppermute(x, "seq", [(n, n ^ 1) for n in range(2 * SIDE * SIDE)])


def along_queries(x, by):
    pairs = []
    for group in QUERY_GROUPS:
        pairs += [(group[n], group[(n + by) % SIDE]) for n in range(SIDE)]
    return lax.ppermute(x, "seq", pairs)


def ring(block):
    ahead, back = [block], [block]
    for _ in range(SIDE // 2 - 1):
        ahead.append(along_queries(ahead[-1], 1))
        back.append(along_queries(back[-1], -1))
    front = along_queries(ahead[-1][:FRONT], 1)
    rest = along_queries(back[-1][FRONT:], -1)
    return ahead + [front, rest] + back[:0:-1]


def body(q_pre, k_pre, v_pre, old_k, old_v, src_page, page_row, page_len, q_dec, dec_k, dec_v):
    seq, grp = lax.axis_index("seq"), lax.axis_index("grp")
    core = seq & 1
    far = pl.BlockSpec(memory_space=pltpu.HBM)
    counts = page_row.shape[1]
    xs = call(
        pages_kernel,
        [((X_MSG, TWO), BF16)] * NG,
        (old_k.reshape(HALF, -1), old_v.reshape(HALF, -1), src_page, page_row, page_len),
        scratch=(
            pltpu.SMEM(src_page.shape, jnp.int32),
            pltpu.SMEM((1, counts), jnp.int32),
            pltpu.SMEM((1, counts), jnp.int32),
            pltpu.SemaphoreType.DMA((3 + 2 * NG,)),
        ),
        specs={n: far for n in range(5)},
    )
    xs = [xs[0]] + [
        lax.ppermute(xs[d], "grp", [(n, (n + d) % NG) for n in range(NG)]) for d in range(1, NG)
    ]
    keep, send = call(
        split_kernel,
        [((PAIR_MSG, 128), BF16)] * 2,
        (q_pre, k_pre, v_pre, *xs),
        scratch=(pltpu.SemaphoreType.DMA((12,)),),
        specs={n: far for n in range(3)},
    )
    q_mine = lax.dynamic_slice_in_dim(q_dec, grp * HEADS * HEAD, HEADS * HEAD, 2)
    q_mine = q_mine.reshape(ITEMS, HEADS * HEAD)

    def own_tokens(x):
        part = lax.dynamic_slice(x, (seq // STEPS, 0, grp * TWO), (1, STEPS, TWO))[0]
        return jnp.pad(part, ((0, 128 - STEPS), (0, 0)))

    kv_send, q_blk = call(
        local_kernel,
        [((SIDE, KV_MSG, 128), BF16), ((QROWS, 128), BF16)],
        (keep, to_other_core(send), q_mine, *xs, own_tokens(dec_k), own_tokens(dec_v)),
        scratch=(
            pltpu.VMEM((DEC_TOK, TWO), BF16),
            pltpu.VMEM((DEC_TOK, TWO), BF16),
            pltpu.VMEM((ITEMS, DEC_TOK), F32),
            pltpu.VMEM((BLK, HEAD), F32),
        ),
    )
    chunk, dec_send = call(
        merge_kernel,
        [((CHUNK, 128), BF16), ((SIDE, 18, 128), F32)],
        (exchange(kv_send, KEY_GROUPS),),
    )
    reduced = exchange(dec_send, QUERY_GROUPS)
    q_last = lax.dynamic_slice(
        q_dec,
        (seq // STEPS, seq % STEPS // 2 * 2, (grp * HEADS + core * 4) * HEAD),
        (1, 2, 4 * HEAD),
    )
    q_last = jnp.pad(q_last.reshape(HEADS, HEAD), ((0, FRESH - HEADS), (0, 0)))
    work = QROWS * SIDE * KEYS
    attn, fresh_o, fresh_s = call(
        attend_kernel,
        [((QROWS, HEAD), BF16), ((FRESH, 128), F32), ((FRESH, 128), F32)],
        (q_blk, q_last, *ring(chunk)),
        scratch=(
            pltpu.VMEM((KEYS, TWO), BF16),
            pltpu.VMEM((KEYS, TWO), BF16),
            pltpu.VMEM((BLK, BLK), F32),
            pltpu.VMEM((QROWS, TWO), BF16),
            pltpu.VMEM((TWO, KEYS), BF16),
            pltpu.VMEM((TWO, KEYS), BF16),
            pltpu.VMEM((QROWS, KEYS), F32),
            pltpu.VMEM((QROWS, KEYS), F32),
            pltpu.VMEM((QROWS, TWO), F32),
            pltpu.VMEM((QROWS, 128), F32),
        ),
        cost=pl.CostEstimate(flops=work * 512, bytes_accessed=4 * 1024 * 1024, transcendentals=work),
    )
    attn_keep, dec_keep, last = call(
        pair_kernel,
        [((4 * TOK, 128), BF16), ((16, 128), F32), ((LAST_MSG, 128), BF16)],
        (reduced, attn, fresh_o, fresh_s),
    )
    attn_out, dec_out = call(
        final_kernel,
        [((TOK, HEADS * HEAD), BF16), ((HEADS, HEAD), BF16)],
        (attn_keep, dec_keep, to_other_core(last)),
    )
    return attn_out, dec_out


def solution(mesh):
    return jax.shard_map(
        body,
        mesh=mesh,
        in_specs=(
            P("seq", "grp"),
            P("seq", "grp"),
            P("seq", "grp"),
            P("seq", "grp", None, None),
            P("seq", "grp", None, None),
            P("seq", None),
            P("seq", "grp"),
            P("seq", "grp"),
            P(),
            P(),
            P(),
        ),
        out_specs=(P("seq", "grp"), P(("seq", "grp"), None)),
        check_vma=False,
    )
```

```python
import functools
import math

import jax
import jax.numpy as jnp
from jax import lax
from jax.experimental import pallas as pl
from jax.experimental.pallas import tpu as pltpu
from jax.sharding import PartitionSpec as P

HEAD = 128
PAGE = 16
OLD = 10
NEWP = 2
ROWS = 32
STEPS = 4
ITEMS = ROWS * STEPS
SIDE = 8
NG = 4
TOK = 64
BLK = 2 * TOK
KEYS = SIDE * BLK
QROWS = 4 * BLK
HEADS = 8
TWO = 2 * HEAD
EXP2_SCALE = math.log2(math.e) / math.sqrt(HEAD)
NEG = -(2.0**100)
HIDE = -(2.0**80)
LOWEST = -(2.0**60)
META = 16
PAIR_MSG = 6 * TOK + META
HALF = OLD * PAGE
X_MSG = 2 * HALF + META
OLD_TOK = NG * HALF
DEC_TOK = OLD_TOK + 128
PER = ITEMS // SIDE
DEC_MSG = HEADS * PER + PER
KV_DEC = 2 * BLK + META
KV_MSG = KV_DEC + DEC_MSG
FRONT = META + KEYS
CHUNK = FRONT + KEYS
PAGES = KEYS // PAGE
LAST_MSG = 4 * TOK + 16
QUAD = 4
PAIR_DEC = 80
PAIR_ALL = CHUNK + PAIR_DEC
Q_META = QROWS
Q_DEC = QROWS + META
Q_MSG = Q_DEC + 32
O_FRESH = QROWS + META
O_MSG = O_FRESH + 16
FRESH = 4 * 16
NT = (((1,), (1,)), ((), ()))
F32 = jnp.float32
BF16 = jnp.bfloat16


def seq_of(z, y, core):
    return (z * SIDE + y) * 2 + core


ALONG_Z = [[[seq_of(i, j, c) for i in range(SIDE)] for j in range(SIDE)] for c in range(2)]
ALONG_Y = [[[seq_of(j, i, c) for i in range(SIDE)] for j in range(SIDE)] for c in range(2)]
KEY_GROUPS = ALONG_Z[0] + ALONG_Y[1]
QUERY_GROUPS = ALONG_Y[0] + ALONG_Z[1]
QUADS = [group[p::2] for group in QUERY_GROUPS for p in range(2)]
NEIGHBOURS = [(group[n], group[n ^ 1]) for group in QUERY_GROUPS for n in range(SIDE)]


def iota(shape, dim):
    return lax.broadcasted_iota(jnp.int32, shape, dim)


def spot():
    seq, grp = lax.axis_index("seq"), lax.axis_index("grp")
    core = seq & 1
    y = (seq >> 1) & (SIDE - 1)
    z = seq >> 4
    even = core == 0
    return seq, grp, z, y, core, jnp.where(even, z, y), jnp.where(even, y, z)


def aligned(x, by):
    return pl.multiple_of(x, by)


def call(kernel, outs, args, scratch=(), limit=32, specs=None, out_specs=None, cost=None, alias=None):
    whole = pl.BlockSpec(memory_space=pltpu.VMEM)
    name = kernel.__name__.removesuffix("_kernel")
    return pl.pallas_call(
        kernel,
        out_shape=[jax.ShapeDtypeStruct(s, t) for s, t in outs],
        in_specs=[specs.get(n, whole) if specs else whole for n in range(len(args))],
        out_specs=out_specs or [whole] * len(outs),
        scratch_shapes=list(scratch),
        compiler_params=pltpu.CompilerParams(vmem_limit_bytes=limit * 1024 * 1024),
        cost_estimate=cost,
        input_output_aliases=alias or {},
        name=name,
    )(*args)


SMEM = pl.BlockSpec(memory_space=pltpu.SMEM)


def pages_kernel(old_k, old_v, src_page, page_row, page_len, *rest):
    outs, (src_s, row_s, len_s, sems) = rest[:NG], rest[NG:]
    grp = spot()[1]
    pairs = [(src_page, src_s), (page_row, row_s), (page_len, len_s)]
    for d in range(NG):
        cols = pl.ds(aligned(((grp + d) % NG) * TWO, TWO), TWO)
        pairs.append((old_k.at[:, cols], outs[d].at[pl.ds(0, HALF), :]))
        pairs.append((old_v.at[:, cols], outs[d].at[pl.ds(HALF, HALF), :]))
    copies = [pltpu.make_async_copy(a, b, sems.at[n]) for n, (a, b) in enumerate(pairs)]
    for copy in copies:
        copy.start()
    for copy in copies[:3]:
        copy.wait()
    sub, lane = iota((META, TWO), 0), iota((META, TWO), 1)
    tile = jnp.zeros((META, TWO), F32)
    for n in range(NEWP):
        src = src_s[0, grp * NEWP + n]
        values = (src >> 2, src & 3, row_s[0, OLD + n], len_s[0, OLD + n])
        for m, value in enumerate(values):
            tile = jnp.where((lane == n) & (sub == m), value.astype(F32), tile)
    for n in range(OLD):
        tile = jnp.where((sub == 8) & (lane == n), row_s[0, n].astype(F32), tile)
        tile = jnp.where((sub == 9) & (lane == n), len_s[0, n].astype(F32), tile)
    for d in range(NG):
        outs[d][2 * HALF :, :] = tile.astype(BF16)
    for copy in copies[3:]:
        copy.wait()


def split_kernel(q, k, v, x0, x1, x2, x3, keep, send, sems):
    _, _, _, _, core, w, u = spot()
    pairs = []
    for dst, head in ((keep, core), (send, 1 - core)):
        one = pl.ds(aligned(head * HEAD, HEAD), HEAD)
        pairs.append((k.at[:, one], dst.at[pl.ds(0, TOK), :]))
        pairs.append((v.at[:, one], dst.at[pl.ds(TOK, TOK), :]))
        for h in range(4):
            cols = pl.ds(aligned((head * 4 + h) * HEAD, HEAD), HEAD)
            pairs.append((q.at[:, cols], dst.at[pl.ds((2 + h) * TOK, TOK), :]))
    copies = [pltpu.make_async_copy(a, b, sems.at[n]) for n, (a, b) in enumerate(pairs)]
    for copy in copies:
        copy.start()
    fresh = (iota((META, 128), 0) < 4) & (iota((META, 128), 1) < NEWP)
    for dst, at in ((keep, w), (send, u)):
        tile = jnp.zeros((META, 128), F32)
        for d, x in enumerate((x0, x1, x2, x3)):
            part = jnp.where(fresh, x[2 * HALF :, :HEAD].astype(F32), 0.0)
            tile = tile + pltpu.roll(part, at * 16 + core * 8 + d * NEWP, 1)
        dst[6 * TOK :, :] = tile.astype(BF16)
    for copy in copies:
        copy.wait()


def local_kernel(keep, got, q, x0, x1, x2, x3, k_dec, v_dec, kv_send, q_blk, ks, vs, cs, kb):
    seq, _, _, _, core, _, _ = spot()
    for src, start in ((keep, core * TOK), (got, (1 - core) * TOK)):
        kb[pl.ds(aligned(start, TOK), TOK), :] = src[:TOK, :].astype(F32)
        kv_send[0, pl.ds(aligned(BLK + start, TOK), TOK), :] = src[TOK : 2 * TOK, :]
        for h in range(4):
            q_blk[pl.ds(aligned(h * BLK + start, TOK), TOK), :] = src[
                (2 + h) * TOK : (3 + h) * TOK, :
            ]
    kv_send[0, :BLK, :] = jnp.transpose(kb[...]).astype(BF16)
    meta = keep[6 * TOK :, :].astype(F32) + got[6 * TOK :, :].astype(F32)
    kv_send[0, 2 * BLK : KV_DEC, :] = meta.astype(BF16)
    for n in range(1, SIDE):
        kv_send[n, :KV_DEC, :] = kv_send[0, :KV_DEC, :]

    parts = (x0, x1, x2, x3)
    for n, part in enumerate(parts):
        ks[n * HALF : (n + 1) * HALF, :] = part[:HALF, :]
        vs[n * HALF : (n + 1) * HALF, :] = part[HALF : 2 * HALF, :]
    ks[OLD_TOK:, :] = k_dec[...]
    vs[OLD_TOK:, :] = v_dec[...]

    def hot(flag):
        return jnp.where(flag, 1.0, 0.0).astype(BF16)

    i = iota((ITEMS, 128), 0)
    swapped = ((i >> 1) & 7) * 16 + (i >> 4) * 2 + (i & 1)
    which = jnp.where(core == 0, i, swapped)
    lane = iota((ITEMS, 128), 1)
    row = (which >> 2).astype(F32)
    token = iota((OLD_TOK, 128), 0)
    at = (token & 15).astype(F32)
    page = (token >> 4) - iota((OLD_TOK, 128), 1)
    count = 0.0
    for n, part in enumerate(parts):
        numbers = part[2 * HALF :, :HEAD].astype(F32)
        owner, length = numbers[8:9, :], numbers[9:10, :]
        inside = (page == n * OLD) & (at < length)
        count = count + lax.dot_general(
            hot(row == owner), hot(inside), NT, preferred_element_type=F32
        )
    cs[:, :OLD_TOK] = count
    cs[:, OLD_TOK:] = jnp.where((which == seq) & (lane <= (seq & 3)), 1.0, 0.0)

    order = hot(which == lane)
    stats = jnp.zeros((ITEMS, 128), F32)
    for h in range(HEADS):
        kv = slice(h // 4 * HEAD, (h // 4 + 1) * HEAD)
        query = jnp.dot(order, q[:, h * HEAD : (h + 1) * HEAD], preferred_element_type=F32).astype(BF16)
        scores = EXP2_SCALE * lax.dot_general(query, ks[:, kv], NT, preferred_element_type=F32)
        terms = cs[...]
        scores = jnp.where(terms > 0.5, scores, NEG)
        top = jnp.max(scores, axis=1, keepdims=True).astype(BF16).astype(F32)
        weights = (jnp.exp2(scores - top) * terms).astype(BF16)
        total = jnp.sum(weights.astype(F32), axis=1, keepdims=True)
        mixed = jnp.dot(weights, vs[:, kv], preferred_element_type=F32)
        rows = slice(KV_DEC + h * PER, KV_DEC + (h + 1) * PER)
        kv_send[:, rows, :] = mixed.astype(BF16).reshape(SIDE, PER, HEAD)
        high = total.astype(BF16).astype(F32)
        stats = jnp.where(lane == h, top, stats)
        stats = jnp.where(lane == HEADS + h, high, stats)
        stats = jnp.where(lane == 2 * HEADS + h, total - high, stats)
    kv_send[:, KV_DEC + HEADS * PER :, :] = stats.astype(BF16).reshape(SIDE, PER, 128)


def attend_kernel(qs, near, other, q_dec, out, *refs):
    vs, tri, sel = refs[:3]
    sides = (refs[3:8], refs[8:13])
    seq, _, z, y, core, w, u = spot()
    even = core == 0
    chunks = ((near, u), (other, u ^ 1))
    row, col = iota((BLK, BLK), 0), iota((BLK, BLK), 1)
    tri[...] = jnp.where(col > row, HIDE, 0.0)
    same = jnp.where(row == col, 1.0, 0.0).astype(BF16)
    for side in sides:
        for h in range(4):
            side[0][h * BLK : (h + 1) * BLK, HEAD:] = same
        for c, (chunk, _) in enumerate(chunks):
            for m in range(SIDE):
                cols = slice(m * BLK, (m + 1) * BLK)
                side[1 + c][:HEAD, cols] = chunk[META + m * BLK : META + (m + 1) * BLK, :]
    for c, (chunk, _) in enumerate(chunks):
        vs[c * KEYS : (c + 1) * KEYS, :HEAD] = chunk[FRONT:CHUNK, :]
    vs[:, HEAD:] = jnp.where(iota((2 * KEYS, HEAD), 1) == 0, 1.0, 0.0).astype(BF16)

    def score(j, qx, kx_a, kx_b, s_a, s_b):
        to = j * 2 + (u & 1)
        qx[:, :HEAD] = qs[j, :QROWS, :]
        for (_, n), kx, s in zip(chunks, (kx_a, kx_b), (s_a, s_b)):
            full = jnp.where(
                even,
                w + jnp.where(n < to, 1, 0),
                jnp.where(n < to, SIDE, jnp.where(n == to, w, 0)),
            )
            edge = jnp.where(n == to, w, SIDE)
            for m in range(SIDE):
                hidden = jnp.where(m == edge, tri[...], HIDE)
                hidden = jnp.where(m < full, 0.0, hidden).astype(BF16)
                kx[HEAD:, m * BLK : (m + 1) * BLK] = hidden
            s[...] = jnp.dot(qx[...], kx[...], preferred_element_type=F32)

    def mix(j, s_a, s_b):
        lane = iota((BLK, 128), 1)
        stats = jnp.zeros((BLK, 128), F32)
        for part in range(2):
            rows = slice(part * 2 * BLK, (part + 1) * 2 * BLK)
            both = (s_a[rows, :], s_b[rows, :])
            top = EXP2_SCALE * jnp.max(jnp.maximum(*both), axis=1, keepdims=True)
            top = jnp.maximum(top, LOWEST).astype(BF16).astype(F32)
            mixed = 0.0
            for c in range(2):
                weights = jnp.exp2(both[c] * EXP2_SCALE - top).astype(BF16)
                mixed = mixed + jnp.dot(
                    weights, vs[c * KEYS : (c + 1) * KEYS, :], preferred_element_type=F32
                )
            out[j, rows, :] = mixed[:, :HEAD].astype(BF16)
            total = mixed[:, HEAD : HEAD + 1]
            high = total.astype(BF16).astype(F32)
            for h in range(2):
                one = slice(h * BLK, (h + 1) * BLK)
                at = part * 2 + h
                stats = jnp.where(lane == at, top[one], stats)
                stats = jnp.where(lane == 4 + at, high[one], stats)
                stats = jnp.where(lane == 8 + at, (total - high)[one], stats)
        out[j, QROWS:O_FRESH, :] = jnp.transpose(stats)[:META].astype(BF16)

    score(0, *sides[0])
    for j in range(QUAD):
        if j + 1 < QUAD:
            score(j + 1, *sides[(j + 1) % 2])
        mix(j, *sides[j % 2][3:])

    def chip_of(there, across):
        return jnp.where(even, across * SIDE + there, there * SIDE + across)

    numbers = jnp.concatenate(
        [qs[j, Q_META : Q_META + 8, :].astype(F32) for j in range(QUAD)], axis=1
    )
    numbers = jnp.concatenate([numbers[0:4], numbers[4:8]], axis=1)
    source = numbers[0:1, :] * 4.0 + numbers[1:2, :]
    slots = source.shape[1]
    inside = iota((PAGE, slots), 0).astype(F32) < numbers[3:4, :]
    live = []
    for j in range(QUAD):
        owner = (chip_of(j * 2 + (u & 1), w) >> 1).astype(F32)
        live.append(jnp.where((numbers[2:3, :] == owner) & inside, 1.0, 0.0))
    live = jnp.concatenate(live, axis=0).astype(BF16)
    spread = iota((PAGES, KEYS), 1) >> 4 == iota((PAGES, KEYS), 0)
    spread = jnp.where(spread, 1.0, 0.0).astype(BF16)
    at = (iota((PAGE * QUAD, KEYS), 1) & 15) == (iota((PAGE * QUAD, KEYS), 0) & 15)

    pick = iota((16, ITEMS), 0)
    item = chip_of((pick >> 1) * 2 + (u & 1), w) * 2 + (pick & 1)
    pick = jnp.where((iota((16, ITEMS), 1) == item) & (pick < 8), 1.0, 0.0).astype(BF16)
    for h in range(4):
        cols = pl.ds(aligned((core * 4 + h) * HEAD, HEAD), HEAD)
        sel[h * 16 : (h + 1) * 16, :] = jnp.dot(
            pick, q_dec[:, cols], preferred_element_type=F32
        ).astype(BF16)

    all_scores, all_terms = [], []
    for c, (_, n) in enumerate(chunks):
        page = iota((PAGES, slots), 0)
        page = (chip_of(n, page >> 3) * SIDE + (page & 7)).astype(F32)
        there = jnp.where(source == page, 1.0, 0.0).astype(BF16)
        count = lax.dot_general(live, there, NT, preferred_element_type=F32)
        high = count.astype(BF16)
        low = (count - high.astype(F32)).astype(BF16)
        count = jnp.dot(high, spread, preferred_element_type=F32) + jnp.dot(
            low, spread, preferred_element_type=F32
        )
        count = jnp.where(at, count, 0.0)
        which = iota((16, KEYS), 0) >> 1
        terms = jnp.zeros((16, KEYS), F32)
        for j in range(QUAD):
            one = jnp.sum(count[j * PAGE : (j + 1) * PAGE], axis=0, keepdims=True)
            terms = jnp.where(which == j, one, terms)
        terms = jnp.concatenate([terms] * 4, axis=0)
        keys = sides[0][1 + c][:HEAD, :]
        scores = EXP2_SCALE * jnp.dot(sel[...], keys, preferred_element_type=F32)
        all_scores.append(jnp.where(terms > 0.5, scores, NEG))
        all_terms.append(terms)
    top = jnp.max(jnp.maximum(*all_scores), axis=1, keepdims=True).astype(BF16).astype(F32)
    mixed = 0.0
    for c in range(2):
        weights = (jnp.exp2(all_scores[c] - top) * all_terms[c]).astype(BF16)
        mixed = mixed + jnp.dot(
            weights, vs[c * KEYS : (c + 1) * KEYS, :], preferred_element_type=F32
        )
    total = mixed[:, HEAD : HEAD + 1]
    high = total.astype(BF16).astype(F32)
    lane = iota((FRESH, 128), 1)
    stats = jnp.where(lane == 0, top, jnp.where(lane == 1, high, 0.0))
    stats = jnp.where(lane == 2, total - high, stats)
    for j in range(QUAD):
        rows = [slice(h * 16 + 2 * j, h * 16 + 2 * j + 2) for h in range(4)]
        pieces = [mixed[r, :HEAD] for r in rows] + [stats[r] for r in rows]
        out[j, O_FRESH:, :] = jnp.concatenate(pieces, axis=0).astype(BF16)


def combine(values, stats, split):
    mixes, tops, totals = [], [], []
    for h in range(HEADS):
        top_of = [s[:, h : h + 1] for s in stats]
        top = functools.reduce(jnp.maximum, top_of)
        total, mixed = 0.0, 0.0
        for value, s, t in zip(values, stats, top_of):
            factor = jnp.exp2(t - top)
            each = s[:, HEADS + h : HEADS + h + 1]
            if split:
                each = each + s[:, 2 * HEADS + h : 2 * HEADS + h + 1]
            total = total + each * factor
            mixed = mixed + value(h) * factor
        mixes.append(mixed)
        tops.append(top)
        totals.append(total)
    return mixes, tops, totals


def stat_tile(tops, totals, split=False):
    lane = iota((tops[0].shape[0], 128), 1)
    tile = jnp.zeros(lane.shape, F32)
    for h in range(HEADS):
        tile = jnp.where(lane == h, tops[h], tile)
        if split:
            high = totals[h].astype(BF16).astype(F32)
            tile = jnp.where(lane == HEADS + h, high, tile)
            tile = jnp.where(lane == 2 * HEADS + h, totals[h] - high, tile)
        else:
            tile = jnp.where(lane == HEADS + h, totals[h], tile)
    return tile


def merge_kernel(got, send, keep):
    send[:META, :] = sum(got[n, 2 * BLK : KV_DEC, :].astype(F32) for n in range(SIDE)).astype(BF16)
    for n in range(SIDE):
        send[META + n * BLK : META + (n + 1) * BLK, :] = got[n, :BLK, :]
        send[FRONT + n * BLK : FRONT + (n + 1) * BLK, :] = got[n, BLK : 2 * BLK, :]

    def values(n):
        return lambda h: got[n, KV_DEC + h * PER : KV_DEC + (h + 1) * PER, :].astype(F32)

    mixes, tops, totals = combine(
        [values(n) for n in range(SIDE)],
        [got[n, KV_MSG - PER :, :].astype(F32) for n in range(SIDE)],
        True,
    )
    even = spot()[6] & 1 == 0

    def halves(x):
        a = jnp.concatenate([x[4 * n : 4 * n + 2] for n in range(QUAD)], axis=0)
        b = jnp.concatenate([x[4 * n + 2 : 4 * n + 4] for n in range(QUAD)], axis=0)
        return jnp.where(even, a, b), jnp.where(even, b, a)

    theirs = []
    for h in range(HEADS):
        mine, other = halves(mixes[h])
        keep[8 * h : 8 * h + 8, :] = mine
        theirs.append(other)
    mine, other = halves(stat_tile(tops, totals, True))
    keep[64:, :] = mine
    theirs += [other, jnp.zeros((8, 128), F32)]
    send[CHUNK:, :] = jnp.concatenate(theirs, axis=0).astype(BF16)


def queries_kernel(q_blk, near, other, keep, send):
    def kept(h):
        return keep[8 * h : 8 * h + 8, :]

    def came(h):
        return other[CHUNK + 8 * h : CHUNK + 8 * h + 8, :].astype(F32)

    mixes, tops, totals = combine(
        [kept, came], [keep[64:, :], other[CHUNK + 64 : CHUNK + 72, :].astype(F32)], True
    )
    pieces = mixes + [stat_tile(tops, totals, True)]
    numbers = jnp.concatenate(
        [near[:META, :].astype(F32)[:4], other[:META, :].astype(F32)[:4], jnp.zeros((8, 128), F32)], 0
    ).astype(BF16)
    for n in range(QUAD):
        send[n, :QROWS, :] = q_blk[...]
        send[n, Q_META:Q_DEC, :] = numbers
        rows = [piece[2 * n : 2 * n + 2] for piece in pieces] + [jnp.zeros((14, 128), F32)]
        send[n, Q_DEC:, :] = jnp.concatenate(rows, axis=0).astype(BF16)


def pair_kernel(got, qs, attn_keep, dec_keep, send, attn):
    core = spot()[4]
    even = core == 0
    stats = [got[n, QROWS:O_FRESH, :].astype(F32) for n in range(QUAD)]
    tops = [s[0:4] for s in stats]
    top = functools.reduce(jnp.maximum, tops)
    factors = [jnp.exp2(t - top) for t in tops]
    total = sum(f * (s[4:8] + s[8:12]) for f, s in zip(factors, stats))
    shares = jnp.concatenate([f / total for f in factors] + [jnp.zeros((112, 128), F32)], 0)
    shares = jnp.transpose(shares)
    for h in range(4):
        rows = slice(h * BLK, (h + 1) * BLK)
        out = 0.0
        for n in range(QUAD):
            out = out + got[n, rows, :].astype(F32) * shares[:, n * 4 + h : n * 4 + h + 1]
        attn[rows, :] = out.astype(BF16)

    def old(n):
        return lambda h: qs[n, Q_DEC:, :].astype(F32)[2 * h : 2 * h + 2]

    def fresh(n):
        return lambda h: got[n, O_FRESH:, :].astype(F32)[2 * (h % 4) : 2 * (h % 4) + 2]

    old_stats = [qs[n, Q_DEC:, :].astype(F32)[16:18] for n in range(QUAD)]
    fresh_stats = []
    lane = iota((2, 128), 1)
    for n in range(QUAD):
        tile = got[n, O_FRESH:, :].astype(F32)[8:]
        placed = jnp.zeros((2, 128), F32)
        for h in range(HEADS):
            both = tile[2 * (h % 4) : 2 * (h % 4) + 2]
            here = core == h // 4
            placed = jnp.where(lane == h, jnp.where(here, both[:, 0:1], NEG), placed)
            for m in (1, 2):
                placed = jnp.where(lane == m * HEADS + h, jnp.where(here, both[:, m : m + 1], 0.0), placed)
        fresh_stats.append(placed)
    mixes, tops, totals = combine(
        [old(n) for n in range(QUAD)] + [fresh(n) for n in range(QUAD)],
        old_stats + fresh_stats,
        True,
    )
    keep_stats = stat_tile(tops, totals)
    send_stats = stat_tile(tops, totals, True)
    dec_keep[8:, :] = jnp.broadcast_to(jnp.where(even, keep_stats[0:1], keep_stats[1:2]), (8, 128))
    sent = []
    for h in range(HEADS):
        dec_keep[h : h + 1, :] = jnp.where(even, mixes[h][0:1], mixes[h][1:2])
        sent.append(jnp.where(even, mixes[h][1:2], mixes[h][0:1]))
    sent.append(jnp.where(even, send_stats[1:2], send_stats[0:1]))
    sent.append(jnp.zeros((7, 128), F32))
    send[4 * TOK :, :] = jnp.concatenate(sent, 0).astype(BF16)
    for h in range(4):
        rows = slice(h * TOK, (h + 1) * TOK)
        attn_keep[rows, :] = attn[pl.ds(aligned(h * BLK + core * TOK, TOK), TOK), :]
        send[rows, :] = attn[pl.ds(aligned(h * BLK + (1 - core) * TOK, TOK), TOK), :]


def final_kernel(attn_keep, dec_keep, got, attn_out, dec_out):
    core = spot()[4]
    for h in range(4):
        rows = slice(h * TOK, (h + 1) * TOK)
        for src, head in ((attn_keep, core), (got, 1 - core)):
            attn_out[:, pl.ds(aligned((head * 4 + h) * HEAD, HEAD), HEAD)] = src[rows, :]
    theirs = got[4 * TOK :, :].astype(F32)
    other = theirs[8:9, :]
    for h in range(HEADS):
        top_a, top_b = dec_keep[8:9, h : h + 1], other[:, h : h + 1]
        total_a = dec_keep[8:9, HEADS + h : HEADS + h + 1]
        total_b = other[:, HEADS + h : HEADS + h + 1] + other[:, 2 * HEADS + h : 2 * HEADS + h + 1]
        top = jnp.maximum(top_a, top_b)
        scale_a, scale_b = jnp.exp2(top_a - top), jnp.exp2(top_b - top)
        mixed = dec_keep[h : h + 1, :] * scale_a + theirs[h : h + 1, :] * scale_b
        dec_out[h : h + 1, :] = (mixed / (total_a * scale_a + total_b * scale_b)).astype(BF16)


def exchange(x, groups):
    return lax.all_to_all(x, "seq", 0, 0, axis_index_groups=groups, tiled=True)


def to_other_core(x):
    return lax.ppermute(x, "seq", [(n, n ^ 1) for n in range(2 * SIDE * SIDE)])


def body(q_pre, k_pre, v_pre, old_k, old_v, src_page, page_row, page_len, q_dec, dec_k, dec_v):
    seq, grp = lax.axis_index("seq"), lax.axis_index("grp")
    core = seq & 1
    far = pl.BlockSpec(memory_space=pltpu.HBM)
    counts = page_row.shape[1]
    xs = call(
        pages_kernel,
        [((X_MSG, TWO), BF16)] * NG,
        (old_k.reshape(HALF, -1), old_v.reshape(HALF, -1), src_page, page_row, page_len),
        scratch=(
            pltpu.SMEM(src_page.shape, jnp.int32),
            pltpu.SMEM((1, counts), jnp.int32),
            pltpu.SMEM((1, counts), jnp.int32),
            pltpu.SemaphoreType.DMA((3 + 2 * NG,)),
        ),
        specs={n: far for n in range(5)},
    )
    xs = [xs[0]] + [
        lax.ppermute(xs[d], "grp", [(n, (n + d) % NG) for n in range(NG)]) for d in range(1, NG)
    ]
    keep, send = call(
        split_kernel,
        [((PAIR_MSG, 128), BF16)] * 2,
        (q_pre, k_pre, v_pre, *xs),
        scratch=(pltpu.SemaphoreType.DMA((12,)),),
        specs={n: far for n in range(3)},
    )
    q_mine = lax.dynamic_slice_in_dim(q_dec, grp * HEADS * HEAD, HEADS * HEAD, 2)
    q_mine = q_mine.reshape(ITEMS, HEADS * HEAD)

    def own_tokens(x):
        part = lax.dynamic_slice(x, (seq // STEPS, 0, grp * TWO), (1, STEPS, TWO))[0]
        return jnp.pad(part, ((0, 128 - STEPS), (0, 0)))

    kv_send, q_blk = call(
        local_kernel,
        [((SIDE, KV_MSG, 128), BF16), ((QROWS, 128), BF16)],
        (keep, to_other_core(send), q_mine, *xs, own_tokens(dec_k), own_tokens(dec_v)),
        scratch=(
            pltpu.VMEM((DEC_TOK, TWO), BF16),
            pltpu.VMEM((DEC_TOK, TWO), BF16),
            pltpu.VMEM((ITEMS, DEC_TOK), F32),
            pltpu.VMEM((BLK, HEAD), F32),
        ),
    )
    near, keep_dec = call(
        merge_kernel,
        [((PAIR_ALL, 128), BF16), ((72, 128), F32)],
        (exchange(kv_send, KEY_GROUPS),),
    )
    other = lax.ppermute(near, "seq", NEIGHBOURS)
    (q_send,) = call(
        queries_kernel, [((QUAD, Q_MSG, 128), BF16)], (q_blk, near, other, keep_dec)
    )
    qs = exchange(q_send, QUADS)
    work = QROWS * SIDE * KEYS
    side = (
        pltpu.VMEM((QROWS, TWO), BF16),
        pltpu.VMEM((TWO, KEYS), BF16),
        pltpu.VMEM((TWO, KEYS), BF16),
        pltpu.VMEM((QROWS, KEYS), F32),
        pltpu.VMEM((QROWS, KEYS), F32),
    )
    (o_send,) = call(
        attend_kernel,
        [((QUAD, O_MSG, 128), BF16)],
        (qs, near, other, q_mine),
        scratch=(
            pltpu.VMEM((2 * KEYS, TWO), BF16),
            pltpu.VMEM((BLK, BLK), F32),
            pltpu.VMEM((FRESH, HEAD), BF16),
            *side,
            *side,
        ),
        cost=pl.CostEstimate(flops=work * 512, bytes_accessed=4 * 1024 * 1024, transcendentals=work),
    )
    attn_keep, dec_keep, last = call(
        pair_kernel,
        [((4 * TOK, 128), BF16), ((16, 128), F32), ((LAST_MSG, 128), BF16)],
        (exchange(o_send, QUADS), qs),
        scratch=(pltpu.VMEM((QROWS, HEAD), BF16),),
    )
    attn_out, dec_out = call(
        final_kernel,
        [((TOK, HEADS * HEAD), BF16), ((HEADS, HEAD), BF16)],
        (attn_keep, dec_keep, to_other_core(last)),
    )
    return attn_out, dec_out


def solution(mesh):
    return jax.shard_map(
        body,
        mesh=mesh,
        in_specs=(
            P("seq", "grp"),
            P("seq", "grp"),
            P("seq", "grp"),
            P("seq", "grp", None, None),
            P("seq", "grp", None, None),
            P("seq", None),
            P("seq", "grp"),
            P("seq", "grp"),
            P(),
            P(),
            P(),
        ),
        out_specs=(P("seq", "grp"), P(("seq", "grp"), None)),
        check_vma=False,
    )
```

```python
import functools
import math

import jax
import jax.numpy as jnp
from jax import lax
from jax.experimental import pallas as pl
from jax.experimental.pallas import tpu as pltpu
from jax.sharding import PartitionSpec as P

HEAD = 128
PAGE = 16
OLD = 10
NEWP = 2
ROWS = 32
STEPS = 4
ITEMS = ROWS * STEPS
SIDE = 8
NG = 4
TOK = 64
BLK = 2 * TOK
KEYS = SIDE * BLK
QROWS = 4 * BLK
HEADS = 8
TWO = 2 * HEAD
EXP2_SCALE = math.log2(math.e) / math.sqrt(HEAD)
NEG = -(2.0**100)
HIDE = -(2.0**80)
LOWEST = -(2.0**60)
META = 16
PAIR_MSG = 6 * TOK + META
HALF = OLD * PAGE
X_MSG = 2 * HALF + META
OLD_TOK = NG * HALF
DEC_TOK = OLD_TOK + 128
PER = ITEMS // SIDE
DEC_MSG = HEADS * PER + PER
KV_DEC = 2 * BLK + META
KV_MSG = KV_DEC + DEC_MSG
CHUNK = 2 * KEYS
PAGES = KEYS // PAGE
LAST_MSG = 4 * TOK + 16
QUAD = 4
PAIR_DEC = 80
PAIR_SMALL = META + PAIR_DEC
Q_META = QROWS
Q_DEC = QROWS + META
Q_MSG = Q_DEC + 32
O_FRESH = QROWS + META
O_MSG = O_FRESH + 16
FRESH = 4 * 16
NT = (((1,), (1,)), ((), ()))
F32 = jnp.float32
BF16 = jnp.bfloat16


def seq_of(z, y, core):
    return (z * SIDE + y) * 2 + core


ALONG_Z = [[[seq_of(i, j, c) for i in range(SIDE)] for j in range(SIDE)] for c in range(2)]
ALONG_Y = [[[seq_of(j, i, c) for i in range(SIDE)] for j in range(SIDE)] for c in range(2)]
KEY_GROUPS = ALONG_Z[0] + ALONG_Y[1]
QUERY_GROUPS = ALONG_Y[0] + ALONG_Z[1]
QUADS = [group[p::2] for group in QUERY_GROUPS for p in range(2)]
NEIGHBOURS = [(group[n], group[n ^ 1]) for group in QUERY_GROUPS for n in range(SIDE)]


def iota(shape, dim):
    return lax.broadcasted_iota(jnp.int32, shape, dim)


def spot():
    seq, grp = lax.axis_index("seq"), lax.axis_index("grp")
    core = seq & 1
    y = (seq >> 1) & (SIDE - 1)
    z = seq >> 4
    even = core == 0
    return seq, grp, z, y, core, jnp.where(even, z, y), jnp.where(even, y, z)


def aligned(x, by):
    return pl.multiple_of(x, by)


def call(kernel, outs, args, scratch=(), limit=32, specs=None, out_specs=None, cost=None, alias=None):
    whole = pl.BlockSpec(memory_space=pltpu.VMEM)
    name = kernel.__name__.removesuffix("_kernel")
    return pl.pallas_call(
        kernel,
        out_shape=[jax.ShapeDtypeStruct(s, t) for s, t in outs],
        in_specs=[specs.get(n, whole) if specs else whole for n in range(len(args))],
        out_specs=out_specs or [whole] * len(outs),
        scratch_shapes=list(scratch),
        compiler_params=pltpu.CompilerParams(vmem_limit_bytes=limit * 1024 * 1024),
        cost_estimate=cost,
        input_output_aliases=alias or {},
        name=name,
    )(*args)


SMEM = pl.BlockSpec(memory_space=pltpu.SMEM)


def pages_kernel(old_k, old_v, src_page, page_row, page_len, *rest):
    outs, (src_s, row_s, len_s, sems) = rest[:NG], rest[NG:]
    grp = spot()[1]
    pairs = [(src_page, src_s), (page_row, row_s), (page_len, len_s)]
    for d in range(NG):
        cols = pl.ds(aligned(((grp + d) % NG) * TWO, TWO), TWO)
        pairs.append((old_k.at[:, cols], outs[d].at[pl.ds(0, HALF), :]))
        pairs.append((old_v.at[:, cols], outs[d].at[pl.ds(HALF, HALF), :]))
    copies = [pltpu.make_async_copy(a, b, sems.at[n]) for n, (a, b) in enumerate(pairs)]
    for copy in copies:
        copy.start()
    for copy in copies[:3]:
        copy.wait()
    sub, lane = iota((META, TWO), 0), iota((META, TWO), 1)
    tile = jnp.zeros((META, TWO), F32)
    for n in range(NEWP):
        src = src_s[0, grp * NEWP + n]
        values = (src >> 2, src & 3, row_s[0, OLD + n], len_s[0, OLD + n])
        for m, value in enumerate(values):
            tile = jnp.where((lane == n) & (sub == m), value.astype(F32), tile)
    for n in range(OLD):
        tile = jnp.where((sub == 8) & (lane == n), row_s[0, n].astype(F32), tile)
        tile = jnp.where((sub == 9) & (lane == n), len_s[0, n].astype(F32), tile)
    for d in range(NG):
        outs[d][2 * HALF :, :] = tile.astype(BF16)
    for copy in copies[3:]:
        copy.wait()


def split_kernel(q, k, v, x0, x1, x2, x3, keep, send, sems):
    _, _, _, _, core, w, u = spot()
    pairs = []
    for dst, head in ((keep, core), (send, 1 - core)):
        one = pl.ds(aligned(head * HEAD, HEAD), HEAD)
        pairs.append((k.at[:, one], dst.at[pl.ds(0, TOK), :]))
        pairs.append((v.at[:, one], dst.at[pl.ds(TOK, TOK), :]))
        for h in range(4):
            cols = pl.ds(aligned((head * 4 + h) * HEAD, HEAD), HEAD)
            pairs.append((q.at[:, cols], dst.at[pl.ds((2 + h) * TOK, TOK), :]))
    copies = [pltpu.make_async_copy(a, b, sems.at[n]) for n, (a, b) in enumerate(pairs)]
    for copy in copies:
        copy.start()
    fresh = (iota((META, 128), 0) < 4) & (iota((META, 128), 1) < NEWP)
    for dst, at in ((keep, w), (send, u)):
        tile = jnp.zeros((META, 128), F32)
        for d, x in enumerate((x0, x1, x2, x3)):
            part = jnp.where(fresh, x[2 * HALF :, :HEAD].astype(F32), 0.0)
            tile = tile + pltpu.roll(part, at * 16 + core * 8 + d * NEWP, 1)
        dst[6 * TOK :, :] = tile.astype(BF16)
    for copy in copies:
        copy.wait()


def local_kernel(keep, got, q, x0, x1, x2, x3, k_dec, v_dec, kv_send, q_blk, ks, vs, cs, kb):
    seq, _, _, _, core, _, _ = spot()
    for src, start in ((keep, core * TOK), (got, (1 - core) * TOK)):
        kb[pl.ds(aligned(start, TOK), TOK), :] = src[:TOK, :].astype(F32)
        kv_send[0, pl.ds(aligned(BLK + start, TOK), TOK), :] = src[TOK : 2 * TOK, :]
        for h in range(4):
            q_blk[pl.ds(aligned(h * BLK + start, TOK), TOK), :] = src[
                (2 + h) * TOK : (3 + h) * TOK, :
            ]
    kv_send[0, :BLK, :] = jnp.transpose(kb[...]).astype(BF16)
    meta = keep[6 * TOK :, :].astype(F32) + got[6 * TOK :, :].astype(F32)
    kv_send[0, 2 * BLK : KV_DEC, :] = meta.astype(BF16)
    for n in range(1, SIDE):
        kv_send[n, :KV_DEC, :] = kv_send[0, :KV_DEC, :]

    parts = (x0, x1, x2, x3)
    for n, part in enumerate(parts):
        ks[n * HALF : (n + 1) * HALF, :] = part[:HALF, :]
        vs[n * HALF : (n + 1) * HALF, :] = part[HALF : 2 * HALF, :]
    ks[OLD_TOK:, :] = k_dec[...]
    vs[OLD_TOK:, :] = v_dec[...]

    def hot(flag):
        return jnp.where(flag, 1.0, 0.0).astype(BF16)

    i = iota((ITEMS, 128), 0)
    swapped = ((i >> 1) & 7) * 16 + (i >> 4) * 2 + (i & 1)
    which = jnp.where(core == 0, i, swapped)
    lane = iota((ITEMS, 128), 1)
    row = (which >> 2).astype(F32)
    token = iota((OLD_TOK, 128), 0)
    at = (token & 15).astype(F32)
    page = (token >> 4) - iota((OLD_TOK, 128), 1)
    count = 0.0
    for n, part in enumerate(parts):
        numbers = part[2 * HALF :, :HEAD].astype(F32)
        owner, length = numbers[8:9, :], numbers[9:10, :]
        inside = (page == n * OLD) & (at < length)
        count = count + lax.dot_general(
            hot(row == owner), hot(inside), NT, preferred_element_type=F32
        )
    cs[:, :OLD_TOK] = count
    cs[:, OLD_TOK:] = jnp.where((which == seq) & (lane <= (seq & 3)), 1.0, 0.0)

    order = hot(which == lane)
    stats = jnp.zeros((ITEMS, 128), F32)
    for h in range(HEADS):
        kv = slice(h // 4 * HEAD, (h // 4 + 1) * HEAD)
        query = jnp.dot(order, q[:, h * HEAD : (h + 1) * HEAD], preferred_element_type=F32).astype(BF16)
        scores = EXP2_SCALE * lax.dot_general(query, ks[:, kv], NT, preferred_element_type=F32)
        terms = cs[...]
        scores = jnp.where(terms > 0.5, scores, NEG)
        top = jnp.max(scores, axis=1, keepdims=True).astype(BF16).astype(F32)
        weights = (jnp.exp2(scores - top) * terms).astype(BF16)
        total = jnp.sum(weights.astype(F32), axis=1, keepdims=True)
        mixed = jnp.dot(weights, vs[:, kv], preferred_element_type=F32)
        rows = slice(KV_DEC + h * PER, KV_DEC + (h + 1) * PER)
        kv_send[:, rows, :] = mixed.astype(BF16).reshape(SIDE, PER, HEAD)
        high = total.astype(BF16).astype(F32)
        stats = jnp.where(lane == h, top, stats)
        stats = jnp.where(lane == HEADS + h, high, stats)
        stats = jnp.where(lane == 2 * HEADS + h, total - high, stats)
    kv_send[:, KV_DEC + HEADS * PER :, :] = stats.astype(BF16).reshape(SIDE, PER, 128)


def attend_kernel(qs, near, other, q_dec, out, *refs):
    vs, tri, sel = refs[:3]
    sides = (refs[3:8], refs[8:13])
    seq, _, z, y, core, w, u = spot()
    even = core == 0
    chunks = ((near, u), (other, u ^ 1))
    row, col = iota((BLK, BLK), 0), iota((BLK, BLK), 1)
    tri[...] = jnp.where(col > row, HIDE, 0.0)
    same = jnp.where(row == col, 1.0, 0.0).astype(BF16)
    for side in sides:
        for h in range(4):
            side[0][h * BLK : (h + 1) * BLK, HEAD:] = same
        for c, (chunk, _) in enumerate(chunks):
            for m in range(SIDE):
                cols = slice(m * BLK, (m + 1) * BLK)
                side[1 + c][:HEAD, cols] = chunk[m * BLK : (m + 1) * BLK, :]
    for c, (chunk, _) in enumerate(chunks):
        vs[c * KEYS : (c + 1) * KEYS, :HEAD] = chunk[KEYS:, :]
    vs[:, HEAD:] = jnp.where(iota((2 * KEYS, HEAD), 1) == 0, 1.0, 0.0).astype(BF16)

    def score(j, qx, kx_a, kx_b, s_a, s_b):
        to = j * 2 + (u & 1)
        qx[:, :HEAD] = qs[j, :QROWS, :]
        for (_, n), kx, s in zip(chunks, (kx_a, kx_b), (s_a, s_b)):
            full = jnp.where(
                even,
                w + jnp.where(n < to, 1, 0),
                jnp.where(n < to, SIDE, jnp.where(n == to, w, 0)),
            )
            edge = jnp.where(n == to, w, SIDE)
            for m in range(SIDE):
                hidden = jnp.where(m == edge, tri[...], HIDE)
                hidden = jnp.where(m < full, 0.0, hidden).astype(BF16)
                kx[HEAD:, m * BLK : (m + 1) * BLK] = hidden
            s[...] = jnp.dot(qx[...], kx[...], preferred_element_type=F32)

    def mix(j, s_a, s_b):
        lane = iota((BLK, 128), 1)
        stats = jnp.zeros((BLK, 128), F32)
        for part in range(2):
            rows = slice(part * 2 * BLK, (part + 1) * 2 * BLK)
            both = (s_a[rows, :], s_b[rows, :])
            top = EXP2_SCALE * jnp.max(jnp.maximum(*both), axis=1, keepdims=True)
            top = jnp.maximum(top, LOWEST).astype(BF16).astype(F32)
            mixed = 0.0
            for c in range(2):
                weights = jnp.exp2(both[c] * EXP2_SCALE - top).astype(BF16)
                mixed = mixed + jnp.dot(
                    weights, vs[c * KEYS : (c + 1) * KEYS, :], preferred_element_type=F32
                )
            out[j, rows, :] = mixed[:, :HEAD].astype(BF16)
            total = mixed[:, HEAD : HEAD + 1]
            high = total.astype(BF16).astype(F32)
            for h in range(2):
                one = slice(h * BLK, (h + 1) * BLK)
                at = part * 2 + h
                stats = jnp.where(lane == at, top[one], stats)
                stats = jnp.where(lane == 4 + at, high[one], stats)
                stats = jnp.where(lane == 8 + at, (total - high)[one], stats)
        out[j, QROWS:O_FRESH, :] = jnp.transpose(stats)[:META].astype(BF16)

    score(0, *sides[0])
    for j in range(QUAD):
        if j + 1 < QUAD:
            score(j + 1, *sides[(j + 1) % 2])
        mix(j, *sides[j % 2][3:])

    def chip_of(there, across):
        return jnp.where(even, across * SIDE + there, there * SIDE + across)

    numbers = jnp.concatenate(
        [qs[j, Q_META : Q_META + 8, :].astype(F32) for j in range(QUAD)], axis=1
    )
    numbers = jnp.concatenate([numbers[0:4], numbers[4:8]], axis=1)
    source = numbers[0:1, :] * 4.0 + numbers[1:2, :]
    slots = source.shape[1]
    inside = iota((PAGE, slots), 0).astype(F32) < numbers[3:4, :]
    live = []
    for j in range(QUAD):
        owner = (chip_of(j * 2 + (u & 1), w) >> 1).astype(F32)
        live.append(jnp.where((numbers[2:3, :] == owner) & inside, 1.0, 0.0))
    live = jnp.concatenate(live, axis=0).astype(BF16)
    spread = iota((PAGES, KEYS), 1) >> 4 == iota((PAGES, KEYS), 0)
    spread = jnp.where(spread, 1.0, 0.0).astype(BF16)
    at = (iota((PAGE * QUAD, KEYS), 1) & 15) == (iota((PAGE * QUAD, KEYS), 0) & 15)

    pick = iota((16, ITEMS), 0)
    item = chip_of((pick >> 1) * 2 + (u & 1), w) * 2 + (pick & 1)
    pick = jnp.where((iota((16, ITEMS), 1) == item) & (pick < 8), 1.0, 0.0).astype(BF16)
    for h in range(4):
        cols = pl.ds(aligned((core * 4 + h) * HEAD, HEAD), HEAD)
        sel[h * 16 : (h + 1) * 16, :] = jnp.dot(
            pick, q_dec[:, cols], preferred_element_type=F32
        ).astype(BF16)

    all_scores, all_terms = [], []
    for c, (_, n) in enumerate(chunks):
        page = iota((PAGES, slots), 0)
        page = (chip_of(n, page >> 3) * SIDE + (page & 7)).astype(F32)
        there = jnp.where(source == page, 1.0, 0.0).astype(BF16)
        count = lax.dot_general(live, there, NT, preferred_element_type=F32)
        high = count.astype(BF16)
        low = (count - high.astype(F32)).astype(BF16)
        count = jnp.dot(high, spread, preferred_element_type=F32) + jnp.dot(
            low, spread, preferred_element_type=F32
        )
        count = jnp.where(at, count, 0.0)
        which = iota((16, KEYS), 0) >> 1
        terms = jnp.zeros((16, KEYS), F32)
        for j in range(QUAD):
            one = jnp.sum(count[j * PAGE : (j + 1) * PAGE], axis=0, keepdims=True)
            terms = jnp.where(which == j, one, terms)
        terms = jnp.concatenate([terms] * 4, axis=0)
        keys = sides[0][1 + c][:HEAD, :]
        scores = EXP2_SCALE * jnp.dot(sel[...], keys, preferred_element_type=F32)
        all_scores.append(jnp.where(terms > 0.5, scores, NEG))
        all_terms.append(terms)
    top = jnp.max(jnp.maximum(*all_scores), axis=1, keepdims=True).astype(BF16).astype(F32)
    mixed = 0.0
    for c in range(2):
        weights = (jnp.exp2(all_scores[c] - top) * all_terms[c]).astype(BF16)
        mixed = mixed + jnp.dot(
            weights, vs[c * KEYS : (c + 1) * KEYS, :], preferred_element_type=F32
        )
    total = mixed[:, HEAD : HEAD + 1]
    high = total.astype(BF16).astype(F32)
    lane = iota((FRESH, 128), 1)
    stats = jnp.where(lane == 0, top, jnp.where(lane == 1, high, 0.0))
    stats = jnp.where(lane == 2, total - high, stats)
    for j in range(QUAD):
        rows = [slice(h * 16 + 2 * j, h * 16 + 2 * j + 2) for h in range(4)]
        pieces = [mixed[r, :HEAD] for r in rows] + [stats[r] for r in rows]
        out[j, O_FRESH:, :] = jnp.concatenate(pieces, axis=0).astype(BF16)


def combine(values, stats, split):
    mixes, tops, totals = [], [], []
    for h in range(HEADS):
        top_of = [s[:, h : h + 1] for s in stats]
        top = functools.reduce(jnp.maximum, top_of)
        total, mixed = 0.0, 0.0
        for value, s, t in zip(values, stats, top_of):
            factor = jnp.exp2(t - top)
            each = s[:, HEADS + h : HEADS + h + 1]
            if split:
                each = each + s[:, 2 * HEADS + h : 2 * HEADS + h + 1]
            total = total + each * factor
            mixed = mixed + value(h) * factor
        mixes.append(mixed)
        tops.append(top)
        totals.append(total)
    return mixes, tops, totals


def stat_tile(tops, totals, split=False):
    lane = iota((tops[0].shape[0], 128), 1)
    tile = jnp.zeros(lane.shape, F32)
    for h in range(HEADS):
        tile = jnp.where(lane == h, tops[h], tile)
        if split:
            high = totals[h].astype(BF16).astype(F32)
            tile = jnp.where(lane == HEADS + h, high, tile)
            tile = jnp.where(lane == 2 * HEADS + h, totals[h] - high, tile)
        else:
            tile = jnp.where(lane == HEADS + h, totals[h], tile)
    return tile


def merge_kernel(got, chunk, send, keep):
    send[:META, :] = sum(got[n, 2 * BLK : KV_DEC, :].astype(F32) for n in range(SIDE)).astype(BF16)
    for n in range(SIDE):
        chunk[n * BLK : (n + 1) * BLK, :] = got[n, :BLK, :]
        chunk[KEYS + n * BLK : KEYS + (n + 1) * BLK, :] = got[n, BLK : 2 * BLK, :]

    def values(n):
        return lambda h: got[n, KV_DEC + h * PER : KV_DEC + (h + 1) * PER, :].astype(F32)

    mixes, tops, totals = combine(
        [values(n) for n in range(SIDE)],
        [got[n, KV_MSG - PER :, :].astype(F32) for n in range(SIDE)],
        True,
    )
    even = spot()[6] & 1 == 0

    def halves(x):
        a = jnp.concatenate([x[4 * n : 4 * n + 2] for n in range(QUAD)], axis=0)
        b = jnp.concatenate([x[4 * n + 2 : 4 * n + 4] for n in range(QUAD)], axis=0)
        return jnp.where(even, a, b), jnp.where(even, b, a)

    theirs = []
    for h in range(HEADS):
        mine, other = halves(mixes[h])
        keep[8 * h : 8 * h + 8, :] = mine
        theirs.append(other)
    mine, other = halves(stat_tile(tops, totals, True))
    keep[64:, :] = mine
    theirs += [other, jnp.zeros((8, 128), F32)]
    send[META:, :] = jnp.concatenate(theirs, axis=0).astype(BF16)


def queries_kernel(q_blk, mine, other, keep, send):
    def kept(h):
        return keep[8 * h : 8 * h + 8, :]

    def came(h):
        return other[META + 8 * h : META + 8 * h + 8, :].astype(F32)

    mixes, tops, totals = combine(
        [kept, came], [keep[64:, :], other[META + 64 : META + 72, :].astype(F32)], True
    )
    pieces = mixes + [stat_tile(tops, totals, True)]
    numbers = jnp.concatenate(
        [mine[:META, :].astype(F32)[:4], other[:META, :].astype(F32)[:4], jnp.zeros((8, 128), F32)], 0
    ).astype(BF16)
    for n in range(QUAD):
        send[n, :QROWS, :] = q_blk[...]
        send[n, Q_META:Q_DEC, :] = numbers
        rows = [piece[2 * n : 2 * n + 2] for piece in pieces] + [jnp.zeros((14, 128), F32)]
        send[n, Q_DEC:, :] = jnp.concatenate(rows, axis=0).astype(BF16)


def pair_kernel(got, qs, attn_keep, dec_keep, send, attn):
    core = spot()[4]
    even = core == 0
    stats = [got[n, QROWS:O_FRESH, :].astype(F32) for n in range(QUAD)]
    tops = [s[0:4] for s in stats]
    top = functools.reduce(jnp.maximum, tops)
    factors = [jnp.exp2(t - top) for t in tops]
    total = sum(f * (s[4:8] + s[8:12]) for f, s in zip(factors, stats))
    shares = jnp.concatenate([f / total for f in factors] + [jnp.zeros((112, 128), F32)], 0)
    shares = jnp.transpose(shares)
    for h in range(4):
        rows = slice(h * BLK, (h + 1) * BLK)
        out = 0.0
        for n in range(QUAD):
            out = out + got[n, rows, :].astype(F32) * shares[:, n * 4 + h : n * 4 + h + 1]
        attn[rows, :] = out.astype(BF16)

    def old(n):
        return lambda h: qs[n, Q_DEC:, :].astype(F32)[2 * h : 2 * h + 2]

    def fresh(n):
        return lambda h: got[n, O_FRESH:, :].astype(F32)[2 * (h % 4) : 2 * (h % 4) + 2]

    old_stats = [qs[n, Q_DEC:, :].astype(F32)[16:18] for n in range(QUAD)]
    fresh_stats = []
    lane = iota((2, 128), 1)
    for n in range(QUAD):
        tile = got[n, O_FRESH:, :].astype(F32)[8:]
        placed = jnp.zeros((2, 128), F32)
        for h in range(HEADS):
            both = tile[2 * (h % 4) : 2 * (h % 4) + 2]
            here = core == h // 4
            placed = jnp.where(lane == h, jnp.where(here, both[:, 0:1], NEG), placed)
            for m in (1, 2):
                placed = jnp.where(lane == m * HEADS + h, jnp.where(here, both[:, m : m + 1], 0.0), placed)
        fresh_stats.append(placed)
    mixes, tops, totals = combine(
        [old(n) for n in range(QUAD)] + [fresh(n) for n in range(QUAD)],
        old_stats + fresh_stats,
        True,
    )
    keep_stats = stat_tile(tops, totals)
    send_stats = stat_tile(tops, totals, True)
    dec_keep[8:, :] = jnp.broadcast_to(jnp.where(even, keep_stats[0:1], keep_stats[1:2]), (8, 128))
    sent = []
    for h in range(HEADS):
        dec_keep[h : h + 1, :] = jnp.where(even, mixes[h][0:1], mixes[h][1:2])
        sent.append(jnp.where(even, mixes[h][1:2], mixes[h][0:1]))
    sent.append(jnp.where(even, send_stats[1:2], send_stats[0:1]))
    sent.append(jnp.zeros((7, 128), F32))
    send[4 * TOK :, :] = jnp.concatenate(sent, 0).astype(BF16)
    for h in range(4):
        rows = slice(h * TOK, (h + 1) * TOK)
        attn_keep[rows, :] = attn[pl.ds(aligned(h * BLK + core * TOK, TOK), TOK), :]
        send[rows, :] = attn[pl.ds(aligned(h * BLK + (1 - core) * TOK, TOK), TOK), :]


def final_kernel(attn_keep, dec_keep, got, attn_out, dec_out):
    core = spot()[4]
    for h in range(4):
        rows = slice(h * TOK, (h + 1) * TOK)
        for src, head in ((attn_keep, core), (got, 1 - core)):
            attn_out[:, pl.ds(aligned((head * 4 + h) * HEAD, HEAD), HEAD)] = src[rows, :]
    theirs = got[4 * TOK :, :].astype(F32)
    other = theirs[8:9, :]
    for h in range(HEADS):
        top_a, top_b = dec_keep[8:9, h : h + 1], other[:, h : h + 1]
        total_a = dec_keep[8:9, HEADS + h : HEADS + h + 1]
        total_b = other[:, HEADS + h : HEADS + h + 1] + other[:, 2 * HEADS + h : 2 * HEADS + h + 1]
        top = jnp.maximum(top_a, top_b)
        scale_a, scale_b = jnp.exp2(top_a - top), jnp.exp2(top_b - top)
        mixed = dec_keep[h : h + 1, :] * scale_a + theirs[h : h + 1, :] * scale_b
        dec_out[h : h + 1, :] = (mixed / (total_a * scale_a + total_b * scale_b)).astype(BF16)


def exchange(x, groups):
    return lax.all_to_all(x, "seq", 0, 0, axis_index_groups=groups, tiled=True)


def to_other_core(x):
    return lax.ppermute(x, "seq", [(n, n ^ 1) for n in range(2 * SIDE * SIDE)])


def body(q_pre, k_pre, v_pre, old_k, old_v, src_page, page_row, page_len, q_dec, dec_k, dec_v):
    seq, grp = lax.axis_index("seq"), lax.axis_index("grp")
    core = seq & 1
    far = pl.BlockSpec(memory_space=pltpu.HBM)
    counts = page_row.shape[1]
    xs = call(
        pages_kernel,
        [((X_MSG, TWO), BF16)] * NG,
        (old_k.reshape(HALF, -1), old_v.reshape(HALF, -1), src_page, page_row, page_len),
        scratch=(
            pltpu.SMEM(src_page.shape, jnp.int32),
            pltpu.SMEM((1, counts), jnp.int32),
            pltpu.SMEM((1, counts), jnp.int32),
            pltpu.SemaphoreType.DMA((3 + 2 * NG,)),
        ),
        specs={n: far for n in range(5)},
        limit=60,
    )
    xs = [xs[0]] + [
        lax.ppermute(xs[d], "grp", [(n, (n + d) % NG) for n in range(NG)]) for d in range(1, NG)
    ]
    keep, send = call(
        split_kernel,
        [((PAIR_MSG, 128), BF16)] * 2,
        (q_pre, k_pre, v_pre, *xs),
        scratch=(pltpu.SemaphoreType.DMA((12,)),),
        specs={n: far for n in range(3)},
    )
    q_mine = lax.dynamic_slice_in_dim(q_dec, grp * HEADS * HEAD, HEADS * HEAD, 2)
    q_mine = q_mine.reshape(ITEMS, HEADS * HEAD)

    def own_tokens(x):
        part = lax.dynamic_slice(x, (seq // STEPS, 0, grp * TWO), (1, STEPS, TWO))[0]
        return jnp.pad(part, ((0, 128 - STEPS), (0, 0)))

    kv_send, q_blk = call(
        local_kernel,
        [((SIDE, KV_MSG, 128), BF16), ((QROWS, 128), BF16)],
        (keep, to_other_core(send), q_mine, *xs, own_tokens(dec_k), own_tokens(dec_v)),
        scratch=(
            pltpu.VMEM((DEC_TOK, TWO), BF16),
            pltpu.VMEM((DEC_TOK, TWO), BF16),
            pltpu.VMEM((ITEMS, DEC_TOK), F32),
            pltpu.VMEM((BLK, HEAD), F32),
        ),
    )
    near, small, keep_dec = call(
        merge_kernel,
        [((CHUNK, 128), BF16), ((PAIR_SMALL, 128), BF16), ((72, 128), F32)],
        (exchange(kv_send, KEY_GROUPS),),
    )
    small_other = lax.ppermute(small, "seq", NEIGHBOURS)
    near, small_other = lax.optimization_barrier((near, small_other))
    other = lax.ppermute(near, "seq", NEIGHBOURS)
    (q_send,) = call(
        queries_kernel, [((QUAD, Q_MSG, 128), BF16)], (q_blk, small, small_other, keep_dec)
    )
    qs = exchange(q_send, QUADS)
    work = QROWS * SIDE * KEYS
    side = (
        pltpu.VMEM((QROWS, TWO), BF16),
        pltpu.VMEM((TWO, KEYS), BF16),
        pltpu.VMEM((TWO, KEYS), BF16),
        pltpu.VMEM((QROWS, KEYS), F32),
        pltpu.VMEM((QROWS, KEYS), F32),
    )
    (o_send,) = call(
        attend_kernel,
        [((QUAD, O_MSG, 128), BF16)],
        (qs, near, other, q_mine),
        scratch=(
            pltpu.VMEM((2 * KEYS, TWO), BF16),
            pltpu.VMEM((BLK, BLK), F32),
            pltpu.VMEM((FRESH, HEAD), BF16),
            *side,
            *side,
        ),
        cost=pl.CostEstimate(flops=work * 512, bytes_accessed=4 * 1024 * 1024, transcendentals=work),
    )
    attn_keep, dec_keep, last = call(
        pair_kernel,
        [((4 * TOK, 128), BF16), ((16, 128), F32), ((LAST_MSG, 128), BF16)],
        (exchange(o_send, QUADS), qs),
        scratch=(pltpu.VMEM((QROWS, HEAD), BF16),),
    )
    attn_out, dec_out = call(
        final_kernel,
        [((TOK, HEADS * HEAD), BF16), ((HEADS, HEAD), BF16)],
        (attn_keep, dec_keep, to_other_core(last)),
    )
    return attn_out, dec_out


def solution(mesh):
    return jax.shard_map(
        body,
        mesh=mesh,
        in_specs=(
            P("seq", "grp"),
            P("seq", "grp"),
            P("seq", "grp"),
            P("seq", "grp", None, None),
            P("seq", "grp", None, None),
            P("seq", None),
            P("seq", "grp"),
            P("seq", "grp"),
            P(),
            P(),
            P(),
        ),
        out_specs=(P("seq", "grp"), P(("seq", "grp"), None)),
        check_vma=False,
    )
```

```python
import functools
import math

import jax
import jax.numpy as jnp
from jax import lax
from jax.experimental import pallas as pl
from jax.experimental.pallas import tpu as pltpu
from jax.sharding import PartitionSpec as P

HEAD = 128
PAGE = 16
OLD = 10
NEWP = 2
ROWS = 32
STEPS = 4
ITEMS = ROWS * STEPS
SIDE = 8
NG = 4
TOK = 64
BLK = 2 * TOK
KEYS = SIDE * BLK
QROWS = 4 * BLK
HEADS = 8
TWO = 2 * HEAD
EXP2_SCALE = math.log2(math.e) / math.sqrt(HEAD)
NEG = -(2.0**100)
HIDE = -(2.0**80)
LOWEST = -(2.0**60)
META = 16
PAIR_MSG = 6 * TOK + META
HALF = OLD * PAGE
X_MSG = 2 * HALF + META
OLD_TOK = NG * HALF
DEC_TOK = OLD_TOK + 128
PER = ITEMS // SIDE
DEC_MSG = HEADS * PER + PER
KV_DEC = 2 * BLK + META
KV_MSG = KV_DEC + DEC_MSG
PAGES = KEYS // PAGE
LAST_MSG = 4 * TOK + 16
QUAD = 4
PAIR_DEC = 80
PAIR_SMALL = META + PAIR_DEC
Q_META = QROWS
Q_DEC = QROWS + META
Q_MSG = Q_DEC + 32
O_FRESH = QROWS + META
O_MSG = O_FRESH + 16
FRESH = 4 * 16
NT = (((1,), (1,)), ((), ()))
F32 = jnp.float32
BF16 = jnp.bfloat16


def seq_of(z, y, core):
    return (z * SIDE + y) * 2 + core


ALONG_Z = [[[seq_of(i, j, c) for i in range(SIDE)] for j in range(SIDE)] for c in range(2)]
ALONG_Y = [[[seq_of(j, i, c) for i in range(SIDE)] for j in range(SIDE)] for c in range(2)]
KEY_GROUPS = ALONG_Z[0] + ALONG_Y[1]
QUERY_GROUPS = ALONG_Y[0] + ALONG_Z[1]
QUADS = [group[p::2] for group in QUERY_GROUPS for p in range(2)]
NEIGHBOURS = [(group[n], group[n ^ 1]) for group in QUERY_GROUPS for n in range(SIDE)]


def iota(shape, dim):
    return lax.broadcasted_iota(jnp.int32, shape, dim)


def spot():
    seq, grp = lax.axis_index("seq"), lax.axis_index("grp")
    core = seq & 1
    y = (seq >> 1) & (SIDE - 1)
    z = seq >> 4
    even = core == 0
    return seq, grp, z, y, core, jnp.where(even, z, y), jnp.where(even, y, z)


def aligned(x, by):
    return pl.multiple_of(x, by)


def call(kernel, outs, args, scratch=(), limit=32, specs=None, out_specs=None, cost=None, alias=None):
    whole = pl.BlockSpec(memory_space=pltpu.VMEM)
    name = kernel.__name__.removesuffix("_kernel")
    return pl.pallas_call(
        kernel,
        out_shape=[jax.ShapeDtypeStruct(s, t) for s, t in outs],
        in_specs=[specs.get(n, whole) if specs else whole for n in range(len(args))],
        out_specs=out_specs or [whole] * len(outs),
        scratch_shapes=list(scratch),
        compiler_params=pltpu.CompilerParams(vmem_limit_bytes=limit * 1024 * 1024),
        cost_estimate=cost,
        input_output_aliases=alias or {},
        name=name,
    )(*args)


SMEM = pl.BlockSpec(memory_space=pltpu.SMEM)


def pages_kernel(old_k, old_v, src_page, page_row, page_len, out, src_s, row_s, len_s, sems):
    grp = spot()[1]
    pairs = [(src_page, src_s), (page_row, row_s), (page_len, len_s)]
    for d in range(NG):
        cols = pl.ds(d * TWO, TWO)
        pairs.append((old_k.at[:, cols], out.at[d, pl.ds(0, HALF), :]))
        pairs.append((old_v.at[:, cols], out.at[d, pl.ds(HALF, HALF), :]))
    copies = [pltpu.make_async_copy(a, b, sems.at[n]) for n, (a, b) in enumerate(pairs)]
    for copy in copies:
        copy.start()
    for copy in copies[:3]:
        copy.wait()
    sub, lane = iota((META, TWO), 0), iota((META, TWO), 1)
    tile = jnp.zeros((META, TWO), F32)
    for n in range(NEWP):
        src = src_s[0, grp * NEWP + n]
        values = (src >> 2, src & 3, row_s[0, OLD + n], len_s[0, OLD + n])
        for m, value in enumerate(values):
            tile = jnp.where((lane == n) & (sub == m), value.astype(F32), tile)
    for n in range(OLD):
        tile = jnp.where((sub == 8) & (lane == n), row_s[0, n].astype(F32), tile)
        tile = jnp.where((sub == 9) & (lane == n), len_s[0, n].astype(F32), tile)
    for d in range(NG):
        out[d, 2 * HALF :, :] = tile.astype(BF16)
    for copy in copies[3:]:
        copy.wait()


def split_kernel(q, k, v, xs, keep, send, sems):
    _, _, _, _, core, w, u = spot()
    pairs = []
    for dst, head in ((keep, core), (send, 1 - core)):
        one = pl.ds(aligned(head * HEAD, HEAD), HEAD)
        pairs.append((k.at[:, one], dst.at[pl.ds(0, TOK), :]))
        pairs.append((v.at[:, one], dst.at[pl.ds(TOK, TOK), :]))
        for h in range(4):
            cols = pl.ds(aligned((head * 4 + h) * HEAD, HEAD), HEAD)
            pairs.append((q.at[:, cols], dst.at[pl.ds((2 + h) * TOK, TOK), :]))
    copies = [pltpu.make_async_copy(a, b, sems.at[n]) for n, (a, b) in enumerate(pairs)]
    for copy in copies:
        copy.start()
    fresh = (iota((META, 128), 0) < 4) & (iota((META, 128), 1) < NEWP)
    for dst, at in ((keep, w), (send, u)):
        tile = jnp.zeros((META, 128), F32)
        for d in range(NG):
            part = jnp.where(fresh, xs[d, 2 * HALF :, :HEAD].astype(F32), 0.0)
            tile = tile + pltpu.roll(part, at * 16 + core * 8 + d * NEWP, 1)
        dst[6 * TOK :, :] = tile.astype(BF16)
    for copy in copies:
        copy.wait()


def local_kernel(keep, got, q, xs, k_dec, v_dec, kv_send, q_blk, ks, vs, cs, kb):
    seq, _, _, _, core, _, _ = spot()
    for src, start in ((keep, core * TOK), (got, (1 - core) * TOK)):
        kb[pl.ds(aligned(start, TOK), TOK), :] = src[:TOK, :].astype(F32)
        kv_send[0, pl.ds(aligned(BLK + start, TOK), TOK), :] = src[TOK : 2 * TOK, :]
        for h in range(4):
            q_blk[pl.ds(aligned(h * BLK + start, TOK), TOK), :] = src[
                (2 + h) * TOK : (3 + h) * TOK, :
            ]
    kv_send[0, :BLK, :] = jnp.transpose(kb[...]).astype(BF16)
    meta = keep[6 * TOK :, :].astype(F32) + got[6 * TOK :, :].astype(F32)
    kv_send[0, 2 * BLK : KV_DEC, :] = meta.astype(BF16)
    for n in range(1, SIDE):
        kv_send[n, :KV_DEC, :] = kv_send[0, :KV_DEC, :]

    for n in range(NG):
        ks[n * HALF : (n + 1) * HALF, :] = xs[n, :HALF, :]
        vs[n * HALF : (n + 1) * HALF, :] = xs[n, HALF : 2 * HALF, :]
    ks[OLD_TOK:, :] = k_dec[...]
    vs[OLD_TOK:, :] = v_dec[...]

    def hot(flag):
        return jnp.where(flag, 1.0, 0.0).astype(BF16)

    i = iota((ITEMS, 128), 0)
    swapped = ((i >> 1) & 7) * 16 + (i >> 4) * 2 + (i & 1)
    which = jnp.where(core == 0, i, swapped)
    lane = iota((ITEMS, 128), 1)
    row = (which >> 2).astype(F32)
    token = iota((OLD_TOK, 128), 0)
    at = (token & 15).astype(F32)
    page = (token >> 4) - iota((OLD_TOK, 128), 1)
    count = 0.0
    for n in range(NG):
        numbers = xs[n, 2 * HALF :, :HEAD].astype(F32)
        owner, length = numbers[8:9, :], numbers[9:10, :]
        inside = (page == n * OLD) & (at < length)
        count = count + lax.dot_general(
            hot(row == owner), hot(inside), NT, preferred_element_type=F32
        )
    cs[:, :OLD_TOK] = count
    cs[:, OLD_TOK:] = jnp.where((which == seq) & (lane <= (seq & 3)), 1.0, 0.0)

    order = hot(which == lane)
    stats = jnp.zeros((ITEMS, 128), F32)
    for h in range(HEADS):
        kv = slice(h // 4 * HEAD, (h // 4 + 1) * HEAD)
        query = jnp.dot(order, q[:, h * HEAD : (h + 1) * HEAD], preferred_element_type=F32).astype(BF16)
        scores = EXP2_SCALE * lax.dot_general(query, ks[:, kv], NT, preferred_element_type=F32)
        terms = cs[...]
        scores = jnp.where(terms > 0.5, scores, NEG)
        top = jnp.max(scores, axis=1, keepdims=True).astype(BF16).astype(F32)
        weights = (jnp.exp2(scores - top) * terms).astype(BF16)
        total = jnp.sum(weights.astype(F32), axis=1, keepdims=True)
        mixed = jnp.dot(weights, vs[:, kv], preferred_element_type=F32)
        rows = slice(KV_DEC + h * PER, KV_DEC + (h + 1) * PER)
        kv_send[:, rows, :] = mixed.astype(BF16).reshape(SIDE, PER, HEAD)
        high = total.astype(BF16).astype(F32)
        stats = jnp.where(lane == h, top, stats)
        stats = jnp.where(lane == HEADS + h, high, stats)
        stats = jnp.where(lane == 2 * HEADS + h, total - high, stats)
    kv_send[:, KV_DEC + HEADS * PER :, :] = stats.astype(BF16).reshape(SIDE, PER, 128)


def attend_kernel(qs, keys, keys_other, vals, vals_other, q_dec, out, *refs):
    vs, tri, sel = refs[:3]
    sides = (refs[3:8], refs[8:13])
    seq, _, z, y, core, w, u = spot()
    even = core == 0
    chunks = ((keys, u), (keys_other, u ^ 1))
    row, col = iota((BLK, BLK), 0), iota((BLK, BLK), 1)
    tri[...] = jnp.where(col > row, HIDE, 0.0)
    same = jnp.where(row == col, 1.0, 0.0).astype(BF16)
    for side in sides:
        for h in range(4):
            side[0][h * BLK : (h + 1) * BLK, HEAD:] = same
        for c, (chunk, _) in enumerate(chunks):
            for m in range(SIDE):
                cols = slice(m * BLK, (m + 1) * BLK)
                side[1 + c][:HEAD, cols] = chunk[m * BLK : (m + 1) * BLK, :]
    vs[:KEYS, :HEAD] = vals[...]
    vs[KEYS:, :HEAD] = vals_other[...]
    vs[:, HEAD:] = jnp.where(iota((2 * KEYS, HEAD), 1) == 0, 1.0, 0.0).astype(BF16)

    def score(j, qx, kx_a, kx_b, s_a, s_b):
        to = j * 2 + (u & 1)
        qx[:, :HEAD] = qs[j, :QROWS, :]
        for (_, n), kx, s in zip(chunks, (kx_a, kx_b), (s_a, s_b)):
            full = jnp.where(
                even,
                w + jnp.where(n < to, 1, 0),
                jnp.where(n < to, SIDE, jnp.where(n == to, w, 0)),
            )
            edge = jnp.where(n == to, w, SIDE)
            for m in range(SIDE):
                hidden = jnp.where(m == edge, tri[...], HIDE)
                hidden = jnp.where(m < full, 0.0, hidden).astype(BF16)
                kx[HEAD:, m * BLK : (m + 1) * BLK] = hidden
            s[...] = jnp.dot(qx[...], kx[...], preferred_element_type=F32)

    def mix(j, s_a, s_b):
        lane = iota((BLK, 128), 1)
        stats = jnp.zeros((BLK, 128), F32)
        for part in range(2):
            rows = slice(part * 2 * BLK, (part + 1) * 2 * BLK)
            both = (s_a[rows, :], s_b[rows, :])
            top = EXP2_SCALE * jnp.max(jnp.maximum(*both), axis=1, keepdims=True)
            top = jnp.maximum(top, LOWEST).astype(BF16).astype(F32)
            mixed = 0.0
            for c in range(2):
                weights = jnp.exp2(both[c] * EXP2_SCALE - top).astype(BF16)
                mixed = mixed + jnp.dot(
                    weights, vs[c * KEYS : (c + 1) * KEYS, :], preferred_element_type=F32
                )
            out[j, rows, :] = mixed[:, :HEAD].astype(BF16)
            total = mixed[:, HEAD : HEAD + 1]
            high = total.astype(BF16).astype(F32)
            for h in range(2):
                one = slice(h * BLK, (h + 1) * BLK)
                at = part * 2 + h
                stats = jnp.where(lane == at, top[one], stats)
                stats = jnp.where(lane == 4 + at, high[one], stats)
                stats = jnp.where(lane == 8 + at, (total - high)[one], stats)
        out[j, QROWS:O_FRESH, :] = jnp.transpose(stats)[:META].astype(BF16)

    score(0, *sides[0])
    for j in range(QUAD):
        if j + 1 < QUAD:
            score(j + 1, *sides[(j + 1) % 2])
        mix(j, *sides[j % 2][3:])

    def chip_of(there, across):
        return jnp.where(even, across * SIDE + there, there * SIDE + across)

    numbers = jnp.concatenate(
        [qs[j, Q_META : Q_META + 8, :].astype(F32) for j in range(QUAD)], axis=1
    )
    numbers = jnp.concatenate([numbers[0:4], numbers[4:8]], axis=1)
    source = numbers[0:1, :] * 4.0 + numbers[1:2, :]
    slots = source.shape[1]
    inside = iota((PAGE, slots), 0).astype(F32) < numbers[3:4, :]
    live = []
    for j in range(QUAD):
        owner = (chip_of(j * 2 + (u & 1), w) >> 1).astype(F32)
        live.append(jnp.where((numbers[2:3, :] == owner) & inside, 1.0, 0.0))
    live = jnp.concatenate(live, axis=0).astype(BF16)
    spread = iota((PAGES, KEYS), 1) >> 4 == iota((PAGES, KEYS), 0)
    spread = jnp.where(spread, 1.0, 0.0).astype(BF16)
    at = (iota((PAGE * QUAD, KEYS), 1) & 15) == (iota((PAGE * QUAD, KEYS), 0) & 15)

    pick = iota((16, ITEMS), 0)
    item = chip_of((pick >> 1) * 2 + (u & 1), w) * 2 + (pick & 1)
    pick = jnp.where((iota((16, ITEMS), 1) == item) & (pick < 8), 1.0, 0.0).astype(BF16)
    for h in range(4):
        cols = pl.ds(aligned((core * 4 + h) * HEAD, HEAD), HEAD)
        sel[h * 16 : (h + 1) * 16, :] = jnp.dot(
            pick, q_dec[:, cols], preferred_element_type=F32
        ).astype(BF16)

    all_scores, all_terms = [], []
    for c, (_, n) in enumerate(chunks):
        page = iota((PAGES, slots), 0)
        page = (chip_of(n, page >> 3) * SIDE + (page & 7)).astype(F32)
        there = jnp.where(source == page, 1.0, 0.0).astype(BF16)
        count = lax.dot_general(live, there, NT, preferred_element_type=F32)
        high = count.astype(BF16)
        low = (count - high.astype(F32)).astype(BF16)
        count = jnp.dot(high, spread, preferred_element_type=F32) + jnp.dot(
            low, spread, preferred_element_type=F32
        )
        count = jnp.where(at, count, 0.0)
        which = iota((16, KEYS), 0) >> 1
        terms = jnp.zeros((16, KEYS), F32)
        for j in range(QUAD):
            one = jnp.sum(count[j * PAGE : (j + 1) * PAGE], axis=0, keepdims=True)
            terms = jnp.where(which == j, one, terms)
        terms = jnp.concatenate([terms] * 4, axis=0)
        held = sides[0][1 + c][:HEAD, :]
        scores = EXP2_SCALE * jnp.dot(sel[...], held, preferred_element_type=F32)
        all_scores.append(jnp.where(terms > 0.5, scores, NEG))
        all_terms.append(terms)
    top = jnp.max(jnp.maximum(*all_scores), axis=1, keepdims=True).astype(BF16).astype(F32)
    mixed = 0.0
    for c in range(2):
        weights = (jnp.exp2(all_scores[c] - top) * all_terms[c]).astype(BF16)
        mixed = mixed + jnp.dot(
            weights, vs[c * KEYS : (c + 1) * KEYS, :], preferred_element_type=F32
        )
    total = mixed[:, HEAD : HEAD + 1]
    high = total.astype(BF16).astype(F32)
    lane = iota((FRESH, 128), 1)
    stats = jnp.where(lane == 0, top, jnp.where(lane == 1, high, 0.0))
    stats = jnp.where(lane == 2, total - high, stats)
    for j in range(QUAD):
        rows = [slice(h * 16 + 2 * j, h * 16 + 2 * j + 2) for h in range(4)]
        pieces = [mixed[r, :HEAD] for r in rows] + [stats[r] for r in rows]
        out[j, O_FRESH:, :] = jnp.concatenate(pieces, axis=0).astype(BF16)


def combine(values, stats, split):
    mixes, tops, totals = [], [], []
    for h in range(HEADS):
        top_of = [s[:, h : h + 1] for s in stats]
        top = functools.reduce(jnp.maximum, top_of)
        total, mixed = 0.0, 0.0
        for value, s, t in zip(values, stats, top_of):
            factor = jnp.exp2(t - top)
            each = s[:, HEADS + h : HEADS + h + 1]
            if split:
                each = each + s[:, 2 * HEADS + h : 2 * HEADS + h + 1]
            total = total + each * factor
            mixed = mixed + value(h) * factor
        mixes.append(mixed)
        tops.append(top)
        totals.append(total)
    return mixes, tops, totals


def stat_tile(tops, totals, split=False):
    lane = iota((tops[0].shape[0], 128), 1)
    tile = jnp.zeros(lane.shape, F32)
    for h in range(HEADS):
        tile = jnp.where(lane == h, tops[h], tile)
        if split:
            high = totals[h].astype(BF16).astype(F32)
            tile = jnp.where(lane == HEADS + h, high, tile)
            tile = jnp.where(lane == 2 * HEADS + h, totals[h] - high, tile)
        else:
            tile = jnp.where(lane == HEADS + h, totals[h], tile)
    return tile


def merge_kernel(got, keys, vals, send, keep):
    send[:META, :] = sum(got[n, 2 * BLK : KV_DEC, :].astype(F32) for n in range(SIDE)).astype(BF16)
    for n in range(SIDE):
        keys[n * BLK : (n + 1) * BLK, :] = got[n, :BLK, :]
        vals[n * BLK : (n + 1) * BLK, :] = got[n, BLK : 2 * BLK, :]

    def values(n):
        return lambda h: got[n, KV_DEC + h * PER : KV_DEC + (h + 1) * PER, :].astype(F32)

    mixes, tops, totals = combine(
        [values(n) for n in range(SIDE)],
        [got[n, KV_MSG - PER :, :].astype(F32) for n in range(SIDE)],
        True,
    )
    even = spot()[6] & 1 == 0

    def halves(x):
        a = jnp.concatenate([x[4 * n : 4 * n + 2] for n in range(QUAD)], axis=0)
        b = jnp.concatenate([x[4 * n + 2 : 4 * n + 4] for n in range(QUAD)], axis=0)
        return jnp.where(even, a, b), jnp.where(even, b, a)

    theirs = []
    for h in range(HEADS):
        mine, other = halves(mixes[h])
        keep[8 * h : 8 * h + 8, :] = mine
        theirs.append(other)
    mine, other = halves(stat_tile(tops, totals, True))
    keep[64:, :] = mine
    theirs += [other, jnp.zeros((8, 128), F32)]
    send[META:, :] = jnp.concatenate(theirs, axis=0).astype(BF16)


def queries_kernel(q_blk, mine, other, keep, send):
    def kept(h):
        return keep[8 * h : 8 * h + 8, :]

    def came(h):
        return other[META + 8 * h : META + 8 * h + 8, :].astype(F32)

    mixes, tops, totals = combine(
        [kept, came], [keep[64:, :], other[META + 64 : META + 72, :].astype(F32)], True
    )
    pieces = mixes + [stat_tile(tops, totals, True)]
    numbers = jnp.concatenate(
        [mine[:META, :].astype(F32)[:4], other[:META, :].astype(F32)[:4], jnp.zeros((8, 128), F32)], 0
    ).astype(BF16)
    for n in range(QUAD):
        send[n, :QROWS, :] = q_blk[...]
        send[n, Q_META:Q_DEC, :] = numbers
        rows = [piece[2 * n : 2 * n + 2] for piece in pieces] + [jnp.zeros((14, 128), F32)]
        send[n, Q_DEC:, :] = jnp.concatenate(rows, axis=0).astype(BF16)


def pair_kernel(got, qs, attn_keep, dec_keep, send, attn):
    core = spot()[4]
    even = core == 0
    stats = [got[n, QROWS:O_FRESH, :].astype(F32) for n in range(QUAD)]
    tops = [s[0:4] for s in stats]
    top = functools.reduce(jnp.maximum, tops)
    factors = [jnp.exp2(t - top) for t in tops]
    total = sum(f * (s[4:8] + s[8:12]) for f, s in zip(factors, stats))
    shares = jnp.concatenate([f / total for f in factors] + [jnp.zeros((112, 128), F32)], 0)
    shares = jnp.transpose(shares)
    for h in range(4):
        rows = slice(h * BLK, (h + 1) * BLK)
        out = 0.0
        for n in range(QUAD):
            out = out + got[n, rows, :].astype(F32) * shares[:, n * 4 + h : n * 4 + h + 1]
        attn[rows, :] = out.astype(BF16)

    def old(n):
        return lambda h: qs[n, Q_DEC:, :].astype(F32)[2 * h : 2 * h + 2]

    def fresh(n):
        return lambda h: got[n, O_FRESH:, :].astype(F32)[2 * (h % 4) : 2 * (h % 4) + 2]

    old_stats = [qs[n, Q_DEC:, :].astype(F32)[16:18] for n in range(QUAD)]
    fresh_stats = []
    lane = iota((2, 128), 1)
    for n in range(QUAD):
        tile = got[n, O_FRESH:, :].astype(F32)[8:]
        placed = jnp.zeros((2, 128), F32)
        for h in range(HEADS):
            both = tile[2 * (h % 4) : 2 * (h % 4) + 2]
            here = core == h // 4
            placed = jnp.where(lane == h, jnp.where(here, both[:, 0:1], NEG), placed)
            for m in (1, 2):
                placed = jnp.where(lane == m * HEADS + h, jnp.where(here, both[:, m : m + 1], 0.0), placed)
        fresh_stats.append(placed)
    mixes, tops, totals = combine(
        [old(n) for n in range(QUAD)] + [fresh(n) for n in range(QUAD)],
        old_stats + fresh_stats,
        True,
    )
    keep_stats = stat_tile(tops, totals)
    send_stats = stat_tile(tops, totals, True)
    dec_keep[8:, :] = jnp.broadcast_to(jnp.where(even, keep_stats[0:1], keep_stats[1:2]), (8, 128))
    sent = []
    for h in range(HEADS):
        dec_keep[h : h + 1, :] = jnp.where(even, mixes[h][0:1], mixes[h][1:2])
        sent.append(jnp.where(even, mixes[h][1:2], mixes[h][0:1]))
    sent.append(jnp.where(even, send_stats[1:2], send_stats[0:1]))
    sent.append(jnp.zeros((7, 128), F32))
    send[4 * TOK :, :] = jnp.concatenate(sent, 0).astype(BF16)
    for h in range(4):
        rows = slice(h * TOK, (h + 1) * TOK)
        attn_keep[rows, :] = attn[pl.ds(aligned(h * BLK + core * TOK, TOK), TOK), :]
        send[rows, :] = attn[pl.ds(aligned(h * BLK + (1 - core) * TOK, TOK), TOK), :]


def final_kernel(attn_keep, dec_keep, got, attn_out, dec_out):
    core = spot()[4]
    for h in range(4):
        rows = slice(h * TOK, (h + 1) * TOK)
        for src, head in ((attn_keep, core), (got, 1 - core)):
            attn_out[:, pl.ds(aligned((head * 4 + h) * HEAD, HEAD), HEAD)] = src[rows, :]
    theirs = got[4 * TOK :, :].astype(F32)
    other = theirs[8:9, :]
    for h in range(HEADS):
        top_a, top_b = dec_keep[8:9, h : h + 1], other[:, h : h + 1]
        total_a = dec_keep[8:9, HEADS + h : HEADS + h + 1]
        total_b = other[:, HEADS + h : HEADS + h + 1] + other[:, 2 * HEADS + h : 2 * HEADS + h + 1]
        top = jnp.maximum(top_a, top_b)
        scale_a, scale_b = jnp.exp2(top_a - top), jnp.exp2(top_b - top)
        mixed = dec_keep[h : h + 1, :] * scale_a + theirs[h : h + 1, :] * scale_b
        dec_out[h : h + 1, :] = (mixed / (total_a * scale_a + total_b * scale_b)).astype(BF16)


def exchange(x, groups):
    return lax.all_to_all(x, "seq", 0, 0, axis_index_groups=groups, tiled=True)


def to_other_core(x):
    return lax.ppermute(x, "seq", [(n, n ^ 1) for n in range(2 * SIDE * SIDE)])


def body(q_pre, k_pre, v_pre, old_k, old_v, src_page, page_row, page_len, q_dec, dec_k, dec_v):
    seq, grp = lax.axis_index("seq"), lax.axis_index("grp")
    core = seq & 1
    far = pl.BlockSpec(memory_space=pltpu.HBM)
    counts = page_row.shape[1]
    (x_send,) = call(
        pages_kernel,
        [((NG, X_MSG, TWO), BF16)],
        (old_k.reshape(HALF, -1), old_v.reshape(HALF, -1), src_page, page_row, page_len),
        scratch=(
            pltpu.SMEM(src_page.shape, jnp.int32),
            pltpu.SMEM((1, counts), jnp.int32),
            pltpu.SMEM((1, counts), jnp.int32),
            pltpu.SemaphoreType.DMA((3 + 2 * NG,)),
        ),
        specs={n: far for n in range(5)},
        limit=60,
    )
    xs = lax.all_to_all(x_send, "grp", 0, 0, tiled=True)
    keep, send = call(
        split_kernel,
        [((PAIR_MSG, 128), BF16)] * 2,
        (q_pre, k_pre, v_pre, xs),
        scratch=(pltpu.SemaphoreType.DMA((12,)),),
        specs={n: far for n in range(3)},
    )
    q_mine = lax.dynamic_slice_in_dim(q_dec, grp * HEADS * HEAD, HEADS * HEAD, 2)
    q_mine = q_mine.reshape(ITEMS, HEADS * HEAD)

    def own_tokens(x):
        part = lax.dynamic_slice(x, (seq // STEPS, 0, grp * TWO), (1, STEPS, TWO))[0]
        return jnp.pad(part, ((0, 128 - STEPS), (0, 0)))

    kv_send, q_blk = call(
        local_kernel,
        [((SIDE, KV_MSG, 128), BF16), ((QROWS, 128), BF16)],
        (keep, to_other_core(send), q_mine, xs, own_tokens(dec_k), own_tokens(dec_v)),
        scratch=(
            pltpu.VMEM((DEC_TOK, TWO), BF16),
            pltpu.VMEM((DEC_TOK, TWO), BF16),
            pltpu.VMEM((ITEMS, DEC_TOK), F32),
            pltpu.VMEM((BLK, HEAD), F32),
        ),
    )
    keys, vals, small, keep_dec = call(
        merge_kernel,
        [((KEYS, 128), BF16), ((KEYS, 128), BF16), ((PAIR_SMALL, 128), BF16), ((72, 128), F32)],
        (exchange(kv_send, KEY_GROUPS),),
    )
    small_other = lax.ppermute(small, "seq", NEIGHBOURS)
    keys, vals, small_other = lax.optimization_barrier((keys, vals, small_other))
    keys_other = lax.ppermute(keys, "seq", NEIGHBOURS)
    vals_other = lax.ppermute(vals, "seq", NEIGHBOURS)
    (q_send,) = call(
        queries_kernel,
        [((QUAD, Q_MSG, 128), BF16)],
        (q_blk, small, small_other, keep_dec),
    )
    qs = exchange(q_send, QUADS)
    work = QROWS * SIDE * KEYS
    side = (
        pltpu.VMEM((QROWS, TWO), BF16),
        pltpu.VMEM((TWO, KEYS), BF16),
        pltpu.VMEM((TWO, KEYS), BF16),
        pltpu.VMEM((QROWS, KEYS), F32),
        pltpu.VMEM((QROWS, KEYS), F32),
    )
    (o_send,) = call(
        attend_kernel,
        [((QUAD, O_MSG, 128), BF16)],
        (qs, keys, keys_other, vals, vals_other, q_mine),
        scratch=(
            pltpu.VMEM((2 * KEYS, TWO), BF16),
            pltpu.VMEM((BLK, BLK), F32),
            pltpu.VMEM((FRESH, HEAD), BF16),
            *side,
            *side,
        ),
        cost=pl.CostEstimate(flops=work * 512, bytes_accessed=4 * 1024 * 1024, transcendentals=work),
    )
    attn_keep, dec_keep, last = call(
        pair_kernel,
        [((4 * TOK, 128), BF16), ((16, 128), F32), ((LAST_MSG, 128), BF16)],
        (exchange(o_send, QUADS), qs),
        scratch=(pltpu.VMEM((QROWS, HEAD), BF16),),
    )
    attn_out, dec_out = call(
        final_kernel,
        [((TOK, HEADS * HEAD), BF16), ((HEADS, HEAD), BF16)],
        (attn_keep, dec_keep, to_other_core(last)),
    )
    return attn_out, dec_out


def solution(mesh):
    return jax.shard_map(
        body,
        mesh=mesh,
        in_specs=(
            P("seq", "grp"),
            P("seq", "grp"),
            P("seq", "grp"),
            P("seq", "grp", None, None),
            P("seq", "grp", None, None),
            P("seq", None),
            P("seq", "grp"),
            P("seq", "grp"),
            P(),
            P(),
            P(),
        ),
        out_specs=(P("seq", "grp"), P(("seq", "grp"), None)),
        check_vma=False,
    )
```

```python
import functools
import math

import jax
import jax.numpy as jnp
from jax import lax
from jax.experimental import pallas as pl
from jax.experimental.pallas import tpu as pltpu
from jax.sharding import PartitionSpec as P

HEAD = 128
PAGE = 16
OLD = 10
NEWP = 2
ROWS = 32
STEPS = 4
ITEMS = ROWS * STEPS
SIDE = 8
NG = 4
TOK = 64
BLK = 2 * TOK
KEYS = SIDE * BLK
QROWS = 4 * BLK
HEADS = 8
TWO = 2 * HEAD
EXP2_SCALE = math.log2(math.e) / math.sqrt(HEAD)
NEG = -(2.0**100)
HIDE = -(2.0**80)
LOWEST = -(2.0**60)
META = 16
PAIR_MSG = 6 * TOK + META
HALF = OLD * PAGE
X_MSG = 2 * HALF + META
OLD_TOK = NG * HALF
DEC_TOK = OLD_TOK + 128
PER = ITEMS // SIDE
DEC_MSG = HEADS * PER + PER
KV_DEC = 2 * BLK + META
KV_MSG = KV_DEC + DEC_MSG
PAGES = KEYS // PAGE
LAST_MSG = 4 * TOK + 16
QUAD = 4
PAIR_DEC = 80
PAIR_SMALL = META + PAIR_DEC
Q_META = QROWS
Q_DEC = QROWS + META
Q_MSG = Q_DEC + 32
O_FRESH = QROWS + META
O_MSG = O_FRESH + 16
FRESH = 4 * 16
NT = (((1,), (1,)), ((), ()))
F32 = jnp.float32
BF16 = jnp.bfloat16


def seq_of(z, y, core):
    return (z * SIDE + y) * 2 + core


ALONG_Z = [[[seq_of(i, j, c) for i in range(SIDE)] for j in range(SIDE)] for c in range(2)]
ALONG_Y = [[[seq_of(j, i, c) for i in range(SIDE)] for j in range(SIDE)] for c in range(2)]
KEY_GROUPS = ALONG_Z[0] + ALONG_Y[1]
QUERY_GROUPS = ALONG_Y[0] + ALONG_Z[1]
QUADS = [group[p::2] for group in QUERY_GROUPS for p in range(2)]
NEIGHBOURS = [(group[n], group[n ^ 1]) for group in QUERY_GROUPS for n in range(SIDE)]


def iota(shape, dim):
    return lax.broadcasted_iota(jnp.int32, shape, dim)


def spot():
    seq, grp = lax.axis_index("seq"), lax.axis_index("grp")
    core = seq & 1
    y = (seq >> 1) & (SIDE - 1)
    z = seq >> 4
    even = core == 0
    return seq, grp, z, y, core, jnp.where(even, z, y), jnp.where(even, y, z)


def aligned(x, by):
    return pl.multiple_of(x, by)


def call(kernel, outs, args, scratch=(), limit=32, specs=None, out_specs=None, cost=None, alias=None):
    whole = pl.BlockSpec(memory_space=pltpu.VMEM)
    name = kernel.__name__.removesuffix("_kernel")
    return pl.pallas_call(
        kernel,
        out_shape=[jax.ShapeDtypeStruct(s, t) for s, t in outs],
        in_specs=[specs.get(n, whole) if specs else whole for n in range(len(args))],
        out_specs=out_specs or [whole] * len(outs),
        scratch_shapes=list(scratch),
        compiler_params=pltpu.CompilerParams(vmem_limit_bytes=limit * 1024 * 1024),
        cost_estimate=cost,
        input_output_aliases=alias or {},
        name=name,
    )(*args)


SMEM = pl.BlockSpec(memory_space=pltpu.SMEM)


def pages_kernel(old_k, old_v, src_page, page_row, page_len, out, src_s, row_s, len_s, tiles, sems):
    grp = spot()[1]
    pairs = [(src_page, src_s), (page_row, row_s), (page_len, len_s)]
    for d in range(NG):
        cols = pl.ds(d * TWO, TWO)
        pairs.append((old_k.at[:, cols], out.at[d, pl.ds(0, HALF), :]))
        pairs.append((old_v.at[:, cols], out.at[d, pl.ds(HALF, HALF), :]))
    copies = [pltpu.make_async_copy(a, b, sems.at[n]) for n, (a, b) in enumerate(pairs)]
    for copy in copies:
        copy.start()
    for copy in copies[:3]:
        copy.wait()
    sub, lane = iota((META, TWO), 0), iota((META, TWO), 1)
    tile = jnp.zeros((META, TWO), F32)
    for n in range(NEWP):
        src = src_s[0, grp * NEWP + n]
        values = (src >> 2, src & 3, row_s[0, OLD + n], len_s[0, OLD + n])
        for m, value in enumerate(values):
            tile = jnp.where((lane == n) & (sub == m), value.astype(F32), tile)
    for n in range(OLD):
        tile = jnp.where((sub == 8) & (lane == n), row_s[0, n].astype(F32), tile)
        tile = jnp.where((sub == 9) & (lane == n), len_s[0, n].astype(F32), tile)
    tiles[...] = tile.astype(BF16)
    last = [
        pltpu.make_async_copy(tiles, out.at[d, pl.ds(2 * HALF, META), :], sems.at[len(pairs) + d])
        for d in range(NG)
    ]
    for copy in last:
        copy.start()
    for copy in copies[3:] + last:
        copy.wait()


def split_kernel(q, k, v, xs, keep, send, sems):
    _, _, _, _, core, w, u = spot()
    pairs = []
    for dst, head in ((keep, core), (send, 1 - core)):
        one = pl.ds(aligned(head * HEAD, HEAD), HEAD)
        pairs.append((k.at[:, one], dst.at[pl.ds(0, TOK), :]))
        pairs.append((v.at[:, one], dst.at[pl.ds(TOK, TOK), :]))
        for h in range(4):
            cols = pl.ds(aligned((head * 4 + h) * HEAD, HEAD), HEAD)
            pairs.append((q.at[:, cols], dst.at[pl.ds((2 + h) * TOK, TOK), :]))
    copies = [pltpu.make_async_copy(a, b, sems.at[n]) for n, (a, b) in enumerate(pairs)]
    for copy in copies:
        copy.start()
    fresh = (iota((META, 128), 0) < 4) & (iota((META, 128), 1) < NEWP)
    for dst, at in ((keep, w), (send, u)):
        tile = jnp.zeros((META, 128), F32)
        for d in range(NG):
            part = jnp.where(fresh, xs[d, 2 * HALF :, :HEAD].astype(F32), 0.0)
            tile = tile + pltpu.roll(part, at * 16 + core * 8 + d * NEWP, 1)
        dst[6 * TOK :, :] = tile.astype(BF16)
    for copy in copies:
        copy.wait()


def local_kernel(keep, got, q, xs, k_dec, v_dec, kv_send, q_blk, ks, vs, cs, kb):
    seq, _, _, _, core, _, _ = spot()
    for src, start in ((keep, core * TOK), (got, (1 - core) * TOK)):
        kb[pl.ds(aligned(start, TOK), TOK), :] = src[:TOK, :].astype(F32)
        kv_send[0, pl.ds(aligned(BLK + start, TOK), TOK), :] = src[TOK : 2 * TOK, :]
        for h in range(4):
            q_blk[pl.ds(aligned(h * BLK + start, TOK), TOK), :] = src[
                (2 + h) * TOK : (3 + h) * TOK, :
            ]
    kv_send[0, :BLK, :] = jnp.transpose(kb[...]).astype(BF16)
    meta = keep[6 * TOK :, :].astype(F32) + got[6 * TOK :, :].astype(F32)
    kv_send[0, 2 * BLK : KV_DEC, :] = meta.astype(BF16)
    for n in range(1, SIDE):
        kv_send[n, :KV_DEC, :] = kv_send[0, :KV_DEC, :]

    for n in range(NG):
        ks[n * HALF : (n + 1) * HALF, :] = xs[n, :HALF, :]
        vs[n * HALF : (n + 1) * HALF, :] = xs[n, HALF : 2 * HALF, :]
    ks[OLD_TOK:, :] = k_dec[...]
    vs[OLD_TOK:, :] = v_dec[...]

    def hot(flag):
        return jnp.where(flag, 1.0, 0.0).astype(BF16)

    i = iota((ITEMS, 128), 0)
    swapped = ((i >> 1) & 7) * 16 + (i >> 4) * 2 + (i & 1)
    which = jnp.where(core == 0, i, swapped)
    lane = iota((ITEMS, 128), 1)
    row = (which >> 2).astype(F32)
    token = iota((OLD_TOK, 128), 0)
    at = (token & 15).astype(F32)
    page = (token >> 4) - iota((OLD_TOK, 128), 1)
    count = 0.0
    for n in range(NG):
        numbers = xs[n, 2 * HALF :, :HEAD].astype(F32)
        owner, length = numbers[8:9, :], numbers[9:10, :]
        inside = (page == n * OLD) & (at < length)
        count = count + lax.dot_general(
            hot(row == owner), hot(inside), NT, preferred_element_type=F32
        )
    cs[:, :OLD_TOK] = count
    cs[:, OLD_TOK:] = jnp.where((which == seq) & (lane <= (seq & 3)), 1.0, 0.0)

    order = hot(which == lane)
    stats = jnp.zeros((ITEMS, 128), F32)
    for h in range(HEADS):
        kv = slice(h // 4 * HEAD, (h // 4 + 1) * HEAD)
        query = jnp.dot(order, q[:, h * HEAD : (h + 1) * HEAD], preferred_element_type=F32).astype(BF16)
        scores = EXP2_SCALE * lax.dot_general(query, ks[:, kv], NT, preferred_element_type=F32)
        terms = cs[...]
        scores = jnp.where(terms > 0.5, scores, NEG)
        top = jnp.max(scores, axis=1, keepdims=True).astype(BF16).astype(F32)
        weights = (jnp.exp2(scores - top) * terms).astype(BF16)
        total = jnp.sum(weights.astype(F32), axis=1, keepdims=True)
        mixed = jnp.dot(weights, vs[:, kv], preferred_element_type=F32)
        rows = slice(KV_DEC + h * PER, KV_DEC + (h + 1) * PER)
        kv_send[:, rows, :] = mixed.astype(BF16).reshape(SIDE, PER, HEAD)
        high = total.astype(BF16).astype(F32)
        stats = jnp.where(lane == h, top, stats)
        stats = jnp.where(lane == HEADS + h, high, stats)
        stats = jnp.where(lane == 2 * HEADS + h, total - high, stats)
    kv_send[:, KV_DEC + HEADS * PER :, :] = stats.astype(BF16).reshape(SIDE, PER, 128)


def attend_kernel(qs, keys, keys_other, vals, vals_other, q_dec, out, *refs):
    vs, tri, sel = refs[:3]
    sides = (refs[3:8], refs[8:13])
    seq, _, z, y, core, w, u = spot()
    even = core == 0
    chunks = ((keys, u), (keys_other, u ^ 1))
    row, col = iota((BLK, BLK), 0), iota((BLK, BLK), 1)
    tri[...] = jnp.where(col > row, HIDE, 0.0)
    same = jnp.where(row == col, 1.0, 0.0).astype(BF16)
    for side in sides:
        for h in range(4):
            side[0][h * BLK : (h + 1) * BLK, HEAD:] = same
        for c, (chunk, _) in enumerate(chunks):
            for m in range(SIDE):
                cols = slice(m * BLK, (m + 1) * BLK)
                side[1 + c][:HEAD, cols] = chunk[m * BLK : (m + 1) * BLK, :]
    vs[:KEYS, :HEAD] = vals[...]
    vs[KEYS:, :HEAD] = vals_other[...]
    vs[:, HEAD:] = jnp.where(iota((2 * KEYS, HEAD), 1) == 0, 1.0, 0.0).astype(BF16)

    def score(j, qx, kx_a, kx_b, s_a, s_b):
        to = j * 2 + (u & 1)
        qx[:, :HEAD] = qs[j, :QROWS, :]
        for (_, n), kx, s in zip(chunks, (kx_a, kx_b), (s_a, s_b)):
            full = jnp.where(
                even,
                w + jnp.where(n < to, 1, 0),
                jnp.where(n < to, SIDE, jnp.where(n == to, w, 0)),
            )
            edge = jnp.where(n == to, w, SIDE)
            for m in range(SIDE):
                hidden = jnp.where(m == edge, tri[...], HIDE)
                hidden = jnp.where(m < full, 0.0, hidden).astype(BF16)
                kx[HEAD:, m * BLK : (m + 1) * BLK] = hidden
            s[...] = jnp.dot(qx[...], kx[...], preferred_element_type=F32)

    def mix(j, s_a, s_b):
        lane = iota((BLK, 128), 1)
        stats = jnp.zeros((BLK, 128), F32)
        for part in range(2):
            rows = slice(part * 2 * BLK, (part + 1) * 2 * BLK)
            both = (s_a[rows, :], s_b[rows, :])
            top = EXP2_SCALE * jnp.max(jnp.maximum(*both), axis=1, keepdims=True)
            top = jnp.maximum(top, LOWEST).astype(BF16).astype(F32)
            mixed = 0.0
            for c in range(2):
                weights = jnp.exp2(both[c] * EXP2_SCALE - top).astype(BF16)
                mixed = mixed + jnp.dot(
                    weights, vs[c * KEYS : (c + 1) * KEYS, :], preferred_element_type=F32
                )
            out[j, rows, :] = mixed[:, :HEAD].astype(BF16)
            total = mixed[:, HEAD : HEAD + 1]
            high = total.astype(BF16).astype(F32)
            for h in range(2):
                one = slice(h * BLK, (h + 1) * BLK)
                at = part * 2 + h
                stats = jnp.where(lane == at, top[one], stats)
                stats = jnp.where(lane == 4 + at, high[one], stats)
                stats = jnp.where(lane == 8 + at, (total - high)[one], stats)
        out[j, QROWS:O_FRESH, :] = jnp.transpose(stats)[:META].astype(BF16)

    score(0, *sides[0])
    for j in range(QUAD):
        if j + 1 < QUAD:
            score(j + 1, *sides[(j + 1) % 2])
        mix(j, *sides[j % 2][3:])

    def chip_of(there, across):
        return jnp.where(even, across * SIDE + there, there * SIDE + across)

    numbers = jnp.concatenate(
        [qs[j, Q_META : Q_META + 8, :].astype(F32) for j in range(QUAD)], axis=1
    )
    numbers = jnp.concatenate([numbers[0:4], numbers[4:8]], axis=1)
    source = numbers[0:1, :] * 4.0 + numbers[1:2, :]
    slots = source.shape[1]
    inside = iota((PAGE, slots), 0).astype(F32) < numbers[3:4, :]
    live = []
    for j in range(QUAD):
        owner = (chip_of(j * 2 + (u & 1), w) >> 1).astype(F32)
        live.append(jnp.where((numbers[2:3, :] == owner) & inside, 1.0, 0.0))
    live = jnp.concatenate(live, axis=0).astype(BF16)
    spread = iota((PAGES, KEYS), 1) >> 4 == iota((PAGES, KEYS), 0)
    spread = jnp.where(spread, 1.0, 0.0).astype(BF16)
    at = (iota((PAGE * QUAD, KEYS), 1) & 15) == (iota((PAGE * QUAD, KEYS), 0) & 15)

    pick = iota((16, ITEMS), 0)
    item = chip_of((pick >> 1) * 2 + (u & 1), w) * 2 + (pick & 1)
    pick = jnp.where((iota((16, ITEMS), 1) == item) & (pick < 8), 1.0, 0.0).astype(BF16)
    for h in range(4):
        cols = pl.ds(aligned((core * 4 + h) * HEAD, HEAD), HEAD)
        sel[h * 16 : (h + 1) * 16, :] = jnp.dot(
            pick, q_dec[:, cols], preferred_element_type=F32
        ).astype(BF16)

    all_scores, all_terms = [], []
    for c, (_, n) in enumerate(chunks):
        page = iota((PAGES, slots), 0)
        page = (chip_of(n, page >> 3) * SIDE + (page & 7)).astype(F32)
        there = jnp.where(source == page, 1.0, 0.0).astype(BF16)
        count = lax.dot_general(live, there, NT, preferred_element_type=F32)
        high = count.astype(BF16)
        low = (count - high.astype(F32)).astype(BF16)
        count = jnp.dot(high, spread, preferred_element_type=F32) + jnp.dot(
            low, spread, preferred_element_type=F32
        )
        count = jnp.where(at, count, 0.0)
        which = iota((16, KEYS), 0) >> 1
        terms = jnp.zeros((16, KEYS), F32)
        for j in range(QUAD):
            one = jnp.sum(count[j * PAGE : (j + 1) * PAGE], axis=0, keepdims=True)
            terms = jnp.where(which == j, one, terms)
        terms = jnp.concatenate([terms] * 4, axis=0)
        held = sides[0][1 + c][:HEAD, :]
        scores = EXP2_SCALE * jnp.dot(sel[...], held, preferred_element_type=F32)
        all_scores.append(jnp.where(terms > 0.5, scores, NEG))
        all_terms.append(terms)
    top = jnp.max(jnp.maximum(*all_scores), axis=1, keepdims=True).astype(BF16).astype(F32)
    mixed = 0.0
    for c in range(2):
        weights = (jnp.exp2(all_scores[c] - top) * all_terms[c]).astype(BF16)
        mixed = mixed + jnp.dot(
            weights, vs[c * KEYS : (c + 1) * KEYS, :], preferred_element_type=F32
        )
    total = mixed[:, HEAD : HEAD + 1]
    high = total.astype(BF16).astype(F32)
    lane = iota((FRESH, 128), 1)
    stats = jnp.where(lane == 0, top, jnp.where(lane == 1, high, 0.0))
    stats = jnp.where(lane == 2, total - high, stats)
    for j in range(QUAD):
        rows = [slice(h * 16 + 2 * j, h * 16 + 2 * j + 2) for h in range(4)]
        pieces = [mixed[r, :HEAD] for r in rows] + [stats[r] for r in rows]
        out[j, O_FRESH:, :] = jnp.concatenate(pieces, axis=0).astype(BF16)


def combine(values, stats, split):
    mixes, tops, totals = [], [], []
    for h in range(HEADS):
        top_of = [s[:, h : h + 1] for s in stats]
        top = functools.reduce(jnp.maximum, top_of)
        total, mixed = 0.0, 0.0
        for value, s, t in zip(values, stats, top_of):
            factor = jnp.exp2(t - top)
            each = s[:, HEADS + h : HEADS + h + 1]
            if split:
                each = each + s[:, 2 * HEADS + h : 2 * HEADS + h + 1]
            total = total + each * factor
            mixed = mixed + value(h) * factor
        mixes.append(mixed)
        tops.append(top)
        totals.append(total)
    return mixes, tops, totals


def stat_tile(tops, totals, split=False):
    lane = iota((tops[0].shape[0], 128), 1)
    tile = jnp.zeros(lane.shape, F32)
    for h in range(HEADS):
        tile = jnp.where(lane == h, tops[h], tile)
        if split:
            high = totals[h].astype(BF16).astype(F32)
            tile = jnp.where(lane == HEADS + h, high, tile)
            tile = jnp.where(lane == 2 * HEADS + h, totals[h] - high, tile)
        else:
            tile = jnp.where(lane == HEADS + h, totals[h], tile)
    return tile


def merge_kernel(got, keys, vals, send, keep):
    send[:META, :] = sum(got[n, 2 * BLK : KV_DEC, :].astype(F32) for n in range(SIDE)).astype(BF16)
    for n in range(SIDE):
        keys[n * BLK : (n + 1) * BLK, :] = got[n, :BLK, :]
        vals[n * BLK : (n + 1) * BLK, :] = got[n, BLK : 2 * BLK, :]

    def values(n):
        return lambda h: got[n, KV_DEC + h * PER : KV_DEC + (h + 1) * PER, :].astype(F32)

    mixes, tops, totals = combine(
        [values(n) for n in range(SIDE)],
        [got[n, KV_MSG - PER :, :].astype(F32) for n in range(SIDE)],
        True,
    )
    even = spot()[6] & 1 == 0

    def halves(x):
        a = jnp.concatenate([x[4 * n : 4 * n + 2] for n in range(QUAD)], axis=0)
        b = jnp.concatenate([x[4 * n + 2 : 4 * n + 4] for n in range(QUAD)], axis=0)
        return jnp.where(even, a, b), jnp.where(even, b, a)

    theirs = []
    for h in range(HEADS):
        mine, other = halves(mixes[h])
        keep[8 * h : 8 * h + 8, :] = mine
        theirs.append(other)
    mine, other = halves(stat_tile(tops, totals, True))
    keep[64:, :] = mine
    theirs += [other, jnp.zeros((8, 128), F32)]
    send[META:, :] = jnp.concatenate(theirs, axis=0).astype(BF16)


def queries_kernel(q_blk, mine, other, keep, send):
    def kept(h):
        return keep[8 * h : 8 * h + 8, :]

    def came(h):
        return other[META + 8 * h : META + 8 * h + 8, :].astype(F32)

    mixes, tops, totals = combine(
        [kept, came], [keep[64:, :], other[META + 64 : META + 72, :].astype(F32)], True
    )
    pieces = mixes + [stat_tile(tops, totals, True)]
    numbers = jnp.concatenate(
        [mine[:META, :].astype(F32)[:4], other[:META, :].astype(F32)[:4], jnp.zeros((8, 128), F32)], 0
    ).astype(BF16)
    for n in range(QUAD):
        send[n, :QROWS, :] = q_blk[...]
        send[n, Q_META:Q_DEC, :] = numbers
        rows = [piece[2 * n : 2 * n + 2] for piece in pieces] + [jnp.zeros((14, 128), F32)]
        send[n, Q_DEC:, :] = jnp.concatenate(rows, axis=0).astype(BF16)


def pair_kernel(got, qs, attn_keep, dec_keep, send, attn):
    core = spot()[4]
    even = core == 0
    stats = [got[n, QROWS:O_FRESH, :].astype(F32) for n in range(QUAD)]
    tops = [s[0:4] for s in stats]
    top = functools.reduce(jnp.maximum, tops)
    factors = [jnp.exp2(t - top) for t in tops]
    total = sum(f * (s[4:8] + s[8:12]) for f, s in zip(factors, stats))
    shares = jnp.concatenate([f / total for f in factors] + [jnp.zeros((112, 128), F32)], 0)
    shares = jnp.transpose(shares)
    for h in range(4):
        rows = slice(h * BLK, (h + 1) * BLK)
        out = 0.0
        for n in range(QUAD):
            out = out + got[n, rows, :].astype(F32) * shares[:, n * 4 + h : n * 4 + h + 1]
        attn[rows, :] = out.astype(BF16)

    def old(n):
        return lambda h: qs[n, Q_DEC:, :].astype(F32)[2 * h : 2 * h + 2]

    def fresh(n):
        return lambda h: got[n, O_FRESH:, :].astype(F32)[2 * (h % 4) : 2 * (h % 4) + 2]

    old_stats = [qs[n, Q_DEC:, :].astype(F32)[16:18] for n in range(QUAD)]
    fresh_stats = []
    lane = iota((2, 128), 1)
    for n in range(QUAD):
        tile = got[n, O_FRESH:, :].astype(F32)[8:]
        placed = jnp.zeros((2, 128), F32)
        for h in range(HEADS):
            both = tile[2 * (h % 4) : 2 * (h % 4) + 2]
            here = core == h // 4
            placed = jnp.where(lane == h, jnp.where(here, both[:, 0:1], NEG), placed)
            for m in (1, 2):
                placed = jnp.where(lane == m * HEADS + h, jnp.where(here, both[:, m : m + 1], 0.0), placed)
        fresh_stats.append(placed)
    mixes, tops, totals = combine(
        [old(n) for n in range(QUAD)] + [fresh(n) for n in range(QUAD)],
        old_stats + fresh_stats,
        True,
    )
    keep_stats = stat_tile(tops, totals)
    send_stats = stat_tile(tops, totals, True)
    dec_keep[8:, :] = jnp.broadcast_to(jnp.where(even, keep_stats[0:1], keep_stats[1:2]), (8, 128))
    sent = []
    for h in range(HEADS):
        dec_keep[h : h + 1, :] = jnp.where(even, mixes[h][0:1], mixes[h][1:2])
        sent.append(jnp.where(even, mixes[h][1:2], mixes[h][0:1]))
    sent.append(jnp.where(even, send_stats[1:2], send_stats[0:1]))
    sent.append(jnp.zeros((7, 128), F32))
    send[4 * TOK :, :] = jnp.concatenate(sent, 0).astype(BF16)
    for h in range(4):
        rows = slice(h * TOK, (h + 1) * TOK)
        attn_keep[rows, :] = attn[pl.ds(aligned(h * BLK + core * TOK, TOK), TOK), :]
        send[rows, :] = attn[pl.ds(aligned(h * BLK + (1 - core) * TOK, TOK), TOK), :]


def final_kernel(attn_keep, dec_keep, got, attn_out, dec_out):
    core = spot()[4]
    for h in range(4):
        rows = slice(h * TOK, (h + 1) * TOK)
        for src, head in ((attn_keep, core), (got, 1 - core)):
            attn_out[:, pl.ds(aligned((head * 4 + h) * HEAD, HEAD), HEAD)] = src[rows, :]
    theirs = got[4 * TOK :, :].astype(F32)
    other = theirs[8:9, :]
    for h in range(HEADS):
        top_a, top_b = dec_keep[8:9, h : h + 1], other[:, h : h + 1]
        total_a = dec_keep[8:9, HEADS + h : HEADS + h + 1]
        total_b = other[:, HEADS + h : HEADS + h + 1] + other[:, 2 * HEADS + h : 2 * HEADS + h + 1]
        top = jnp.maximum(top_a, top_b)
        scale_a, scale_b = jnp.exp2(top_a - top), jnp.exp2(top_b - top)
        mixed = dec_keep[h : h + 1, :] * scale_a + theirs[h : h + 1, :] * scale_b
        dec_out[h : h + 1, :] = (mixed / (total_a * scale_a + total_b * scale_b)).astype(BF16)


def exchange(x, groups):
    return lax.all_to_all(x, "seq", 0, 0, axis_index_groups=groups, tiled=True)


def to_other_core(x):
    return lax.ppermute(x, "seq", [(n, n ^ 1) for n in range(2 * SIDE * SIDE)])


def body(q_pre, k_pre, v_pre, old_k, old_v, src_page, page_row, page_len, q_dec, dec_k, dec_v):
    seq, grp = lax.axis_index("seq"), lax.axis_index("grp")
    core = seq & 1
    far = pl.BlockSpec(memory_space=pltpu.HBM)
    counts = page_row.shape[1]
    (x_send,) = call(
        pages_kernel,
        [((NG, X_MSG, TWO), BF16)],
        (old_k.reshape(HALF, -1), old_v.reshape(HALF, -1), src_page, page_row, page_len),
        scratch=(
            pltpu.SMEM(src_page.shape, jnp.int32),
            pltpu.SMEM((1, counts), jnp.int32),
            pltpu.SMEM((1, counts), jnp.int32),
            pltpu.VMEM((META, TWO), BF16),
            pltpu.SemaphoreType.DMA((3 + 3 * NG,)),
        ),
        specs={n: far for n in range(5)},
        out_specs=[far],
        limit=60,
    )
    xs = lax.all_to_all(x_send, "grp", 0, 0, tiled=True)
    keep, send = call(
        split_kernel,
        [((PAIR_MSG, 128), BF16)] * 2,
        (q_pre, k_pre, v_pre, xs),
        scratch=(pltpu.SemaphoreType.DMA((12,)),),
        specs={n: far for n in range(3)},
    )
    q_mine = lax.dynamic_slice_in_dim(q_dec, grp * HEADS * HEAD, HEADS * HEAD, 2)
    q_mine = q_mine.reshape(ITEMS, HEADS * HEAD)

    def own_tokens(x):
        part = lax.dynamic_slice(x, (seq // STEPS, 0, grp * TWO), (1, STEPS, TWO))[0]
        return jnp.pad(part, ((0, 128 - STEPS), (0, 0)))

    kv_send, q_blk = call(
        local_kernel,
        [((SIDE, KV_MSG, 128), BF16), ((QROWS, 128), BF16)],
        (keep, to_other_core(send), q_mine, xs, own_tokens(dec_k), own_tokens(dec_v)),
        scratch=(
            pltpu.VMEM((DEC_TOK, TWO), BF16),
            pltpu.VMEM((DEC_TOK, TWO), BF16),
            pltpu.VMEM((ITEMS, DEC_TOK), F32),
            pltpu.VMEM((BLK, HEAD), F32),
        ),
    )
    keys, vals, small, keep_dec = call(
        merge_kernel,
        [((KEYS, 128), BF16), ((KEYS, 128), BF16), ((PAIR_SMALL, 128), BF16), ((72, 128), F32)],
        (exchange(kv_send, KEY_GROUPS),),
    )
    small_other = lax.ppermute(small, "seq", NEIGHBOURS)
    keys, vals, small_other = lax.optimization_barrier((keys, vals, small_other))
    keys_other = lax.ppermute(keys, "seq", NEIGHBOURS)
    vals_other = lax.ppermute(vals, "seq", NEIGHBOURS)
    (q_send,) = call(
        queries_kernel,
        [((QUAD, Q_MSG, 128), BF16)],
        (q_blk, small, small_other, keep_dec),
    )
    qs = exchange(q_send, QUADS)
    work = QROWS * SIDE * KEYS
    side = (
        pltpu.VMEM((QROWS, TWO), BF16),
        pltpu.VMEM((TWO, KEYS), BF16),
        pltpu.VMEM((TWO, KEYS), BF16),
        pltpu.VMEM((QROWS, KEYS), F32),
        pltpu.VMEM((QROWS, KEYS), F32),
    )
    (o_send,) = call(
        attend_kernel,
        [((QUAD, O_MSG, 128), BF16)],
        (qs, keys, keys_other, vals, vals_other, q_mine),
        scratch=(
            pltpu.VMEM((2 * KEYS, TWO), BF16),
            pltpu.VMEM((BLK, BLK), F32),
            pltpu.VMEM((FRESH, HEAD), BF16),
            *side,
            *side,
        ),
        cost=pl.CostEstimate(flops=work * 512, bytes_accessed=4 * 1024 * 1024, transcendentals=work),
    )
    attn_keep, dec_keep, last = call(
        pair_kernel,
        [((4 * TOK, 128), BF16), ((16, 128), F32), ((LAST_MSG, 128), BF16)],
        (exchange(o_send, QUADS), qs),
        scratch=(pltpu.VMEM((QROWS, HEAD), BF16),),
    )
    attn_out, dec_out = call(
        final_kernel,
        [((TOK, HEADS * HEAD), BF16), ((HEADS, HEAD), BF16)],
        (attn_keep, dec_keep, to_other_core(last)),
    )
    return attn_out, dec_out


def solution(mesh):
    return jax.shard_map(
        body,
        mesh=mesh,
        in_specs=(
            P("seq", "grp"),
            P("seq", "grp"),
            P("seq", "grp"),
            P("seq", "grp", None, None),
            P("seq", "grp", None, None),
            P("seq", None),
            P("seq", "grp"),
            P("seq", "grp"),
            P(),
            P(),
            P(),
        ),
        out_specs=(P("seq", "grp"), P(("seq", "grp"), None)),
        check_vma=False,
    )
```

```python
import functools
import math

import jax
import jax.numpy as jnp
from jax import lax
from jax.experimental import pallas as pl
from jax.experimental.pallas import tpu as pltpu
from jax.sharding import PartitionSpec as P

HEAD = 128
PAGE = 16
OLD = 10
NEWP = 2
ROWS = 32
STEPS = 4
ITEMS = ROWS * STEPS
SIDE = 8
NG = 4
TOK = 64
BLK = 2 * TOK
KEYS = SIDE * BLK
QROWS = 4 * BLK
HEADS = 8
TWO = 2 * HEAD
EXP2_SCALE = math.log2(math.e) / math.sqrt(HEAD)
NEG = -(2.0**100)
HIDE = -(2.0**80)
LOWEST = -(2.0**60)
META = 16
PAIR_MSG = 6 * TOK + META
HALF = OLD * PAGE
X_MSG = 2 * HALF + META
OLD_TOK = NG * HALF
DEC_TOK = OLD_TOK + 128
PER = ITEMS // SIDE
DEC_MSG = HEADS * PER + PER
KV_DEC = 2 * BLK + META
KV_MSG = KV_DEC + DEC_MSG
PAGES = KEYS // PAGE
LAST_MSG = 4 * TOK + 16
QUAD = 4
PAIR_DEC = 80
PAIR_SMALL = META + PAIR_DEC
Q_META = QROWS
Q_DEC = QROWS + META
Q_MSG = Q_DEC + 32
O_FRESH = QROWS + META
O_MSG = O_FRESH + 16
FRESH = 4 * 16
NT = (((1,), (1,)), ((), ()))
F32 = jnp.float32
BF16 = jnp.bfloat16


def seq_of(z, y, core):
    return (z * SIDE + y) * 2 + core


ALONG_Z = [[[seq_of(i, j, c) for i in range(SIDE)] for j in range(SIDE)] for c in range(2)]
ALONG_Y = [[[seq_of(j, i, c) for i in range(SIDE)] for j in range(SIDE)] for c in range(2)]
KEY_GROUPS = ALONG_Z[0] + ALONG_Y[1]
QUERY_GROUPS = ALONG_Y[0] + ALONG_Z[1]
QUADS = [group[p::2] for group in QUERY_GROUPS for p in range(2)]
NEIGHBOURS = [(group[n], group[n ^ 1]) for group in QUERY_GROUPS for n in range(SIDE)]


def iota(shape, dim):
    return lax.broadcasted_iota(jnp.int32, shape, dim)


def spot():
    seq, grp = lax.axis_index("seq"), lax.axis_index("grp")
    core = seq & 1
    y = (seq >> 1) & (SIDE - 1)
    z = seq >> 4
    even = core == 0
    return seq, grp, z, y, core, jnp.where(even, z, y), jnp.where(even, y, z)


def aligned(x, by):
    return pl.multiple_of(x, by)


def call(kernel, outs, args, scratch=(), limit=32, specs=None, out_specs=None, cost=None, alias=None):
    whole = pl.BlockSpec(memory_space=pltpu.VMEM)
    name = kernel.__name__.removesuffix("_kernel")
    return pl.pallas_call(
        kernel,
        out_shape=[jax.ShapeDtypeStruct(s, t) for s, t in outs],
        in_specs=[specs.get(n, whole) if specs else whole for n in range(len(args))],
        out_specs=out_specs or [whole] * len(outs),
        scratch_shapes=list(scratch),
        compiler_params=pltpu.CompilerParams(vmem_limit_bytes=limit * 1024 * 1024),
        cost_estimate=cost,
        input_output_aliases=alias or {},
        name=name,
    )(*args)


SMEM = pl.BlockSpec(memory_space=pltpu.SMEM)


def pages_kernel(old_k, old_v, src_page, page_row, page_len, out, src_s, row_s, len_s, sems):
    grp = spot()[1]
    pairs = [(src_page, src_s), (page_row, row_s), (page_len, len_s)]
    for d in range(NG):
        cols = pl.ds(d * TWO, TWO)
        pairs.append((old_k.at[:, cols], out.at[d, pl.ds(0, HALF), :]))
        pairs.append((old_v.at[:, cols], out.at[d, pl.ds(HALF, HALF), :]))
    copies = [pltpu.make_async_copy(a, b, sems.at[n]) for n, (a, b) in enumerate(pairs)]
    for copy in copies:
        copy.start()
    for copy in copies[:3]:
        copy.wait()
    sub, lane = iota((META, TWO), 0), iota((META, TWO), 1)
    tile = jnp.zeros((META, TWO), F32)
    for n in range(NEWP):
        src = src_s[0, grp * NEWP + n]
        values = (src >> 2, src & 3, row_s[0, OLD + n], len_s[0, OLD + n])
        for m, value in enumerate(values):
            tile = jnp.where((lane == n) & (sub == m), value.astype(F32), tile)
    for n in range(OLD):
        tile = jnp.where((sub == 8) & (lane == n), row_s[0, n].astype(F32), tile)
        tile = jnp.where((sub == 9) & (lane == n), len_s[0, n].astype(F32), tile)
    for d in range(NG):
        out[d, 2 * HALF :, :] = tile.astype(BF16)
    for copy in copies[3:]:
        copy.wait()


def split_kernel(q, k, v, xs, keep, send, sems):
    _, _, _, _, core, w, u = spot()
    pairs = []
    for dst, head in ((keep, core), (send, 1 - core)):
        one = pl.ds(aligned(head * HEAD, HEAD), HEAD)
        pairs.append((k.at[:, one], dst.at[pl.ds(0, TOK), :]))
        pairs.append((v.at[:, one], dst.at[pl.ds(TOK, TOK), :]))
        for h in range(4):
            cols = pl.ds(aligned((head * 4 + h) * HEAD, HEAD), HEAD)
            pairs.append((q.at[:, cols], dst.at[pl.ds((2 + h) * TOK, TOK), :]))
    copies = [pltpu.make_async_copy(a, b, sems.at[n]) for n, (a, b) in enumerate(pairs)]
    for copy in copies:
        copy.start()
    fresh = (iota((META, 128), 0) < 4) & (iota((META, 128), 1) < NEWP)
    for dst, at in ((keep, w), (send, u)):
        tile = jnp.zeros((META, 128), F32)
        for d in range(NG):
            part = jnp.where(fresh, xs[d, 2 * HALF :, :HEAD].astype(F32), 0.0)
            tile = tile + pltpu.roll(part, at * 16 + core * 8 + d * NEWP, 1)
        dst[6 * TOK :, :] = tile.astype(BF16)
    for copy in copies:
        copy.wait()


def item_order(core):
    i = iota((ITEMS, 128), 0)
    swapped = ((i >> 1) & 7) * 16 + (i >> 4) * 2 + (i & 1)
    return jnp.where(core == 0, i, swapped)


def order_kernel(q, out):
    flag = item_order(spot()[4]) == iota((ITEMS, 128), 1)
    order = jnp.where(flag, 1.0, 0.0).astype(BF16)
    out[...] = jnp.dot(order, q[...], preferred_element_type=F32).astype(BF16)


def local_kernel(keep, got, q, xs, k_dec, v_dec, kv_send, q_blk, ks, vs, cs, kb):
    seq, _, _, _, core, _, _ = spot()
    for src, start in ((keep, core * TOK), (got, (1 - core) * TOK)):
        kb[pl.ds(aligned(start, TOK), TOK), :] = src[:TOK, :].astype(F32)
        kv_send[0, pl.ds(aligned(BLK + start, TOK), TOK), :] = src[TOK : 2 * TOK, :]
        for h in range(4):
            q_blk[pl.ds(aligned(h * BLK + start, TOK), TOK), :] = src[
                (2 + h) * TOK : (3 + h) * TOK, :
            ]
    kv_send[0, :BLK, :] = jnp.transpose(kb[...]).astype(BF16)
    meta = keep[6 * TOK :, :].astype(F32) + got[6 * TOK :, :].astype(F32)
    kv_send[0, 2 * BLK : KV_DEC, :] = meta.astype(BF16)
    for n in range(1, SIDE):
        kv_send[n, :KV_DEC, :] = kv_send[0, :KV_DEC, :]

    for n in range(NG):
        ks[n * HALF : (n + 1) * HALF, :] = xs[n, :HALF, :]
        vs[n * HALF : (n + 1) * HALF, :] = xs[n, HALF : 2 * HALF, :]
    ks[OLD_TOK:, :] = k_dec[...]
    vs[OLD_TOK:, :] = v_dec[...]

    def hot(flag):
        return jnp.where(flag, 1.0, 0.0).astype(BF16)

    which = item_order(core)
    lane = iota((ITEMS, 128), 1)
    row = (which >> 2).astype(F32)
    token = iota((OLD_TOK, 128), 0)
    at = (token & 15).astype(F32)
    page = (token >> 4) - iota((OLD_TOK, 128), 1)
    count = 0.0
    for n in range(NG):
        numbers = xs[n, 2 * HALF :, :HEAD].astype(F32)
        owner, length = numbers[8:9, :], numbers[9:10, :]
        inside = (page == n * OLD) & (at < length)
        count = count + lax.dot_general(
            hot(row == owner), hot(inside), NT, preferred_element_type=F32
        )
    cs[:, :OLD_TOK] = count
    cs[:, OLD_TOK:] = jnp.where((which == seq) & (lane <= (seq & 3)), 1.0, 0.0)

    stats = jnp.zeros((ITEMS, 128), F32)
    for h in range(HEADS):
        kv = slice(h // 4 * HEAD, (h // 4 + 1) * HEAD)
        query = q[:, h * HEAD : (h + 1) * HEAD]
        scores = EXP2_SCALE * lax.dot_general(query, ks[:, kv], NT, preferred_element_type=F32)
        terms = cs[...]
        scores = jnp.where(terms > 0.5, scores, NEG)
        top = jnp.max(scores, axis=1, keepdims=True).astype(BF16).astype(F32)
        weights = (jnp.exp2(scores - top) * terms).astype(BF16)
        total = jnp.sum(weights.astype(F32), axis=1, keepdims=True)
        mixed = jnp.dot(weights, vs[:, kv], preferred_element_type=F32)
        rows = slice(KV_DEC + h * PER, KV_DEC + (h + 1) * PER)
        kv_send[:, rows, :] = mixed.astype(BF16).reshape(SIDE, PER, HEAD)
        high = total.astype(BF16).astype(F32)
        stats = jnp.where(lane == h, top, stats)
        stats = jnp.where(lane == HEADS + h, high, stats)
        stats = jnp.where(lane == 2 * HEADS + h, total - high, stats)
    kv_send[:, KV_DEC + HEADS * PER :, :] = stats.astype(BF16).reshape(SIDE, PER, 128)


def attend_kernel(qs, keys, keys_other, vals, vals_other, q_dec, out, *refs):
    vs, tri, sel = refs[:3]
    sides = (refs[3:8], refs[8:13])
    seq, _, z, y, core, w, u = spot()
    even = core == 0
    chunks = ((keys, u), (keys_other, u ^ 1))
    row, col = iota((BLK, BLK), 0), iota((BLK, BLK), 1)
    tri[...] = jnp.where(col > row, HIDE, 0.0)
    same = jnp.where(row == col, 1.0, 0.0).astype(BF16)
    for side in sides:
        for h in range(4):
            side[0][h * BLK : (h + 1) * BLK, HEAD:] = same
        for c, (chunk, _) in enumerate(chunks):
            for m in range(SIDE):
                cols = slice(m * BLK, (m + 1) * BLK)
                side[1 + c][:HEAD, cols] = chunk[m * BLK : (m + 1) * BLK, :]
    vs[:KEYS, :HEAD] = vals[...]
    vs[KEYS:, :HEAD] = vals_other[...]
    vs[:, HEAD:] = jnp.where(iota((2 * KEYS, HEAD), 1) == 0, 1.0, 0.0).astype(BF16)

    def score(j, qx, kx_a, kx_b, s_a, s_b):
        to = j * 2 + (u & 1)
        qx[:, :HEAD] = qs[j, :QROWS, :]
        for (_, n), kx, s in zip(chunks, (kx_a, kx_b), (s_a, s_b)):
            full = jnp.where(
                even,
                w + jnp.where(n < to, 1, 0),
                jnp.where(n < to, SIDE, jnp.where(n == to, w, 0)),
            )
            edge = jnp.where(n == to, w, SIDE)
            for m in range(SIDE):
                hidden = jnp.where(m == edge, tri[...], HIDE)
                hidden = jnp.where(m < full, 0.0, hidden).astype(BF16)
                kx[HEAD:, m * BLK : (m + 1) * BLK] = hidden
            s[...] = jnp.dot(qx[...], kx[...], preferred_element_type=F32)

    def mix(j, s_a, s_b):
        lane = iota((BLK, 128), 1)
        stats = jnp.zeros((BLK, 128), F32)
        for part in range(2):
            rows = slice(part * 2 * BLK, (part + 1) * 2 * BLK)
            both = (s_a[rows, :], s_b[rows, :])
            top = EXP2_SCALE * jnp.max(jnp.maximum(*both), axis=1, keepdims=True)
            top = jnp.maximum(top, LOWEST).astype(BF16).astype(F32)
            mixed = 0.0
            for c in range(2):
                weights = jnp.exp2(both[c] * EXP2_SCALE - top).astype(BF16)
                mixed = mixed + jnp.dot(
                    weights, vs[c * KEYS : (c + 1) * KEYS, :], preferred_element_type=F32
                )
            out[j, rows, :] = mixed[:, :HEAD].astype(BF16)
            total = mixed[:, HEAD : HEAD + 1]
            high = total.astype(BF16).astype(F32)
            for h in range(2):
                one = slice(h * BLK, (h + 1) * BLK)
                at = part * 2 + h
                stats = jnp.where(lane == at, top[one], stats)
                stats = jnp.where(lane == 4 + at, high[one], stats)
                stats = jnp.where(lane == 8 + at, (total - high)[one], stats)
        out[j, QROWS:O_FRESH, :] = jnp.transpose(stats)[:META].astype(BF16)

    score(0, *sides[0])
    for j in range(QUAD):
        if j + 1 < QUAD:
            score(j + 1, *sides[(j + 1) % 2])
        mix(j, *sides[j % 2][3:])

    def chip_of(there, across):
        return jnp.where(even, across * SIDE + there, there * SIDE + across)

    numbers = jnp.concatenate(
        [qs[j, Q_META : Q_META + 8, :].astype(F32) for j in range(QUAD)], axis=1
    )
    numbers = jnp.concatenate([numbers[0:4], numbers[4:8]], axis=1)
    source = numbers[0:1, :] * 4.0 + numbers[1:2, :]
    slots = source.shape[1]
    inside = iota((PAGE, slots), 0).astype(F32) < numbers[3:4, :]
    live = []
    for j in range(QUAD):
        owner = (chip_of(j * 2 + (u & 1), w) >> 1).astype(F32)
        live.append(jnp.where((numbers[2:3, :] == owner) & inside, 1.0, 0.0))
    live = jnp.concatenate(live, axis=0).astype(BF16)
    spread = iota((PAGES, KEYS), 1) >> 4 == iota((PAGES, KEYS), 0)
    spread = jnp.where(spread, 1.0, 0.0).astype(BF16)
    at = (iota((PAGE * QUAD, KEYS), 1) & 15) == (iota((PAGE * QUAD, KEYS), 0) & 15)

    pick = iota((16, ITEMS), 0)
    item = chip_of((pick >> 1) * 2 + (u & 1), w) * 2 + (pick & 1)
    pick = jnp.where((iota((16, ITEMS), 1) == item) & (pick < 8), 1.0, 0.0).astype(BF16)
    for h in range(4):
        cols = pl.ds(aligned((core * 4 + h) * HEAD, HEAD), HEAD)
        sel[h * 16 : (h + 1) * 16, :] = jnp.dot(
            pick, q_dec[:, cols], preferred_element_type=F32
        ).astype(BF16)

    all_scores, all_terms = [], []
    for c, (_, n) in enumerate(chunks):
        page = iota((PAGES, slots), 0)
        page = (chip_of(n, page >> 3) * SIDE + (page & 7)).astype(F32)
        there = jnp.where(source == page, 1.0, 0.0).astype(BF16)
        count = lax.dot_general(live, there, NT, preferred_element_type=F32)
        high = count.astype(BF16)
        low = (count - high.astype(F32)).astype(BF16)
        count = jnp.dot(high, spread, preferred_element_type=F32) + jnp.dot(
            low, spread, preferred_element_type=F32
        )
        count = jnp.where(at, count, 0.0)
        which = iota((16, KEYS), 0) >> 1
        terms = jnp.zeros((16, KEYS), F32)
        for j in range(QUAD):
            one = jnp.sum(count[j * PAGE : (j + 1) * PAGE], axis=0, keepdims=True)
            terms = jnp.where(which == j, one, terms)
        terms = jnp.concatenate([terms] * 4, axis=0)
        held = sides[0][1 + c][:HEAD, :]
        scores = EXP2_SCALE * jnp.dot(sel[...], held, preferred_element_type=F32)
        all_scores.append(jnp.where(terms > 0.5, scores, NEG))
        all_terms.append(terms)
    top = jnp.max(jnp.maximum(*all_scores), axis=1, keepdims=True).astype(BF16).astype(F32)
    mixed = 0.0
    for c in range(2):
        weights = (jnp.exp2(all_scores[c] - top) * all_terms[c]).astype(BF16)
        mixed = mixed + jnp.dot(
            weights, vs[c * KEYS : (c + 1) * KEYS, :], preferred_element_type=F32
        )
    total = mixed[:, HEAD : HEAD + 1]
    high = total.astype(BF16).astype(F32)
    lane = iota((FRESH, 128), 1)
    stats = jnp.where(lane == 0, top, jnp.where(lane == 1, high, 0.0))
    stats = jnp.where(lane == 2, total - high, stats)
    for j in range(QUAD):
        rows = [slice(h * 16 + 2 * j, h * 16 + 2 * j + 2) for h in range(4)]
        pieces = [mixed[r, :HEAD] for r in rows] + [stats[r] for r in rows]
        out[j, O_FRESH:, :] = jnp.concatenate(pieces, axis=0).astype(BF16)


def combine(values, stats, split):
    mixes, tops, totals = [], [], []
    for h in range(HEADS):
        top_of = [s[:, h : h + 1] for s in stats]
        top = functools.reduce(jnp.maximum, top_of)
        total, mixed = 0.0, 0.0
        for value, s, t in zip(values, stats, top_of):
            factor = jnp.exp2(t - top)
            each = s[:, HEADS + h : HEADS + h + 1]
            if split:
                each = each + s[:, 2 * HEADS + h : 2 * HEADS + h + 1]
            total = total + each * factor
            mixed = mixed + value(h) * factor
        mixes.append(mixed)
        tops.append(top)
        totals.append(total)
    return mixes, tops, totals


def stat_tile(tops, totals, split=False):
    lane = iota((tops[0].shape[0], 128), 1)
    tile = jnp.zeros(lane.shape, F32)
    for h in range(HEADS):
        tile = jnp.where(lane == h, tops[h], tile)
        if split:
            high = totals[h].astype(BF16).astype(F32)
            tile = jnp.where(lane == HEADS + h, high, tile)
            tile = jnp.where(lane == 2 * HEADS + h, totals[h] - high, tile)
        else:
            tile = jnp.where(lane == HEADS + h, totals[h], tile)
    return tile


def merge_kernel(got, keys, vals, send, keep):
    send[:META, :] = sum(got[n, 2 * BLK : KV_DEC, :].astype(F32) for n in range(SIDE)).astype(BF16)
    for n in range(SIDE):
        keys[n * BLK : (n + 1) * BLK, :] = got[n, :BLK, :]
        vals[n * BLK : (n + 1) * BLK, :] = got[n, BLK : 2 * BLK, :]

    def values(n):
        return lambda h: got[n, KV_DEC + h * PER : KV_DEC + (h + 1) * PER, :].astype(F32)

    mixes, tops, totals = combine(
        [values(n) for n in range(SIDE)],
        [got[n, KV_MSG - PER :, :].astype(F32) for n in range(SIDE)],
        True,
    )
    even = spot()[6] & 1 == 0

    def halves(x):
        a = jnp.concatenate([x[4 * n : 4 * n + 2] for n in range(QUAD)], axis=0)
        b = jnp.concatenate([x[4 * n + 2 : 4 * n + 4] for n in range(QUAD)], axis=0)
        return jnp.where(even, a, b), jnp.where(even, b, a)

    theirs = []
    for h in range(HEADS):
        mine, other = halves(mixes[h])
        keep[8 * h : 8 * h + 8, :] = mine
        theirs.append(other)
    mine, other = halves(stat_tile(tops, totals, True))
    keep[64:, :] = mine
    theirs += [other, jnp.zeros((8, 128), F32)]
    send[META:, :] = jnp.concatenate(theirs, axis=0).astype(BF16)


def queries_kernel(q_blk, mine, other, keep, send):
    def kept(h):
        return keep[8 * h : 8 * h + 8, :]

    def came(h):
        return other[META + 8 * h : META + 8 * h + 8, :].astype(F32)

    mixes, tops, totals = combine(
        [kept, came], [keep[64:, :], other[META + 64 : META + 72, :].astype(F32)], True
    )
    pieces = mixes + [stat_tile(tops, totals, True)]
    numbers = jnp.concatenate(
        [mine[:META, :].astype(F32)[:4], other[:META, :].astype(F32)[:4], jnp.zeros((8, 128), F32)], 0
    ).astype(BF16)
    for n in range(QUAD):
        send[n, :QROWS, :] = q_blk[...]
        send[n, Q_META:Q_DEC, :] = numbers
        rows = [piece[2 * n : 2 * n + 2] for piece in pieces] + [jnp.zeros((14, 128), F32)]
        send[n, Q_DEC:, :] = jnp.concatenate(rows, axis=0).astype(BF16)


def pair_kernel(got, qs, attn_keep, dec_keep, send, attn):
    core = spot()[4]
    even = core == 0
    stats = [got[n, QROWS:O_FRESH, :].astype(F32) for n in range(QUAD)]
    tops = [s[0:4] for s in stats]
    top = functools.reduce(jnp.maximum, tops)
    factors = [jnp.exp2(t - top) for t in tops]
    total = sum(f * (s[4:8] + s[8:12]) for f, s in zip(factors, stats))
    shares = jnp.concatenate([f / total for f in factors] + [jnp.zeros((112, 128), F32)], 0)
    shares = jnp.transpose(shares)
    for h in range(4):
        rows = slice(h * BLK, (h + 1) * BLK)
        out = 0.0
        for n in range(QUAD):
            out = out + got[n, rows, :].astype(F32) * shares[:, n * 4 + h : n * 4 + h + 1]
        attn[rows, :] = out.astype(BF16)

    def old(n):
        return lambda h: qs[n, Q_DEC:, :].astype(F32)[2 * h : 2 * h + 2]

    def fresh(n):
        return lambda h: got[n, O_FRESH:, :].astype(F32)[2 * (h % 4) : 2 * (h % 4) + 2]

    old_stats = [qs[n, Q_DEC:, :].astype(F32)[16:18] for n in range(QUAD)]
    fresh_stats = []
    lane = iota((2, 128), 1)
    for n in range(QUAD):
        tile = got[n, O_FRESH:, :].astype(F32)[8:]
        placed = jnp.zeros((2, 128), F32)
        for h in range(HEADS):
            both = tile[2 * (h % 4) : 2 * (h % 4) + 2]
            here = core == h // 4
            placed = jnp.where(lane == h, jnp.where(here, both[:, 0:1], NEG), placed)
            for m in (1, 2):
                placed = jnp.where(lane == m * HEADS + h, jnp.where(here, both[:, m : m + 1], 0.0), placed)
        fresh_stats.append(placed)
    mixes, tops, totals = combine(
        [old(n) for n in range(QUAD)] + [fresh(n) for n in range(QUAD)],
        old_stats + fresh_stats,
        True,
    )
    keep_stats = stat_tile(tops, totals)
    send_stats = stat_tile(tops, totals, True)
    dec_keep[8:, :] = jnp.broadcast_to(jnp.where(even, keep_stats[0:1], keep_stats[1:2]), (8, 128))
    sent = []
    for h in range(HEADS):
        dec_keep[h : h + 1, :] = jnp.where(even, mixes[h][0:1], mixes[h][1:2])
        sent.append(jnp.where(even, mixes[h][1:2], mixes[h][0:1]))
    sent.append(jnp.where(even, send_stats[1:2], send_stats[0:1]))
    sent.append(jnp.zeros((7, 128), F32))
    send[4 * TOK :, :] = jnp.concatenate(sent, 0).astype(BF16)
    for h in range(4):
        rows = slice(h * TOK, (h + 1) * TOK)
        attn_keep[rows, :] = attn[pl.ds(aligned(h * BLK + core * TOK, TOK), TOK), :]
        send[rows, :] = attn[pl.ds(aligned(h * BLK + (1 - core) * TOK, TOK), TOK), :]


def final_kernel(attn_keep, dec_keep, got, attn_out, dec_out):
    core = spot()[4]
    for h in range(4):
        rows = slice(h * TOK, (h + 1) * TOK)
        for src, head in ((attn_keep, core), (got, 1 - core)):
            attn_out[:, pl.ds(aligned((head * 4 + h) * HEAD, HEAD), HEAD)] = src[rows, :]
    theirs = got[4 * TOK :, :].astype(F32)
    other = theirs[8:9, :]
    for h in range(HEADS):
        top_a, top_b = dec_keep[8:9, h : h + 1], other[:, h : h + 1]
        total_a = dec_keep[8:9, HEADS + h : HEADS + h + 1]
        total_b = other[:, HEADS + h : HEADS + h + 1] + other[:, 2 * HEADS + h : 2 * HEADS + h + 1]
        top = jnp.maximum(top_a, top_b)
        scale_a, scale_b = jnp.exp2(top_a - top), jnp.exp2(top_b - top)
        mixed = dec_keep[h : h + 1, :] * scale_a + theirs[h : h + 1, :] * scale_b
        dec_out[h : h + 1, :] = (mixed / (total_a * scale_a + total_b * scale_b)).astype(BF16)


def exchange(x, groups):
    return lax.all_to_all(x, "seq", 0, 0, axis_index_groups=groups, tiled=True)


def to_other_core(x):
    return lax.ppermute(x, "seq", [(n, n ^ 1) for n in range(2 * SIDE * SIDE)])


def body(q_pre, k_pre, v_pre, old_k, old_v, src_page, page_row, page_len, q_dec, dec_k, dec_v):
    seq, grp = lax.axis_index("seq"), lax.axis_index("grp")
    core = seq & 1
    far = pl.BlockSpec(memory_space=pltpu.HBM)
    counts = page_row.shape[1]
    (x_send,) = call(
        pages_kernel,
        [((NG, X_MSG, TWO), BF16)],
        (old_k.reshape(HALF, -1), old_v.reshape(HALF, -1), src_page, page_row, page_len),
        scratch=(
            pltpu.SMEM(src_page.shape, jnp.int32),
            pltpu.SMEM((1, counts), jnp.int32),
            pltpu.SMEM((1, counts), jnp.int32),
            pltpu.SemaphoreType.DMA((3 + 2 * NG,)),
        ),
        specs={n: far for n in range(5)},
        limit=60,
    )
    xs = lax.all_to_all(x_send, "grp", 0, 0, tiled=True)
    keep, send = call(
        split_kernel,
        [((PAIR_MSG, 128), BF16)] * 2,
        (q_pre, k_pre, v_pre, xs),
        scratch=(pltpu.SemaphoreType.DMA((12,)),),
        specs={n: far for n in range(3)},
    )
    q_mine = lax.dynamic_slice_in_dim(q_dec, grp * HEADS * HEAD, HEADS * HEAD, 2)
    q_mine = q_mine.reshape(ITEMS, HEADS * HEAD)

    (q_ordered,) = call(order_kernel, [((ITEMS, HEADS * HEAD), BF16)], (q_mine,))

    def own_tokens(x):
        part = lax.dynamic_slice(x, (seq // STEPS, 0, grp * TWO), (1, STEPS, TWO))[0]
        return jnp.pad(part, ((0, 128 - STEPS), (0, 0)))

    kv_send, q_blk = call(
        local_kernel,
        [((SIDE, KV_MSG, 128), BF16), ((QROWS, 128), BF16)],
        (keep, to_other_core(send), q_ordered, xs, own_tokens(dec_k), own_tokens(dec_v)),
        scratch=(
            pltpu.VMEM((DEC_TOK, TWO), BF16),
            pltpu.VMEM((DEC_TOK, TWO), BF16),
            pltpu.VMEM((ITEMS, DEC_TOK), F32),
            pltpu.VMEM((BLK, HEAD), F32),
        ),
    )
    keys, vals, small, keep_dec = call(
        merge_kernel,
        [((KEYS, 128), BF16), ((KEYS, 128), BF16), ((PAIR_SMALL, 128), BF16), ((72, 128), F32)],
        (exchange(kv_send, KEY_GROUPS),),
    )
    small_other = lax.ppermute(small, "seq", NEIGHBOURS)
    keys, vals, small_other = lax.optimization_barrier((keys, vals, small_other))
    keys_other = lax.ppermute(keys, "seq", NEIGHBOURS)
    vals_other = lax.ppermute(vals, "seq", NEIGHBOURS)
    (q_send,) = call(
        queries_kernel,
        [((QUAD, Q_MSG, 128), BF16)],
        (q_blk, small, small_other, keep_dec),
    )
    qs = exchange(q_send, QUADS)
    work = QROWS * SIDE * KEYS
    side = (
        pltpu.VMEM((QROWS, TWO), BF16),
        pltpu.VMEM((TWO, KEYS), BF16),
        pltpu.VMEM((TWO, KEYS), BF16),
        pltpu.VMEM((QROWS, KEYS), F32),
        pltpu.VMEM((QROWS, KEYS), F32),
    )
    (o_send,) = call(
        attend_kernel,
        [((QUAD, O_MSG, 128), BF16)],
        (qs, keys, keys_other, vals, vals_other, q_mine),
        scratch=(
            pltpu.VMEM((2 * KEYS, TWO), BF16),
            pltpu.VMEM((BLK, BLK), F32),
            pltpu.VMEM((FRESH, HEAD), BF16),
            *side,
            *side,
        ),
        cost=pl.CostEstimate(flops=work * 512, bytes_accessed=4 * 1024 * 1024, transcendentals=work),
    )
    attn_keep, dec_keep, last = call(
        pair_kernel,
        [((4 * TOK, 128), BF16), ((16, 128), F32), ((LAST_MSG, 128), BF16)],
        (exchange(o_send, QUADS), qs),
        scratch=(pltpu.VMEM((QROWS, HEAD), BF16),),
    )
    attn_out, dec_out = call(
        final_kernel,
        [((TOK, HEADS * HEAD), BF16), ((HEADS, HEAD), BF16)],
        (attn_keep, dec_keep, to_other_core(last)),
    )
    return attn_out, dec_out


def solution(mesh):
    return jax.shard_map(
        body,
        mesh=mesh,
        in_specs=(
            P("seq", "grp"),
            P("seq", "grp"),
            P("seq", "grp"),
            P("seq", "grp", None, None),
            P("seq", "grp", None, None),
            P("seq", None),
            P("seq", "grp"),
            P("seq", "grp"),
            P(),
            P(),
            P(),
        ),
        out_specs=(P("seq", "grp"), P(("seq", "grp"), None)),
        check_vma=False,
    )
```
